32 devices in a mesh: dom: 8 (over z, x), grp: 4 (over y, core).
Axes of the slice: x: 2, y: 2, z: 4, core: 2. Of those that a mesh axis runs over, the one named last changes fastest.
Arguments:
- heads: int32 [262144], P(('dom', 'grp')), may hold values from 0 to 2047
- tails: int32 [262144], P(('dom', 'grp')), may hold values from 0 to 4095, as said below
- signs: int32 [2, 262144], P(None, ('dom', 'grp')), may hold values from 0 to 4095
- edge_weights: float32 [262144], P(('dom', 'grp')), may hold values from 0.25 to 4
- ground: float32 [16384], P(('dom', 'grp')), may hold values from 2 to 40
Outputs:
- solution: float32 [24, 16384], P(None, ('dom', 'grp'))
- residual: float32 [24, 16384], P(None, ('dom', 'grp'))
The draws below stay inside these ranges and needn't reach their ends.
Inputs may be any that keep to these rules, and one draw needn't show every extreme that they name: `tails`: every second endpoint is a vertex of the graph.
All inputs are finite; a program needn't handle non-finite values.
Results may differ from the reference program's by a relative error of at most 0.0003.
Values sent between devices are 32-bit elements; how exact they have to be, the bound alone decides.
No kernel may reach another device: no remote copies, remote signals or barrier semaphores. Data moves between devices by JAX's collectives and lax.ppermute only.
A program may use at most 64 MiB of HBM per device.

```python
import math
import jax
import jax.numpy as jnp
from jax import lax

K = 24
ITERS = 3
DOMAIN = 2048
REACH = 1024
EDEV = 8192
EDOM = 32768
DOMAINS = 8
VERTS = 16384
EDGES = 262144


def draw_heads(key, part):
    key = jax.random.fold_in(key, 11)
    values = jax.random.randint(key, (EDGES,), 0, DOMAIN, dtype=jnp.int32)
    position = jnp.arange(EDGES, dtype=jnp.int32) % EDEV
    values = jnp.where(position == 2, DOMAIN - 1, values)
    return jnp.where(position == 3, 0, values).astype(jnp.int32)


def draw_tails(key, part):
    key = jax.random.fold_in(key, 23)
    index = jnp.arange(EDGES, dtype=jnp.int32)
    domain_of = index // EDOM
    lowest = jnp.where(domain_of == 0, REACH, 0).astype(jnp.int32)
    highest = jnp.where(domain_of == DOMAINS - 1, DOMAIN + REACH, 2 * DOMAIN).astype(jnp.int32)
    values = jax.random.randint(key, (EDGES,), lowest, highest, dtype=jnp.int32)
    position = index % EDEV
    values = jnp.where(position == 0, lowest, values)
    return jnp.where(position == 1, highest - 1, values).astype(jnp.int32)


def draw_signs(key, part):
    key = jax.random.fold_in(key, 37)
    values = jax.random.randint(key, (2, EDGES), 0, 4096, dtype=jnp.int32)
    position = jnp.arange(EDGES, dtype=jnp.int32) % EDEV
    values = jnp.where(position[None, :] == 0, 4095, values)
    return jnp.where(position[None, :] == 1, 0, values).astype(jnp.int32)


def block_levels(own_key, shape, pieces, smallest, largest):
    factor_of, own = 1.0, jax.random.fold_in(own_key, 6)
    for axis_at, shards_of in pieces:
        steps = jnp.exp(jax.random.uniform(jax.random.fold_in(own, axis_at), (shards_of,), jnp.float32, smallest / len(pieces), largest / len(pieces)))
        factor_of = factor_of * jnp.repeat(steps, shape[axis_at] // shards_of).reshape([-1 if axis == axis_at else 1 for axis in range(len(shape))])
    return factor_of


def setup_inputs(seed: int = 0) -> dict:
    key_of = jax.random.split(jax.random.key(seed), 6)
    return {
        "heads": draw_heads(jax.random.fold_in(key_of[5], 71), 0),
        "tails": draw_tails(jax.random.fold_in(key_of[5], 71), 0),
        "signs": draw_signs(jax.random.fold_in(key_of[5], 71), 0),
        "edge_weights": jnp.clip(jnp.exp(math.log(4.0) - 2.7725887 * jax.random.uniform(key_of[3], (EDGES,), jnp.float32) ** block_levels(key_of[3], (EDGES,), ((0, 32),), -0.2, 0.2)), 0.25, 4.0),
        "ground": jnp.clip(jnp.exp(math.log(40.0) - 2.9957323 * jax.random.uniform(key_of[4], (VERTS,), jnp.float32) ** block_levels(key_of[4], (VERTS,), ((0, 32),), -0.2, 0.2)), 2.0, 40.0),
    }


def unpack(signs):
    half = K // 2
    shifts = jnp.arange(half, dtype=jnp.int32)
    bits = jnp.right_shift(signs[:, None, :], shifts[None, :, None]) & 1
    return (2 * bits - 1).reshape(2 * half, -1).astype(jnp.float32)

def reference(heads, tails, signs, edge_weights, ground):
    domain_of = jnp.arange(EDGES, dtype=jnp.int32) // EDOM
    start = (domain_of * DOMAIN).astype(jnp.int32)
    first = (start + heads).astype(jnp.int32)
    second = (start - REACH + tails).astype(jnp.int32)
    blocks = EDGES // EDEV
    first_b = first.reshape(blocks, EDEV)
    second_b = second.reshape(blocks, EDEV)
    weight_b = edge_weights.reshape(blocks, EDEV)
    signs_b = jnp.transpose(signs.reshape(2, blocks, EDEV), (1, 0, 2))

    def sketch_step(acc, block):
        head_idx, tail_idx, weight, sign_words = block
        scaled = unpack(sign_words) * jnp.sqrt(weight)[None, :]
        plus = jnp.concatenate([scaled, weight[None, :]], axis=0)
        minus = jnp.concatenate([-scaled, weight[None, :]], axis=0)
        return (acc.at[:, head_idx].add(plus).at[:, tail_idx].add(minus), None)
    start_acc = jnp.zeros((K + 1, VERTS), jnp.float32)
    gathered, _ = lax.scan(sketch_step, start_acc, (first_b, second_b, weight_b, signs_b))
    right = gathered[:K]
    diag = gathered[K] + ground

    def operate(field):

        def step(acc, block):
            head_idx, tail_idx, weight = block
            diff = weight[None, :] * (field[:, head_idx] - field[:, tail_idx])
            return (acc.at[:, head_idx].add(diff).at[:, tail_idx].add(-diff), None)
        acc, _ = lax.scan(step, jnp.zeros((K, VERTS), jnp.float32), (first_b, second_b, weight_b))
        return acc + ground[None, :] * field
    solution = jnp.zeros_like(right)
    residual = right
    scaled_res = residual / diag[None, :]
    direction = scaled_res
    gamma = lax.optimization_barrier(jnp.sum(residual * scaled_res, axis=1))
    for step in range(ITERS):
        image = operate(direction)
        alpha = gamma / lax.optimization_barrier(jnp.sum(direction * image, axis=1))
        solution = solution + alpha[:, None] * direction
        residual = residual - alpha[:, None] * image
        scaled_res = residual / diag[None, :]
        following = lax.optimization_barrier(jnp.sum(residual * scaled_res, axis=1))
        direction = scaled_res + (following / gamma)[:, None] * direction
        gamma = following
    return (solution, residual)
```

```python
import functools

import jax
import jax.numpy as jnp
from jax import lax
from jax.experimental import pallas as pl
from jax.experimental.pallas import tpu as pltpu
from jax.sharding import PartitionSpec as P

K = 24
HALF = 12
LANES = 128
SUB = 8
WIDE = 256
BF = jnp.bfloat16
F32 = jnp.float32


def row_of(block, r, count):
    return jnp.broadcast_to(block[r : r + 1, :], (count, LANES))


def low_rows():
    rows = lax.broadcasted_iota(jnp.int32, (16, LANES), 0)
    return [(rows + 16 * j).astype(F32).astype(BF) for j in range(WIDE // 16)]


def expand(values, index, buf_v, buf_o, lanes, highs, rows):
    high = values.astype(BF).astype(F32)
    pair = jnp.concatenate([high, values - high], axis=0).astype(BF)
    big = jnp.broadcast_to((index // WIDE).astype(F32), (16, LANES)).astype(BF)
    small = jnp.broadcast_to((index % WIDE).astype(F32), (16, LANES)).astype(BF)
    zero = jnp.zeros((16, LANES), BF)
    one = jnp.ones((16, LANES), BF)
    for a in range(highs):
        buf_v[a * 16 : (a + 1) * 16, lanes] = jnp.where(big == jnp.full((16, LANES), a, BF), pair, zero)
    for j in range(WIDE // 16):
        buf_o[j * 16 : (j + 1) * 16, lanes] = jnp.where(small == rows[j], one, zero)


def product(buf_v, buf_o, acc):
    acc[...] += lax.dot_general(
        buf_v[...], buf_o[...], (((1,), (1,)), ((), ())), preferred_element_type=F32
    )


def pick(table, index, first, blocks):
    low = index % LANES
    high = index // LANES
    out = jnp.zeros((SUB, LANES), F32)
    for a in range(blocks):
        part = table[:, first + a * LANES : first + (a + 1) * LANES]
        got = jnp.take_along_axis(part, low, axis=1, mode="promise_in_bounds")
        out = jnp.where(high == a, got, out)
    return out


class Sizes:
    def __init__(self, edev, verts, group):
        self.edev, self.verts, self.group = edev, verts, group
        self.domain = verts * group
        self.reach = self.domain // 2
        self.extent = self.domain + 2 * self.reach
        self.rows = K // group
        self.section = edev // LANES
        self.ground_rows = verts // LANES
        self.payload = -(-(5 * self.section + self.ground_rows) // SUB) * SUB
        self.per_device = self.section // SUB
        self.chunks = self.per_device * group
        self.high_h = self.domain // WIDE
        self.high_t = self.extent // WIDE

    def scratch(self):
        span = SUB * LANES
        one = [
            pltpu.VMEM((self.high_h * 16, span), BF),
            pltpu.VMEM((WIDE, span), BF),
            pltpu.VMEM((self.high_t * 16, span), BF),
            pltpu.VMEM((WIDE, span), BF),
        ]
        return one + one + [
            pltpu.VMEM((self.high_h * 16, WIDE), F32),
            pltpu.VMEM((self.high_t * 16, WIDE), F32),
        ]

    def block(self, pay, i, which):
        start = pl.multiple_of(which * self.section + (i % self.per_device) * SUB, SUB)
        return pay[i // self.per_device, pl.ds(start, SUB), :]


def sweep(size, fill, bufs):
    set_a, set_b, acc_h, acc_t = bufs[0:4], bufs[4:8], bufs[8], bufs[9]
    acc_h[...] = jnp.zeros_like(acc_h)
    acc_t[...] = jnp.zeros_like(acc_t)

    def use(bufs):
        product(bufs[0], bufs[1], acc_h)
        product(bufs[2], bufs[3], acc_t)

    fill(0, set_a)

    def step(i, carry):
        fill(2 * i + 1, set_b)
        use(set_a)
        fill((2 * i + 2) % size.chunks, set_a)
        use(set_b)
        return carry

    lax.fori_loop(0, size.chunks // 2, step, 0)


def collect(size, bufs, out_l, out_r):
    acc_h, acc_t = bufs[8], bufs[9]
    shift = size.reach // WIDE
    half = size.domain // WIDE
    for a in range(size.high_t):
        value = acc_t[a * 16 : a * 16 + 8, :] + acc_t[a * 16 + 8 : a * 16 + 16, :]
        h = a - shift
        if 0 <= h < size.high_h:
            value += acc_h[h * 16 : h * 16 + 8, :] + acc_h[h * 16 + 8 : h * 16 + 16, :]
        out, at = (out_l, a) if a < half else (out_r, a - half)
        out[:, at * WIDE : (at + 1) * WIDE] = value


def sketch_kernel(size, place, pay, out_l, out_r, *bufs):
    rows = low_rows()
    sub = lax.broadcasted_iota(jnp.int32, (SUB, LANES), 0)
    word, shift = place[0], place[1]
    is_sign = sub < size.rows

    def fill(i, bufs):
        heads = size.block(pay, i, 0).astype(jnp.int32)
        tails = size.block(pay, i, 1).astype(jnp.int32)
        signs = jnp.where(word == 0, size.block(pay, i, 2), size.block(pay, i, 3)).astype(jnp.int32)
        weight = size.block(pay, i, 4)
        root = jnp.sqrt(weight)
        for r in range(SUB):
            bit = jnp.right_shift(row_of(signs, r, SUB), sub + shift) & 1
            signed = (2 * bit - 1).astype(F32) * row_of(root, r, SUB)
            last = jnp.where(sub == size.rows, row_of(weight, r, SUB), 0.0)
            lanes = slice(r * LANES, (r + 1) * LANES)
            expand(jnp.where(is_sign, signed, last), heads[r : r + 1, :], bufs[0], bufs[1], lanes, size.high_h, rows)
            expand(jnp.where(is_sign, -signed, last), tails[r : r + 1, :], bufs[2], bufs[3], lanes, size.high_t, rows)

    sweep(size, fill, bufs)
    collect(size, bufs, out_l, out_r)
    for g in range(size.group):
        for r in range(size.ground_rows):
            at = size.reach + g * size.verts + r * LANES
            out, at = (out_l, at) if at < size.domain else (out_r, at - size.domain)
            row = 5 * size.section + r
            value = jnp.broadcast_to(pay[g, row : row + 1, :], (SUB, LANES))
            out[:, at : at + LANES] += jnp.where(sub == size.rows, value, 0.0)


def operator_core(size, pay, table, out_l, out_r, bufs):
    rows = low_rows()

    def fill(i, bufs):
        heads = size.block(pay, i, 0).astype(jnp.int32)
        tails = size.block(pay, i, 1).astype(jnp.int32)
        weight = size.block(pay, i, 4)
        for r in range(SUB):
            lanes = slice(r * LANES, (r + 1) * LANES)
            w = row_of(weight, r, SUB)
            at_head = pick(table, row_of(heads, r, SUB), size.reach, size.domain // LANES)
            at_tail = pick(table, row_of(tails, r, SUB), 0, size.extent // LANES)
            expand(w * at_tail, heads[r : r + 1, :], bufs[0], bufs[1], lanes, size.high_h, rows)
            expand(w * at_head, tails[r : r + 1, :], bufs[2], bufs[3], lanes, size.high_t, rows)

    sweep(size, fill, bufs)
    collect(size, bufs, out_l, out_r)


def halves(size, own_l, own_r, got_l, got_r):
    return ((0, own_l, got_l), (size.domain, own_r, got_r))


def first_kernel(size, pay, own_l, own_r, got_l, got_r, out_l, out_r, v, diag, *bufs):
    sub = lax.broadcasted_iota(jnp.int32, (SUB, size.domain), 0)
    for at, own, got in halves(size, own_l, own_r, got_l, got_r):
        total = own[...] + got[...]
        spread = jnp.broadcast_to(total[size.rows : size.rows + 1, :], total.shape)
        safe = jnp.where(spread > 0.0, spread, 1.0)
        diag[:, at : at + size.domain] = safe
        v[:, at : at + size.domain] = jnp.where(sub < size.rows, total / safe, 0.0)
    operator_core(size, pay, v, out_l, out_r, bufs)


def next_v(size, own_l, own_r, got_l, got_r, diag, v):
    for at, own, got in halves(size, own_l, own_r, got_l, got_r):
        v[:, at : at + size.domain] = (own[...] + got[...]) / diag[:, at : at + size.domain]


def second_kernel(size, pay, own_l, own_r, got_l, got_r, diag, out_l, out_r, v, *bufs):
    next_v(size, own_l, own_r, got_l, got_r, diag, v)
    operator_core(size, pay, v, out_l, out_r, bufs)


def third_kernel(size, pay, own_l, own_r, got_l, got_r, diag, v0, v1, out_l, out_r, v2, moments, *bufs):
    next_v(size, own_l, own_r, got_l, got_r, diag, v2)
    operator_core(size, pay, v2, out_l, out_r, bufs)
    lane = lax.broadcasted_iota(jnp.int32, (SUB, LANES), 1)
    middle = slice(size.reach, size.reach + size.domain)
    weighted = diag[:, middle] * v0[:, middle]
    other = diag[:, middle] * v1[:, middle]
    sums = [
        weighted * v0[:, middle],
        weighted * v1[:, middle],
        other * v1[:, middle],
        other * v2[:, middle],
        diag[:, middle] * v2[:, middle] * v2[:, middle],
        v2[:, : size.domain] * out_l[...] + v2[:, size.domain :] * out_r[...],
    ]
    out = jnp.zeros((SUB, LANES), F32)
    for k, value in enumerate(sums):
        out = jnp.where(lane == k, jnp.sum(value, axis=1, keepdims=True), out)
    moments[...] = out


def coefficients(mu):
    zero = jnp.zeros_like(mu[0])

    def inner(a, b):
        total = None
        for i, x in enumerate(a):
            for j, y in enumerate(b):
                term = mu[i + j] if x is None and y is None else mu[i + j] * (y if x is None else x if y is None else x * y)
                total = term if total is None else total + term
        return total

    def image(a):
        a = [jnp.ones_like(zero) if x is None else x for x in a] + [zero]
        return [a[0]] + [a[i] - a[i - 1] for i in range(1, len(a))]

    def ratio(top, bottom):
        return jnp.where(bottom > 0.0, top / jnp.where(bottom > 0.0, bottom, 1.0), 0.0)

    rho, pi, x = [jnp.ones_like(zero)], [jnp.ones_like(zero)], []
    gamma = inner(rho, rho)
    for step in range(3):
        moved = image(pi)
        alpha = ratio(gamma, inner(pi, moved))
        x = [(x[i] if i < len(x) else zero) + alpha * pi[i] for i in range(len(pi))]
        rho = [(rho[i] if i < len(rho) else zero) - alpha * moved[i] for i in range(len(moved))]
        if step < 2:
            following = inner(rho, rho)
            beta = ratio(following, gamma)
            pi = [rho[i] + (beta * pi[i] if i < len(pi) else zero) for i in range(len(rho))]
            gamma = following
    return x, rho


def last_kernel(size, moments, own_l, own_r, got_l, got_r, diag, v0, v1, v2, out):
    total = moments[0]
    for d in range(1, moments.shape[0]):
        total = total + moments[d]
    mu = [jnp.broadcast_to(total[:, k : k + 1], (SUB, LANES)) for k in range(6)]
    x, rho = coefficients(mu)
    x = [value[:, :1] for value in x]
    rho = [value[:, :1] for value in rho]
    for g in range(size.group):
        at = size.reach + g * size.verts
        here = slice(at, at + size.verts)
        if at < size.domain:
            sums = own_l[:, here] + got_l[:, g * size.verts : (g + 1) * size.verts]
        else:
            back = at - size.domain
            inside = slice(back, back + size.verts)
            sums = own_r[:, inside] + got_r[:, inside]
        a, b, c, scale = v0[:, here], v1[:, here], v2[:, here], diag[:, here]
        out[g, 0] = x[0] * a + x[1] * b + x[2] * c
        out[g, 1] = scale * (rho[0] * a + rho[1] * b + rho[2] * c) + rho[3] * sums


def on_device(heads, tails, signs, edge_weights, ground):
    group = lax.axis_size("grp")
    count = lax.axis_size("dom")
    size = Sizes(heads.shape[0], ground.shape[0], group)
    vmem = pl.BlockSpec(memory_space=pltpu.VMEM)
    smem = pl.BlockSpec(memory_space=pltpu.SMEM)
    params = pltpu.CompilerParams(vmem_limit_bytes=48 * 1024 * 1024)

    def flat(value):
        return value.astype(F32).reshape(-1, LANES)

    parts = [flat(heads), flat(tails), flat(signs[0]), flat(signs[1]), flat(edge_weights), flat(ground)]
    used = sum(part.shape[0] for part in parts)
    parts.append(jnp.zeros((size.payload - used, LANES), F32))
    pay = lax.all_gather(jnp.concatenate(parts, axis=0), "grp")

    half = jax.ShapeDtypeStruct((SUB, size.domain), F32)
    full = jax.ShapeDtypeStruct((SUB, size.extent), F32)

    def exchange(left, right):
        up = [(i, i + 1) for i in range(count - 1)]
        down = [(i + 1, i) for i in range(count - 1)]
        return lax.ppermute(right, "dom", up), lax.ppermute(left, "dom", down)

    me = lax.axis_index("grp")
    first_row = me * size.rows
    place = jnp.stack([first_row // HALF, first_row % HALF]).astype(jnp.int32)
    acc = pl.pallas_call(
        functools.partial(sketch_kernel, size),
        out_shape=(half, half),
        in_specs=[smem, vmem],
        out_specs=(vmem, vmem),
        scratch_shapes=size.scratch(),
        compiler_params=params,
        name="sketch",
    )(place, pay)
    got = exchange(*acc)
    *acc, v0, diag = pl.pallas_call(
        functools.partial(first_kernel, size),
        out_shape=(half, half, full, full),
        in_specs=[vmem] * 5,
        out_specs=(vmem,) * 4,
        scratch_shapes=size.scratch(),
        compiler_params=params,
        name="operator_first",
    )(pay, *acc, *got)
    got = exchange(*acc)
    *acc, v1 = pl.pallas_call(
        functools.partial(second_kernel, size),
        out_shape=(half, half, full),
        in_specs=[vmem] * 6,
        out_specs=(vmem,) * 3,
        scratch_shapes=size.scratch(),
        compiler_params=params,
        name="operator_second",
    )(pay, *acc, *got, diag)
    got = exchange(*acc)
    *acc, v2, moments = pl.pallas_call(
        functools.partial(third_kernel, size),
        out_shape=(half, half, full, jax.ShapeDtypeStruct((SUB, LANES), F32)),
        in_specs=[vmem] * 8,
        out_specs=(vmem,) * 4,
        scratch_shapes=size.scratch(),
        compiler_params=params,
        name="operator_third",
    )(pay, *acc, *got, diag, v0, v1)
    up = [(i, i + 1) for i in range(count - 1)]
    down = [(i + 1, i) for i in range(count - 1)]
    got_l = lax.ppermute(acc[1][:, size.reach :], "dom", up)
    got_r = lax.ppermute(acc[0][:, : size.reach], "dom", down)
    shared = lax.all_gather(moments, "dom")
    out = pl.pallas_call(
        functools.partial(last_kernel, size),
        out_shape=jax.ShapeDtypeStruct((group, 2, SUB, size.verts), F32),
        in_specs=[vmem] * 9,
        out_specs=vmem,
        compiler_params=params,
        name="combine",
    )(shared, *acc, got_l, got_r, diag, v0, v1, v2)
    out = lax.all_to_all(out[:, :, : size.rows, :], "grp", 0, 0)
    return (out[:, 0].reshape(K, size.verts), out[:, 1].reshape(K, size.verts))


def solution(mesh):
    in_specs = (
        P(("dom", "grp")),
        P(("dom", "grp")),
        P(None, ("dom", "grp")),
        P(("dom", "grp")),
        P(("dom", "grp")),
    )
    out_specs = (P(None, ("dom", "grp")), P(None, ("dom", "grp")))
    return jax.shard_map(
        on_device, mesh=mesh, in_specs=in_specs, out_specs=out_specs, check_vma=False
    )
```

```python
import functools

import jax
import jax.numpy as jnp
from jax import lax
from jax.experimental import pallas as pl
from jax.experimental.pallas import tpu as pltpu
from jax.sharding import PartitionSpec as P

K = 24
HALF = 12
LANES = 128
SUB = 8
WIDE = 256
BF = jnp.bfloat16
F32 = jnp.float32


def row_of(block, r, count):
    return jnp.broadcast_to(block[r : r + 1, :], (count, LANES))


def low_rows():
    rows = lax.broadcasted_iota(jnp.int32, (16, LANES), 0)
    return [(rows + 16 * j).astype(F32).astype(BF) for j in range(WIDE // 16)]


def expand(values, index, buf_v, buf_o, lanes, highs, rows):
    high = values.astype(BF).astype(F32)
    pair = jnp.concatenate([high, values - high], axis=0).astype(BF)
    big = jnp.broadcast_to((index // WIDE).astype(F32), (16, LANES)).astype(BF)
    small = jnp.broadcast_to((index % WIDE).astype(F32), (16, LANES)).astype(BF)
    zero = jnp.zeros((16, LANES), BF)
    one = jnp.ones((16, LANES), BF)
    for a in range(highs):
        buf_v[a * 16 : (a + 1) * 16, lanes] = jnp.where(big == jnp.full((16, LANES), a, BF), pair, zero)
    for j in range(WIDE // 16):
        buf_o[j * 16 : (j + 1) * 16, lanes] = jnp.where(small == rows[j], one, zero)


def product(buf_v, buf_o, acc):
    acc[...] += lax.dot_general(
        buf_v[...], buf_o[...], (((1,), (1,)), ((), ())), preferred_element_type=F32
    )


def pick(table, index, first, blocks):
    low = index % LANES
    high = index // LANES
    out = jnp.zeros((SUB, LANES), F32)
    for a in range(blocks):
        part = table[:, first + a * LANES : first + (a + 1) * LANES]
        got = jnp.take_along_axis(part, low, axis=1, mode="promise_in_bounds")
        out = jnp.where(high == a, got, out)
    return out


class Sizes:
    def __init__(self, edev, verts, group):
        self.edev, self.verts, self.group = edev, verts, group
        self.domain = verts * group
        self.reach = self.domain // 2
        self.extent = self.domain + 2 * self.reach
        self.rows = K // group
        self.section = edev // LANES
        self.ground_rows = verts // LANES
        self.payload = -(-(5 * self.section + self.ground_rows) // SUB) * SUB
        self.per_device = self.section // SUB
        self.chunks = self.per_device * group
        self.high_h = self.domain // WIDE
        self.high_t = self.extent // WIDE

    def scratch(self):
        span = SUB * LANES
        one = [
            pltpu.VMEM((self.high_h * 16, span), BF),
            pltpu.VMEM((WIDE, span), BF),
            pltpu.VMEM((self.high_t * 16, span), BF),
            pltpu.VMEM((WIDE, span), BF),
        ]
        return one + one + [
            pltpu.VMEM((self.high_h * 16, WIDE), F32),
            pltpu.VMEM((self.high_t * 16, WIDE), F32),
        ]

    def block(self, pay, i, which):
        start = pl.multiple_of(which * self.section + (i % self.per_device) * SUB, SUB)
        return pay[i // self.per_device, pl.ds(start, SUB), :]


def sweep(size, fill, bufs):
    set_a, set_b, acc_h, acc_t = bufs[0:4], bufs[4:8], bufs[8], bufs[9]
    acc_h[...] = jnp.zeros_like(acc_h)
    acc_t[...] = jnp.zeros_like(acc_t)

    def use(bufs):
        product(bufs[0], bufs[1], acc_h)
        product(bufs[2], bufs[3], acc_t)

    fill(0, set_a)

    def step(i, carry):
        fill(2 * i + 1, set_b)
        use(set_a)
        fill((2 * i + 2) % size.chunks, set_a)
        use(set_b)
        return carry

    lax.fori_loop(0, size.chunks // 2, step, 0)


def collect(size, bufs, out_l, out_r):
    acc_h, acc_t = bufs[8], bufs[9]
    shift = size.reach // WIDE
    half = size.domain // WIDE
    for a in range(size.high_t):
        value = acc_t[a * 16 : a * 16 + 8, :] + acc_t[a * 16 + 8 : a * 16 + 16, :]
        h = a - shift
        if 0 <= h < size.high_h:
            value += acc_h[h * 16 : h * 16 + 8, :] + acc_h[h * 16 + 8 : h * 16 + 16, :]
        out, at = (out_l, a) if a < half else (out_r, a - half)
        out[:, at * WIDE : (at + 1) * WIDE] = value


def sketch_kernel(size, place, pay, out_l, out_r, *bufs):
    rows = low_rows()
    sub = lax.broadcasted_iota(jnp.int32, (SUB, LANES), 0)
    word, shift = place[0], place[1]
    is_sign = sub < size.rows

    def fill(i, bufs):
        heads = size.block(pay, i, 0).astype(jnp.int32)
        tails = size.block(pay, i, 1).astype(jnp.int32)
        signs = jnp.where(word == 0, size.block(pay, i, 2), size.block(pay, i, 3)).astype(jnp.int32)
        weight = size.block(pay, i, 4)
        root = jnp.sqrt(weight)
        for r in range(SUB):
            bit = jnp.right_shift(row_of(signs, r, SUB), sub + shift) & 1
            signed = (2 * bit - 1).astype(F32) * row_of(root, r, SUB)
            last = jnp.where(sub == size.rows, row_of(weight, r, SUB), 0.0)
            lanes = slice(r * LANES, (r + 1) * LANES)
            expand(jnp.where(is_sign, signed, last), heads[r : r + 1, :], bufs[0], bufs[1], lanes, size.high_h, rows)
            expand(jnp.where(is_sign, -signed, last), tails[r : r + 1, :], bufs[2], bufs[3], lanes, size.high_t, rows)

    sweep(size, fill, bufs)
    collect(size, bufs, out_l, out_r)
    for g in range(size.group):
        for r in range(size.ground_rows):
            at = size.reach + g * size.verts + r * LANES
            out, at = (out_l, at) if at < size.domain else (out_r, at - size.domain)
            row = 5 * size.section + r
            value = jnp.broadcast_to(pay[g, row : row + 1, :], (SUB, LANES))
            out[:, at : at + LANES] += jnp.where(sub == size.rows, value, 0.0)


def operator_core(size, pay, table, out_l, out_r, bufs):
    rows = low_rows()

    def fill(i, bufs):
        heads = size.block(pay, i, 0).astype(jnp.int32)
        tails = size.block(pay, i, 1).astype(jnp.int32)
        weight = size.block(pay, i, 4)
        for r in range(SUB):
            lanes = slice(r * LANES, (r + 1) * LANES)
            w = row_of(weight, r, SUB)
            at_head = pick(table, row_of(heads, r, SUB), size.reach, size.domain // LANES)
            at_tail = pick(table, row_of(tails, r, SUB), 0, size.extent // LANES)
            expand(w * at_tail, heads[r : r + 1, :], bufs[0], bufs[1], lanes, size.high_h, rows)
            expand(w * at_head, tails[r : r + 1, :], bufs[2], bufs[3], lanes, size.high_t, rows)

    sweep(size, fill, bufs)
    collect(size, bufs, out_l, out_r)


def halves(size, own_l, own_r, got_l, got_r):
    return ((0, own_l, got_l), (size.domain, own_r, got_r))


def first_kernel(size, pay, own_l, own_r, got_l, got_r, out_l, out_r, v, diag, *bufs):
    sub = lax.broadcasted_iota(jnp.int32, (SUB, size.domain), 0)
    for at, own, got in halves(size, own_l, own_r, got_l, got_r):
        total = own[...] + got[...]
        spread = jnp.broadcast_to(total[size.rows : size.rows + 1, :], total.shape)
        safe = jnp.where(spread > 0.0, spread, 1.0)
        diag[:, at : at + size.domain] = safe
        v[:, at : at + size.domain] = jnp.where(sub < size.rows, total / safe, 0.0)
    operator_core(size, pay, v, out_l, out_r, bufs)


def next_v(size, own_l, own_r, got_l, got_r, diag, v):
    for at, own, got in halves(size, own_l, own_r, got_l, got_r):
        v[:, at : at + size.domain] = (own[...] + got[...]) / diag[:, at : at + size.domain]


def second_kernel(size, pay, own_l, own_r, got_l, got_r, diag, out_l, out_r, v, *bufs):
    next_v(size, own_l, own_r, got_l, got_r, diag, v)
    operator_core(size, pay, v, out_l, out_r, bufs)


def third_kernel(size, pay, own_l, own_r, got_l, got_r, diag, v0, v1, out_l, out_r, v2, moments, *bufs):
    next_v(size, own_l, own_r, got_l, got_r, diag, v2)
    operator_core(size, pay, v2, out_l, out_r, bufs)
    lane = lax.broadcasted_iota(jnp.int32, (SUB, LANES), 1)
    middle = slice(size.reach, size.reach + size.domain)
    weighted = diag[:, middle] * v0[:, middle]
    other = diag[:, middle] * v1[:, middle]
    sums = [
        weighted * v0[:, middle],
        weighted * v1[:, middle],
        other * v1[:, middle],
        other * v2[:, middle],
        diag[:, middle] * v2[:, middle] * v2[:, middle],
        v2[:, : size.domain] * out_l[...] + v2[:, size.domain :] * out_r[...],
    ]
    out = jnp.zeros((SUB, LANES), F32)
    for k, value in enumerate(sums):
        out = jnp.where(lane == k, jnp.sum(value, axis=1, keepdims=True), out)
    moments[...] = out


def coefficients(mu):
    zero = jnp.zeros_like(mu[0])

    def inner(a, b):
        total = None
        for i, x in enumerate(a):
            for j, y in enumerate(b):
                term = mu[i + j] if x is None and y is None else mu[i + j] * (y if x is None else x if y is None else x * y)
                total = term if total is None else total + term
        return total

    def image(a):
        a = [jnp.ones_like(zero) if x is None else x for x in a] + [zero]
        return [a[0]] + [a[i] - a[i - 1] for i in range(1, len(a))]

    def ratio(top, bottom):
        return jnp.where(bottom > 0.0, top / jnp.where(bottom > 0.0, bottom, 1.0), 0.0)

    rho, pi, x = [jnp.ones_like(zero)], [jnp.ones_like(zero)], []
    gamma = inner(rho, rho)
    for step in range(3):
        moved = image(pi)
        alpha = ratio(gamma, inner(pi, moved))
        x = [(x[i] if i < len(x) else zero) + alpha * pi[i] for i in range(len(pi))]
        rho = [(rho[i] if i < len(rho) else zero) - alpha * moved[i] for i in range(len(moved))]
        if step < 2:
            following = inner(rho, rho)
            beta = ratio(following, gamma)
            pi = [rho[i] + (beta * pi[i] if i < len(pi) else zero) for i in range(len(rho))]
            gamma = following
    return x, rho


def last_kernel(size, moments, own_l, own_r, got_l, got_r, diag, v0, v1, v2, out):
    total = moments[...]
    mu = [jnp.broadcast_to(total[:, k : k + 1], (SUB, LANES)) for k in range(6)]
    x, rho = coefficients(mu)
    x = [value[:, :1] for value in x]
    rho = [value[:, :1] for value in rho]
    for g in range(size.group):
        at = size.reach + g * size.verts
        here = slice(at, at + size.verts)
        if at < size.domain:
            sums = own_l[:, here] + got_l[:, g * size.verts : (g + 1) * size.verts]
        else:
            back = at - size.domain
            inside = slice(back, back + size.verts)
            sums = own_r[:, inside] + got_r[:, inside]
        a, b, c, scale = v0[:, here], v1[:, here], v2[:, here], diag[:, here]
        out[g, 0] = x[0] * a + x[1] * b + x[2] * c
        out[g, 1] = scale * (rho[0] * a + rho[1] * b + rho[2] * c) + rho[3] * sums


def total_over_dom(value, count):
    if count & (count - 1):
        return jnp.sum(lax.all_gather(value, "dom"), axis=0)
    step = 1
    while step < count:
        value = value + lax.ppermute(value, "dom", [(i, i ^ step) for i in range(count)])
        step *= 2
    return value


def on_device(heads, tails, signs, edge_weights, ground):
    group = lax.axis_size("grp")
    count = lax.axis_size("dom")
    size = Sizes(heads.shape[0], ground.shape[0], group)
    vmem = pl.BlockSpec(memory_space=pltpu.VMEM)
    smem = pl.BlockSpec(memory_space=pltpu.SMEM)
    params = pltpu.CompilerParams(vmem_limit_bytes=48 * 1024 * 1024)

    def flat(value):
        return value.astype(F32).reshape(-1, LANES)

    parts = [flat(heads), flat(tails), flat(signs[0]), flat(signs[1]), flat(edge_weights), flat(ground)]
    used = sum(part.shape[0] for part in parts)
    parts.append(jnp.zeros((size.payload - used, LANES), F32))
    pay = lax.all_gather(jnp.concatenate(parts, axis=0), "grp")

    half = jax.ShapeDtypeStruct((SUB, size.domain), F32)
    full = jax.ShapeDtypeStruct((SUB, size.extent), F32)

    def exchange(left, right):
        up = [(i, i + 1) for i in range(count - 1)]
        down = [(i + 1, i) for i in range(count - 1)]
        return lax.ppermute(right, "dom", up), lax.ppermute(left, "dom", down)

    me = lax.axis_index("grp")
    first_row = me * size.rows
    place = jnp.stack([first_row // HALF, first_row % HALF]).astype(jnp.int32)
    acc = pl.pallas_call(
        functools.partial(sketch_kernel, size),
        out_shape=(half, half),
        in_specs=[smem, vmem],
        out_specs=(vmem, vmem),
        scratch_shapes=size.scratch(),
        compiler_params=params,
        name="sketch",
    )(place, pay)
    got = exchange(*acc)
    *acc, v0, diag = pl.pallas_call(
        functools.partial(first_kernel, size),
        out_shape=(half, half, full, full),
        in_specs=[vmem] * 5,
        out_specs=(vmem,) * 4,
        scratch_shapes=size.scratch(),
        compiler_params=params,
        name="operator_first",
    )(pay, *acc, *got)
    got = exchange(*acc)
    *acc, v1 = pl.pallas_call(
        functools.partial(second_kernel, size),
        out_shape=(half, half, full),
        in_specs=[vmem] * 6,
        out_specs=(vmem,) * 3,
        scratch_shapes=size.scratch(),
        compiler_params=params,
        name="operator_second",
    )(pay, *acc, *got, diag)
    got = exchange(*acc)
    *acc, v2, moments = pl.pallas_call(
        functools.partial(third_kernel, size),
        out_shape=(half, half, full, jax.ShapeDtypeStruct((SUB, LANES), F32)),
        in_specs=[vmem] * 8,
        out_specs=(vmem,) * 4,
        scratch_shapes=size.scratch(),
        compiler_params=params,
        name="operator_third",
    )(pay, *acc, *got, diag, v0, v1)
    up = [(i, i + 1) for i in range(count - 1)]
    down = [(i + 1, i) for i in range(count - 1)]
    got_l = lax.ppermute(acc[1][:, size.reach :], "dom", up)
    got_r = lax.ppermute(acc[0][:, : size.reach], "dom", down)
    shared = total_over_dom(moments, count)
    out = pl.pallas_call(
        functools.partial(last_kernel, size),
        out_shape=jax.ShapeDtypeStruct((group, 2, SUB, size.verts), F32),
        in_specs=[vmem] * 9,
        out_specs=vmem,
        compiler_params=params,
        name="combine",
    )(shared, *acc, got_l, got_r, diag, v0, v1, v2)
    out = lax.all_to_all(out[:, :, : size.rows, :], "grp", 0, 0)
    return (out[:, 0].reshape(K, size.verts), out[:, 1].reshape(K, size.verts))


def solution(mesh):
    in_specs = (
        P(("dom", "grp")),
        P(("dom", "grp")),
        P(None, ("dom", "grp")),
        P(("dom", "grp")),
        P(("dom", "grp")),
    )
    out_specs = (P(None, ("dom", "grp")), P(None, ("dom", "grp")))
    return jax.shard_map(
        on_device, mesh=mesh, in_specs=in_specs, out_specs=out_specs, check_vma=False
    )
```

```python
import functools

import jax
import jax.numpy as jnp
from jax import lax
from jax.experimental import pallas as pl
from jax.experimental.pallas import tpu as pltpu
from jax.sharding import PartitionSpec as P

K = 24
HALF = 12
LANES = 128
SUB = 8
BF = jnp.bfloat16
F32 = jnp.float32


def row_of(block, r, count):
    return jnp.broadcast_to(block[r : r + 1, :], (count, LANES))


def bits_of(n):
    return (n - 1).bit_length()


class Sizes:
    def __init__(self, edev, verts, group):
        self.edev, self.verts, self.group = edev, verts, group
        self.domain = verts * group
        self.reach = self.domain // 2
        self.extent = self.domain + 2 * self.reach
        self.rows = K // group
        self.section = edev // LANES
        self.ground_rows = verts // LANES
        self.payload = -(-(5 * self.section + self.ground_rows) // SUB) * SUB
        self.regs = edev * group // (SUB * LANES)
        self.parts = self.regs * SUB // LANES
        self.ranges = (self.domain, self.extent)
        self.windows = (self.window(self.domain), self.window(self.extent))

    def window(self, span):
        return max(64, -(-2 * span // LANES // 16) * 16)

    def spread(self):
        shape = (self.parts, LANES, LANES)
        return (2,) + shape


def flip_mask(size, level):
    low = bits_of(size.regs)
    if level >= low + 10:
        return None
    if level < low + 3:
        place = lax.broadcasted_iota(jnp.int32, (SUB, LANES), 0)
        bit = level - low
    else:
        place = lax.broadcasted_iota(jnp.int32, (SUB, LANES), 1)
        bit = level - low - 3
    return -(jnp.right_shift(place, bit) & 1)


def partner(size, j):
    low = bits_of(size.regs)
    axis, bit = (0, j - low) if j < low + 3 else (1, j - low - 3)
    place = lax.broadcasted_iota(jnp.int32, (SUB, LANES), axis)
    lower = (jnp.right_shift(place, bit) & 1) == 0
    index = jnp.bitwise_xor(place, 1 << bit)
    return axis, index, lower


def sort_edges(size, keys, weights, which):
    low = bits_of(size.regs)
    levels = low + 10

    def between(group, stages):
        key = {v: keys[which, v] for v in group}
        weight = {v: weights[which, v] for v in group}
        for level, j in stages:
            for v in group:
                if v >> j & 1:
                    continue
                a, b = v, v | 1 << j
                if level < low and v >> level & 1:
                    a, b = b, a
                swap = key[a] > key[b]
                key[a], key[b] = jnp.where(swap, key[b], key[a]), jnp.where(swap, key[a], key[b])
                weight[a], weight[b] = (
                    jnp.where(swap, weight[b], weight[a]),
                    jnp.where(swap, weight[a], weight[b]),
                )
        for v in group:
            keys[which, v] = key[v]
            weights[which, v] = weight[v]

    def registers(level):
        top = min(level, low)
        if top > 3:
            for v in range(8):
                between(list(range(v, size.regs, 8)), [(level, j) for j in range(top - 1, 2, -1)])
        for v in range(0, size.regs, 8):
            between(list(range(v, v + 8)), [(level, j) for j in range(min(top, 3) - 1, -1, -1)])

    for v in range(0, size.regs, 8):
        between(list(range(v, v + 8)), [(level, j) for level in (1, 2, 3) for j in range(level - 1, -1, -1)])
    for level in range(4, low):
        registers(level)

    for level in range(low, levels + 1):
        before = flip_mask(size, level - 1) if level > low else None
        now = flip_mask(size, level)
        flip = now if before is None else before if now is None else jnp.bitwise_xor(before, now)
        stages = [partner(size, j) for j in range(level - 1, low - 1, -1)]

        def across(i, carry, flip=flip, stages=stages):
            group = [i * 8 + u for u in range(8)]
            key = [jnp.bitwise_xor(keys[which, v], flip) for v in group]
            weight = [weights[which, v] for v in group]
            for axis, index, lower in stages:
                for u in range(8):
                    k, w = key[u], weight[u]
                    other = jnp.take_along_axis(k, index, axis=axis, mode="promise_in_bounds")
                    other_w = jnp.take_along_axis(w, index, axis=axis, mode="promise_in_bounds")
                    best = jnp.where(lower, jnp.minimum(k, other), jnp.maximum(k, other))
                    weight[u] = jnp.where(best == k, w, other_w)
                    key[u] = best
            for u, v in enumerate(group):
                keys[which, v] = key[u]
                weights[which, v] = weight[u]
            return carry

        lax.fori_loop(0, size.regs // 8, across, 0)
        registers(level)


def sort_kernel(size, place, pay, key_out, weight_out, bounds, keys, weights):
    word, shift = place[0], place[1]
    per = size.section // SUB
    mask = (1 << size.rows) - 1
    bits_h, bits_t = bits_of(size.domain), bits_of(size.extent)

    def section(which, g, c):
        return pay[g, which * size.section + c * SUB : which * size.section + (c + 1) * SUB, :]

    for g in range(size.group):
        for c in range(per):
            heads = section(0, g, c).astype(jnp.int32)
            tails = section(1, g, c).astype(jnp.int32)
            signs = jnp.where(word == 0, section(2, g, c), section(3, g, c)).astype(jnp.int32)
            signs = jnp.right_shift(signs, shift) & mask
            weight = section(4, g, c)
            v = g * per + c
            keys[0, v] = (heads << (bits_t + size.rows)) | (tails << size.rows) | signs
            keys[1, v] = (tails << (bits_h + size.rows)) | (heads << size.rows) | signs
            weights[0, v] = weight
            weights[1, v] = weight

    def one(which, carry):
        sort_edges(size, keys, weights, which)
        return carry

    lax.fori_loop(0, 2, one, 0)
    for which in range(2):
        drop = size.rows + (bits_t, bits_h)[which]
        first = jnp.right_shift(keys[which, 0], drop)
        last = jnp.right_shift(keys[which, size.regs - 1], drop)
        bounds[2 * which : 2 * which + 1, :] = first[0:1, :] & -8
        bounds[2 * which + 1 : 2 * which + 2, :] = last[SUB - 1 : SUB, :]
        for j in range(size.parts):
            here = range(j * 16, (j + 1) * 16)
            key_out[which, j] = jnp.concatenate([keys[which, v] for v in here], axis=0).T
            weight_out[which, j] = jnp.concatenate([weights[which, v] for v in here], axis=0).T


def scatter(size, which, own, values, bounds, i, held, acc):
    window = size.windows[which]
    iota = lax.broadcasted_iota(jnp.int32, (16, LANES), 0)
    rows = [(iota + 16 * m).astype(F32).astype(BF) for m in range(window // 16)]
    zero, one = jnp.zeros((16, LANES), BF), jnp.ones((16, LANES), BF)

    def add(q, start, pair):
        hot = []
        for j in range(size.parts):
            local = own[j][q : q + 1, :] - start
            local = jnp.where((local >= 0) & (local < window), local, window).astype(F32)
            local = jnp.broadcast_to(local, (16, LANES)).astype(BF)
            hot.append(jnp.concatenate([jnp.where(local == row, one, zero) for row in rows], axis=0))
        hot = jnp.concatenate(hot, axis=1)
        got = lax.dot_general(hot, pair, (((1,), (1,)), ((), ())), preferred_element_type=F32)
        start = pl.multiple_of(start, SUB)
        acc[pl.ds(start, window), 0:16] += got

    far = 0
    for q in range(SUB):
        pair = []
        for j in range(size.parts):
            value = values[q][j]
            high = value.astype(BF).astype(F32)
            pair.append(jnp.concatenate([high, value - high], axis=0).astype(BF))
        pair = jnp.concatenate(pair, axis=1)
        held[q] = pair
        run = i * SUB + q
        start = bounds[2 * which, run]
        far = jnp.maximum(far, bounds[2 * which + 1, run] - start)
        add(q, start, pair)

    @pl.when(far >= window)
    def _():
        for q in range(SUB):
            run = i * SUB + q
            start = bounds[2 * which, run]
            more = (bounds[2 * which + 1, run] - start) // window

            def step(m, carry, q=q, start=start):
                add(q, start + (m + 1) * window, held[q])
                return carry

            lax.fori_loop(0, more, step, 0)


def collect(size, acc_h, acc_t, out_l, out_r):
    shift = size.reach // LANES
    half = size.domain // LANES

    def turned(acc, a):
        value = acc[a * LANES : (a + 1) * LANES, :].T
        return value[0:8, :] + value[8:16, :]

    for a in range(size.extent // LANES):
        value = turned(acc_t, a)
        h = a - shift
        if 0 <= h < half:
            value += turned(acc_h, h)
        out, at = (out_l, a) if a < half else (out_r, a - half)
        out[:, at * LANES : (at + 1) * LANES] = value


def clear(acc_h, acc_t):
    acc_h[...] = jnp.zeros_like(acc_h)
    acc_t[...] = jnp.zeros_like(acc_t)


def fields(size, key, which):
    other = (bits_of(size.extent), bits_of(size.domain))[which]
    return (
        jnp.right_shift(key, other + size.rows),
        jnp.right_shift(key, size.rows) & ((1 << other) - 1),
    )


def block(ref, which, j, i):
    return ref[which, j, pl.ds(pl.multiple_of(i * SUB, SUB), SUB), :]


def sketch_kernel(size, bounds, keys, weights, pay, out_l, out_r, acc_h, acc_t, held_h, held_t):
    sub = lax.broadcasted_iota(jnp.int32, (SUB, LANES), 0)
    is_sign = sub < size.rows
    clear(acc_h, acc_t)

    def step(i, carry):
        for which, acc, held, sense in ((0, acc_h, held_h, 2), (1, acc_t, held_t, -2)):
            own, values = [], [[] for _ in range(SUB)]
            for j in range(size.parts):
                key, weight = block(keys, which, j, i), block(weights, which, j, i)
                own.append(fields(size, key, which)[0])
                root = jnp.sqrt(weight)
                for q in range(SUB):
                    bit = jnp.right_shift(row_of(key, q, SUB), sub) & 1
                    signed = (sense * bit - sense // 2).astype(F32) * row_of(root, q, SUB)
                    last = jnp.where(sub == size.rows, row_of(weight, q, SUB), 0.0)
                    values[q].append(jnp.where(is_sign, signed, last))
            scatter(size, which, own, values, bounds, i, held, acc)
        return carry

    lax.fori_loop(0, LANES // SUB, step, 0)
    collect(size, acc_h, acc_t, out_l, out_r)
    for g in range(size.group):
        for r in range(size.ground_rows):
            at = size.reach + g * size.verts + r * LANES
            out, at = (out_l, at) if at < size.domain else (out_r, at - size.domain)
            row = 5 * size.section + r
            value = jnp.broadcast_to(pay[g, row : row + 1, :], (SUB, LANES))
            out[:, at : at + LANES] += jnp.where(sub == size.rows, value, 0.0)


def operator_core(size, bounds, keys, weights, table, out_l, out_r, bufs):
    acc_h, acc_t, held_h, held_t = bufs
    clear(acc_h, acc_t)

    def step(i, carry):
        for which, acc, held in ((0, acc_h, held_h), (1, acc_t, held_t)):
            first, blocks = ((0, size.extent // LANES), (size.reach, size.domain // LANES))[which]
            own, values = [], [[] for _ in range(SUB)]
            for j in range(size.parts):
                key, weight = block(keys, which, j, i), block(weights, which, j, i)
                mine, other = fields(size, key, which)
                own.append(mine)
                low = [row_of(other % LANES, q, SUB) for q in range(SUB)]
                high = [row_of(other // LANES, q, SUB) for q in range(SUB)]
                out = [jnp.zeros((SUB, LANES), F32)] * SUB
                for a in range(blocks):
                    part = table[:, first + a * LANES : first + (a + 1) * LANES]
                    for q in range(SUB):
                        got = jnp.take_along_axis(part, low[q], axis=1, mode="promise_in_bounds")
                        out[q] = jnp.where(high[q] == a, got, out[q])
                for q in range(SUB):
                    values[q].append(out[q] * row_of(weight, q, SUB))
            scatter(size, which, own, values, bounds, i, held, acc)
        return carry

    lax.fori_loop(0, LANES // SUB, step, 0)
    collect(size, acc_h, acc_t, out_l, out_r)


def halves(size, own_l, own_r, got_l, got_r):
    return ((0, own_l, got_l), (size.domain, own_r, got_r))


def first_kernel(size, bounds, keys, weights, own_l, own_r, got_l, got_r, out_l, out_r, v, diag, *bufs):
    sub = lax.broadcasted_iota(jnp.int32, (SUB, size.domain), 0)
    for at, own, got in halves(size, own_l, own_r, got_l, got_r):
        total = own[...] + got[...]
        spread = jnp.broadcast_to(total[size.rows : size.rows + 1, :], total.shape)
        safe = jnp.where(spread > 0.0, spread, 1.0)
        diag[:, at : at + size.domain] = safe
        v[:, at : at + size.domain] = jnp.where(sub < size.rows, total / safe, 0.0)
    operator_core(size, bounds, keys, weights, v, out_l, out_r, bufs)


def next_v(size, own_l, own_r, got_l, got_r, diag, v):
    for at, own, got in halves(size, own_l, own_r, got_l, got_r):
        v[:, at : at + size.domain] = (own[...] + got[...]) / diag[:, at : at + size.domain]


def second_kernel(size, bounds, keys, weights, own_l, own_r, got_l, got_r, diag, out_l, out_r, v, *bufs):
    next_v(size, own_l, own_r, got_l, got_r, diag, v)
    operator_core(size, bounds, keys, weights, v, out_l, out_r, bufs)


def third_kernel(size, bounds, keys, weights, own_l, own_r, got_l, got_r, diag, v0, v1, out_l, out_r, v2, moments, *bufs):
    next_v(size, own_l, own_r, got_l, got_r, diag, v2)
    operator_core(size, bounds, keys, weights, v2, out_l, out_r, bufs)
    lane = lax.broadcasted_iota(jnp.int32, (SUB, LANES), 1)
    middle = slice(size.reach, size.reach + size.domain)
    weighted = diag[:, middle] * v0[:, middle]
    other = diag[:, middle] * v1[:, middle]
    sums = [
        weighted * v0[:, middle],
        weighted * v1[:, middle],
        other * v1[:, middle],
        other * v2[:, middle],
        diag[:, middle] * v2[:, middle] * v2[:, middle],
        v2[:, : size.domain] * out_l[...] + v2[:, size.domain :] * out_r[...],
    ]
    out = jnp.zeros((SUB, LANES), F32)
    for k, value in enumerate(sums):
        out = jnp.where(lane == k, jnp.sum(value, axis=1, keepdims=True), out)
    moments[...] = out


def coefficients(mu):
    zero = jnp.zeros_like(mu[0])

    def inner(a, b):
        total = None
        for i, x in enumerate(a):
            for j, y in enumerate(b):
                term = mu[i + j] if x is None and y is None else mu[i + j] * (y if x is None else x if y is None else x * y)
                total = term if total is None else total + term
        return total

    def image(a):
        a = [jnp.ones_like(zero) if x is None else x for x in a] + [zero]
        return [a[0]] + [a[i] - a[i - 1] for i in range(1, len(a))]

    def ratio(top, bottom):
        return jnp.where(bottom > 0.0, top / jnp.where(bottom > 0.0, bottom, 1.0), 0.0)

    rho, pi, x = [jnp.ones_like(zero)], [jnp.ones_like(zero)], []
    gamma = inner(rho, rho)
    for step in range(3):
        moved = image(pi)
        alpha = ratio(gamma, inner(pi, moved))
        x = [(x[i] if i < len(x) else zero) + alpha * pi[i] for i in range(len(pi))]
        rho = [(rho[i] if i < len(rho) else zero) - alpha * moved[i] for i in range(len(moved))]
        if step < 2:
            following = inner(rho, rho)
            beta = ratio(following, gamma)
            pi = [rho[i] + (beta * pi[i] if i < len(pi) else zero) for i in range(len(rho))]
            gamma = following
    return x, rho


def last_kernel(size, moments, own_l, own_r, got_l, got_r, diag, v0, v1, v2, out):
    total = moments[...]
    mu = [jnp.broadcast_to(total[:, k : k + 1], (SUB, LANES)) for k in range(6)]
    x, rho = coefficients(mu)
    x = [value[:, :1] for value in x]
    rho = [value[:, :1] for value in rho]
    for g in range(size.group):
        at = size.reach + g * size.verts
        here = slice(at, at + size.verts)
        if at < size.domain:
            sums = own_l[:, here] + got_l[:, g * size.verts : (g + 1) * size.verts]
        else:
            back = at - size.domain
            inside = slice(back, back + size.verts)
            sums = own_r[:, inside] + got_r[:, inside]
        a, b, c, scale = v0[:, here], v1[:, here], v2[:, here], diag[:, here]
        out[g, 0] = x[0] * a + x[1] * b + x[2] * c
        out[g, 1] = scale * (rho[0] * a + rho[1] * b + rho[2] * c) + rho[3] * sums


def total_over_dom(value, count):
    if count & (count - 1):
        return jnp.sum(lax.all_gather(value, "dom"), axis=0)
    step = 1
    while step < count:
        value = value + lax.ppermute(value, "dom", [(i, i ^ step) for i in range(count)])
        step *= 2
    return value


def on_device(heads, tails, signs, edge_weights, ground):
    group = lax.axis_size("grp")
    count = lax.axis_size("dom")
    size = Sizes(heads.shape[0], ground.shape[0], group)
    vmem = pl.BlockSpec(memory_space=pltpu.VMEM)
    smem = pl.BlockSpec(memory_space=pltpu.SMEM)
    params = pltpu.CompilerParams(vmem_limit_bytes=48 * 1024 * 1024)

    def flat(value):
        return value.astype(F32).reshape(-1, LANES)

    parts = [flat(heads), flat(tails), flat(signs[0]), flat(signs[1]), flat(edge_weights), flat(ground)]
    used = sum(part.shape[0] for part in parts)
    parts.append(jnp.zeros((size.payload - used, LANES), F32))
    pay = lax.all_gather(jnp.concatenate(parts, axis=0), "grp")

    half = jax.ShapeDtypeStruct((SUB, size.domain), F32)
    full = jax.ShapeDtypeStruct((SUB, size.extent), F32)

    def exchange(left, right):
        up = [(i, i + 1) for i in range(count - 1)]
        down = [(i + 1, i) for i in range(count - 1)]
        return lax.ppermute(right, "dom", up), lax.ppermute(left, "dom", down)

    me = lax.axis_index("grp")
    first_row = me * size.rows
    place = jnp.stack([first_row // HALF, first_row % HALF]).astype(jnp.int32)
    spread = size.spread()
    keys, weights, bounds = pl.pallas_call(
        functools.partial(sort_kernel, size),
        out_shape=(
            jax.ShapeDtypeStruct(spread, jnp.int32),
            jax.ShapeDtypeStruct(spread, F32),
            jax.ShapeDtypeStruct((4, LANES), jnp.int32),
        ),
        in_specs=[smem, vmem],
        out_specs=(vmem,) * 3,
        scratch_shapes=[
            pltpu.VMEM((2, size.regs, SUB, LANES), jnp.int32),
            pltpu.VMEM((2, size.regs, SUB, LANES), F32),
        ],
        compiler_params=params,
        name="sort_edges",
    )(place, pay)
    edges = (bounds, keys, weights)
    edge_specs = [smem, vmem, vmem]
    scratch = [
        pltpu.VMEM((size.domain + size.windows[0], LANES), F32),
        pltpu.VMEM((size.extent + size.windows[1], LANES), F32),
        pltpu.VMEM((SUB, 16, size.parts * LANES), BF),
        pltpu.VMEM((SUB, 16, size.parts * LANES), BF),
    ]
    acc = pl.pallas_call(
        functools.partial(sketch_kernel, size),
        out_shape=(half, half),
        in_specs=edge_specs + [vmem],
        out_specs=(vmem, vmem),
        scratch_shapes=scratch,
        compiler_params=params,
        name="sketch",
    )(*edges, pay)
    got = exchange(*acc)
    *acc, v0, diag = pl.pallas_call(
        functools.partial(first_kernel, size),
        out_shape=(half, half, full, full),
        in_specs=edge_specs + [vmem] * 4,
        out_specs=(vmem,) * 4,
        scratch_shapes=scratch,
        compiler_params=params,
        name="operator_first",
    )(*edges, *acc, *got)
    got = exchange(*acc)
    *acc, v1 = pl.pallas_call(
        functools.partial(second_kernel, size),
        out_shape=(half, half, full),
        in_specs=edge_specs + [vmem] * 5,
        out_specs=(vmem,) * 3,
        scratch_shapes=scratch,
        compiler_params=params,
        name="operator_second",
    )(*edges, *acc, *got, diag)
    got = exchange(*acc)
    *acc, v2, moments = pl.pallas_call(
        functools.partial(third_kernel, size),
        out_shape=(half, half, full, jax.ShapeDtypeStruct((SUB, LANES), F32)),
        in_specs=edge_specs + [vmem] * 7,
        out_specs=(vmem,) * 4,
        scratch_shapes=scratch,
        compiler_params=params,
        name="operator_third",
    )(*edges, *acc, *got, diag, v0, v1)
    up = [(i, i + 1) for i in range(count - 1)]
    down = [(i + 1, i) for i in range(count - 1)]
    got_l = lax.ppermute(acc[1][:, size.reach :], "dom", up)
    got_r = lax.ppermute(acc[0][:, : size.reach], "dom", down)
    shared = total_over_dom(moments, count)
    out = pl.pallas_call(
        functools.partial(last_kernel, size),
        out_shape=jax.ShapeDtypeStruct((group, 2, SUB, size.verts), F32),
        in_specs=[vmem] * 9,
        out_specs=vmem,
        compiler_params=params,
        name="combine",
    )(shared, *acc, got_l, got_r, diag, v0, v1, v2)
    out = lax.all_to_all(out[:, :, : size.rows, :], "grp", 0, 0)
    return (out[:, 0].reshape(K, size.verts), out[:, 1].reshape(K, size.verts))


def solution(mesh):
    in_specs = (
        P(("dom", "grp")),
        P(("dom", "grp")),
        P(None, ("dom", "grp")),
        P(("dom", "grp")),
        P(("dom", "grp")),
    )
    out_specs = (P(None, ("dom", "grp")), P(None, ("dom", "grp")))
    return jax.shard_map(
        on_device, mesh=mesh, in_specs=in_specs, out_specs=out_specs, check_vma=False
    )
```

```python
import functools

import jax
import jax.numpy as jnp
from jax import lax
from jax.experimental import pallas as pl
from jax.experimental.pallas import tpu as pltpu
from jax.sharding import PartitionSpec as P

K = 24
HALF = 12
LANES = 128
SUB = 8
BF = jnp.bfloat16
F32 = jnp.float32


def row_of(block, r, count):
    return jnp.broadcast_to(block[r : r + 1, :], (count, LANES))


def bits_of(n):
    return (n - 1).bit_length()


class Sizes:
    def __init__(self, edev, verts, group):
        self.edev, self.verts, self.group = edev, verts, group
        self.domain = verts * group
        self.reach = self.domain // 2
        self.extent = self.domain + 2 * self.reach
        self.rows = K // group
        self.section = edev // LANES
        self.ground_rows = verts // LANES
        self.payload = -(-(5 * self.section + self.ground_rows) // SUB) * SUB
        self.regs = edev * group // (SUB * LANES)
        self.parts = self.regs * SUB // LANES
        self.ranges = (self.domain, self.extent)
        self.windows = (self.window(self.domain), self.window(self.extent))

    def window(self, span):
        return max(64, -(-2 * span // LANES // 16) * 16)

    def spread(self):
        shape = (self.parts, LANES, LANES)
        return (2,) + shape


def flip_mask(size, level):
    low = bits_of(size.regs)
    if level >= low + 10:
        return None
    if level < low + 3:
        place = lax.broadcasted_iota(jnp.int32, (SUB, LANES), 0)
        bit = level - low
    else:
        place = lax.broadcasted_iota(jnp.int32, (SUB, LANES), 1)
        bit = level - low - 3
    return -(jnp.right_shift(place, bit) & 1)


def partner(size, j):
    low = bits_of(size.regs)
    axis, bit = (0, j - low) if j < low + 3 else (1, j - low - 3)
    place = lax.broadcasted_iota(jnp.int32, (SUB, LANES), axis)
    lower = (jnp.right_shift(place, bit) & 1) == 0
    index = jnp.bitwise_xor(place, 1 << bit)
    return axis, index, lower


def sort_edges(size, keys, weights, which):
    low = bits_of(size.regs)
    levels = low + 10

    def between(group, stages):
        key = {v: keys[which, v] for v in group}
        weight = {v: weights[which, v] for v in group}
        for level, j in stages:
            for v in group:
                if v >> j & 1:
                    continue
                a, b = v, v | 1 << j
                if level < low and v >> level & 1:
                    a, b = b, a
                swap = key[a] > key[b]
                key[a], key[b] = jnp.where(swap, key[b], key[a]), jnp.where(swap, key[a], key[b])
                weight[a], weight[b] = (
                    jnp.where(swap, weight[b], weight[a]),
                    jnp.where(swap, weight[a], weight[b]),
                )
        for v in group:
            keys[which, v] = key[v]
            weights[which, v] = weight[v]

    def registers(level):
        top = min(level, low)
        if top > 3:
            for v in range(8):
                between(list(range(v, size.regs, 8)), [(level, j) for j in range(top - 1, 2, -1)])
        for v in range(0, size.regs, 8):
            between(list(range(v, v + 8)), [(level, j) for j in range(min(top, 3) - 1, -1, -1)])

    for v in range(0, size.regs, 8):
        between(list(range(v, v + 8)), [(level, j) for level in (1, 2, 3) for j in range(level - 1, -1, -1)])
    for level in range(4, low):
        registers(level)

    for level in range(low, levels + 1):
        before = flip_mask(size, level - 1) if level > low else None
        now = flip_mask(size, level)
        flip = now if before is None else before if now is None else jnp.bitwise_xor(before, now)
        stages = [partner(size, j) for j in range(level - 1, low - 1, -1)]

        def across(i, carry, flip=flip, stages=stages):
            group = [i * 8 + u for u in range(8)]
            key = [jnp.bitwise_xor(keys[which, v], flip) for v in group]
            weight = [weights[which, v] for v in group]
            for axis, index, lower in stages:
                for u in range(8):
                    k, w = key[u], weight[u]
                    other = jnp.take_along_axis(k, index, axis=axis, mode="promise_in_bounds")
                    other_w = jnp.take_along_axis(w, index, axis=axis, mode="promise_in_bounds")
                    best = jnp.where(lower, jnp.minimum(k, other), jnp.maximum(k, other))
                    weight[u] = jnp.where(best == k, w, other_w)
                    key[u] = best
            for u, v in enumerate(group):
                keys[which, v] = key[u]
                weights[which, v] = weight[u]
            return carry

        lax.fori_loop(0, size.regs // 8, across, 0)
        registers(level)


def sort_kernel(size, place, pay, key_out, weight_out, bounds, keys, weights):
    word, shift = place[0], place[1]
    per = size.section // SUB
    mask = (1 << size.rows) - 1
    bits_h, bits_t = bits_of(size.domain), bits_of(size.extent)

    def section(which, g, c):
        return pay[g, which * size.section + c * SUB : which * size.section + (c + 1) * SUB, :]

    for g in range(size.group):
        for c in range(per):
            heads = section(0, g, c).astype(jnp.int32)
            tails = section(1, g, c).astype(jnp.int32)
            signs = jnp.where(word == 0, section(2, g, c), section(3, g, c)).astype(jnp.int32)
            signs = jnp.right_shift(signs, shift) & mask
            weight = section(4, g, c)
            v = g * per + c
            keys[0, v] = (heads << (bits_t + size.rows)) | (tails << size.rows) | signs
            keys[1, v] = (tails << (bits_h + size.rows)) | (heads << size.rows) | signs
            weights[0, v] = weight
            weights[1, v] = weight

    def one(which, carry):
        sort_edges(size, keys, weights, which)
        return carry

    lax.fori_loop(0, 2, one, 0)
    for which in range(2):
        drop = size.rows + (bits_t, bits_h)[which]
        first = jnp.right_shift(keys[which, 0], drop)
        last = jnp.right_shift(keys[which, size.regs - 1], drop)
        bounds[2 * which : 2 * which + 1, :] = first[0:1, :] & -8
        bounds[2 * which + 1 : 2 * which + 2, :] = last[SUB - 1 : SUB, :]
        for j in range(size.parts):
            here = range(j * 16, (j + 1) * 16)
            key_out[which, j] = jnp.concatenate([keys[which, v] for v in here], axis=0).T
            weight_out[which, j] = jnp.concatenate([weights[which, v] for v in here], axis=0).T


def scatter(size, which, own, values, bounds, i, held, acc):
    window = size.windows[which]
    iota = lax.broadcasted_iota(jnp.int32, (16, LANES), 0)
    rows = [(iota + 16 * m).astype(F32).astype(BF) for m in range(window // 16)]
    zero, one = jnp.zeros((16, LANES), BF), jnp.ones((16, LANES), BF)

    def add(q, start, pair):
        hot = []
        for j in range(size.parts):
            local = own[j][q : q + 1, :] - start
            local = jnp.where((local >= 0) & (local < window), local, window).astype(F32)
            local = jnp.broadcast_to(local, (16, LANES)).astype(BF)
            hot.append(jnp.concatenate([jnp.where(local == row, one, zero) for row in rows], axis=0))
        hot = jnp.concatenate(hot, axis=1)
        got = lax.dot_general(hot, pair, (((1,), (1,)), ((), ())), preferred_element_type=F32)
        start = pl.multiple_of(start, SUB)
        acc[pl.ds(start, window), 0:16] += got

    far = 0
    for q in range(SUB):
        pair = []
        for j in range(size.parts):
            value = values[q][j]
            high = value.astype(BF).astype(F32)
            pair.append(jnp.concatenate([high, value - high], axis=0).astype(BF))
        pair = jnp.concatenate(pair, axis=1)
        held[q] = pair
        run = i * SUB + q
        start = bounds[2 * which, run]
        far = jnp.maximum(far, bounds[2 * which + 1, run] - start)
        add(q, start, pair)

    @pl.when(far >= window)
    def _():
        for q in range(SUB):
            run = i * SUB + q
            start = bounds[2 * which, run]
            more = (bounds[2 * which + 1, run] - start) // window

            def step(m, carry, q=q, start=start):
                add(q, start + (m + 1) * window, held[q])
                return carry

            lax.fori_loop(0, more, step, 0)


def collect(size, acc_h, acc_t, out_l, out_r):
    shift = size.reach // LANES
    half = size.domain // LANES

    def turned(acc, a):
        value = acc[a * LANES : (a + 1) * LANES, :].T
        return value[0:8, :] + value[8:16, :]

    for a in range(size.extent // LANES):
        value = turned(acc_t, a)
        h = a - shift
        if 0 <= h < half:
            value += turned(acc_h, h)
        out, at = (out_l, a) if a < half else (out_r, a - half)
        out[:, at * LANES : (at + 1) * LANES] = value


def clear(acc_h, acc_t):
    acc_h[...] = jnp.zeros_like(acc_h)
    acc_t[...] = jnp.zeros_like(acc_t)


def fields(size, key, which):
    other = (bits_of(size.extent), bits_of(size.domain))[which]
    return (
        jnp.right_shift(key, other + size.rows),
        jnp.right_shift(key, size.rows) & ((1 << other) - 1),
    )


def block(ref, which, j, i):
    return ref[which, j, pl.ds(pl.multiple_of(i * SUB, SUB), SUB), :]


def sketch_kernel(size, bounds, keys, weights, pay, out_l, out_r, acc_h, acc_t, held_h, held_t):
    sub = lax.broadcasted_iota(jnp.int32, (SUB, LANES), 0)
    is_sign = sub < size.rows
    clear(acc_h, acc_t)

    def step(i, carry):
        for which, acc, held, sense in ((0, acc_h, held_h, 2), (1, acc_t, held_t, -2)):
            own, values = [], [[] for _ in range(SUB)]
            for j in range(size.parts):
                key, weight = block(keys, which, j, i), block(weights, which, j, i)
                own.append(fields(size, key, which)[0])
                root = jnp.sqrt(weight)
                for q in range(SUB):
                    bit = jnp.right_shift(row_of(key, q, SUB), sub) & 1
                    signed = (sense * bit - sense // 2).astype(F32) * row_of(root, q, SUB)
                    last = jnp.where(sub == size.rows, row_of(weight, q, SUB), 0.0)
                    values[q].append(jnp.where(is_sign, signed, last))
            scatter(size, which, own, values, bounds, i, held, acc)
        return carry

    lax.fori_loop(0, LANES // SUB, step, 0)
    collect(size, acc_h, acc_t, out_l, out_r)
    for g in range(size.group):
        for r in range(size.ground_rows):
            at = size.reach + g * size.verts + r * LANES
            out, at = (out_l, at) if at < size.domain else (out_r, at - size.domain)
            row = 5 * size.section + r
            value = jnp.broadcast_to(pay[g, row : row + 1, :], (SUB, LANES))
            out[:, at : at + LANES] += jnp.where(sub == size.rows, value, 0.0)


def pick(table, low, high, first, blocks):
    out = jnp.zeros((SUB, LANES), F32)
    for a in range(blocks):
        part = table[:, first + a * LANES : first + (a + 1) * LANES]
        got = jnp.take_along_axis(part, low, axis=1, mode="promise_in_bounds")
        out = jnp.where(high == a, got, out)
    return out


def operator_core(size, bounds, keys, weights, table, out_l, out_r, bufs):
    acc_h, acc_t, held_h, held_t = bufs
    clear(acc_h, acc_t)

    def step(i, carry):
        for which, acc, held in ((0, acc_h, held_h), (1, acc_t, held_t)):
            first, blocks = ((0, size.extent // LANES), (size.reach, size.domain // LANES))[which]
            own, values = [], [[] for _ in range(SUB)]
            for j in range(size.parts):
                key, weight = block(keys, which, j, i), block(weights, which, j, i)
                mine, other = fields(size, key, which)
                own.append(mine)
                low, high = other % LANES, other // LANES
                out = [pick(table, row_of(low, q, SUB), row_of(high, q, SUB), first, blocks) for q in range(SUB)]
                for q in range(SUB):
                    values[q].append(out[q] * row_of(weight, q, SUB))
            scatter(size, which, own, values, bounds, i, held, acc)
        return carry

    lax.fori_loop(0, LANES // SUB, step, 0)
    collect(size, acc_h, acc_t, out_l, out_r)


def halves(size, own_l, own_r, got_l, got_r):
    return ((0, own_l, got_l), (size.domain, own_r, got_r))


def first_kernel(size, bounds, keys, weights, own_l, own_r, got_l, got_r, out_l, out_r, v, diag, *bufs):
    sub = lax.broadcasted_iota(jnp.int32, (SUB, size.domain), 0)
    for at, own, got in halves(size, own_l, own_r, got_l, got_r):
        total = own[...] + got[...]
        spread = jnp.broadcast_to(total[size.rows : size.rows + 1, :], total.shape)
        safe = jnp.where(spread > 0.0, spread, 1.0)
        diag[:, at : at + size.domain] = safe
        v[:, at : at + size.domain] = jnp.where(sub < size.rows, total / safe, 0.0)
    operator_core(size, bounds, keys, weights, v, out_l, out_r, bufs)


def next_v(size, own_l, own_r, got_l, got_r, diag, v):
    for at, own, got in halves(size, own_l, own_r, got_l, got_r):
        v[:, at : at + size.domain] = (own[...] + got[...]) / diag[:, at : at + size.domain]


def second_kernel(size, bounds, keys, weights, own_l, own_r, got_l, got_r, diag, out_l, out_r, v, *bufs):
    next_v(size, own_l, own_r, got_l, got_r, diag, v)
    operator_core(size, bounds, keys, weights, v, out_l, out_r, bufs)


def third_kernel(size, bounds, keys, weights, own_l, own_r, got_l, got_r, diag, v0, v1, out_l, out_r, v2, moments, *bufs):
    next_v(size, own_l, own_r, got_l, got_r, diag, v2)
    operator_core(size, bounds, keys, weights, v2, out_l, out_r, bufs)
    lane = lax.broadcasted_iota(jnp.int32, (SUB, LANES), 1)
    middle = slice(size.reach, size.reach + size.domain)
    weighted = diag[:, middle] * v0[:, middle]
    other = diag[:, middle] * v1[:, middle]
    sums = [
        weighted * v0[:, middle],
        weighted * v1[:, middle],
        other * v1[:, middle],
        other * v2[:, middle],
        diag[:, middle] * v2[:, middle] * v2[:, middle],
        v2[:, : size.domain] * out_l[...] + v2[:, size.domain :] * out_r[...],
    ]
    out = jnp.zeros((SUB, LANES), F32)
    for k, value in enumerate(sums):
        out = jnp.where(lane == k, jnp.sum(value, axis=1, keepdims=True), out)
    moments[...] = out


def coefficients(mu):
    zero = jnp.zeros_like(mu[0])

    def inner(a, b):
        total = None
        for i, x in enumerate(a):
            for j, y in enumerate(b):
                term = mu[i + j] if x is None and y is None else mu[i + j] * (y if x is None else x if y is None else x * y)
                total = term if total is None else total + term
        return total

    def image(a):
        a = [jnp.ones_like(zero) if x is None else x for x in a] + [zero]
        return [a[0]] + [a[i] - a[i - 1] for i in range(1, len(a))]

    def ratio(top, bottom):
        return jnp.where(bottom > 0.0, top / jnp.where(bottom > 0.0, bottom, 1.0), 0.0)

    rho, pi, x = [jnp.ones_like(zero)], [jnp.ones_like(zero)], []
    gamma = inner(rho, rho)
    for step in range(3):
        moved = image(pi)
        alpha = ratio(gamma, inner(pi, moved))
        x = [(x[i] if i < len(x) else zero) + alpha * pi[i] for i in range(len(pi))]
        rho = [(rho[i] if i < len(rho) else zero) - alpha * moved[i] for i in range(len(moved))]
        if step < 2:
            following = inner(rho, rho)
            beta = ratio(following, gamma)
            pi = [rho[i] + (beta * pi[i] if i < len(pi) else zero) for i in range(len(rho))]
            gamma = following
    return x, rho


def last_kernel(size, moments, own_l, own_r, got_l, got_r, diag, v0, v1, v2, out):
    total = moments[...]
    mu = [jnp.broadcast_to(total[:, k : k + 1], (SUB, LANES)) for k in range(6)]
    x, rho = coefficients(mu)
    x = [value[:, :1] for value in x]
    rho = [value[:, :1] for value in rho]
    for g in range(size.group):
        at = size.reach + g * size.verts
        here = slice(at, at + size.verts)
        if at < size.domain:
            sums = own_l[:, here] + got_l[:, g * size.verts : (g + 1) * size.verts]
        else:
            back = at - size.domain
            inside = slice(back, back + size.verts)
            sums = own_r[:, inside] + got_r[:, inside]
        a, b, c, scale = v0[:, here], v1[:, here], v2[:, here], diag[:, here]
        out[g, 0] = x[0] * a + x[1] * b + x[2] * c
        out[g, 1] = scale * (rho[0] * a + rho[1] * b + rho[2] * c) + rho[3] * sums


def total_over_dom(value, count):
    if count & (count - 1):
        return jnp.sum(lax.all_gather(value, "dom"), axis=0)
    step = 1
    while step < count:
        value = value + lax.ppermute(value, "dom", [(i, i ^ step) for i in range(count)])
        step *= 2
    return value


def on_device(heads, tails, signs, edge_weights, ground):
    group = lax.axis_size("grp")
    count = lax.axis_size("dom")
    size = Sizes(heads.shape[0], ground.shape[0], group)
    vmem = pl.BlockSpec(memory_space=pltpu.VMEM)
    smem = pl.BlockSpec(memory_space=pltpu.SMEM)
    params = pltpu.CompilerParams(vmem_limit_bytes=48 * 1024 * 1024)

    def flat(value):
        return value.astype(F32).reshape(-1, LANES)

    parts = [flat(heads), flat(tails), flat(signs[0]), flat(signs[1]), flat(edge_weights), flat(ground)]
    used = sum(part.shape[0] for part in parts)
    parts.append(jnp.zeros((size.payload - used, LANES), F32))
    pay = lax.all_gather(jnp.concatenate(parts, axis=0), "grp")

    half = jax.ShapeDtypeStruct((SUB, size.domain), F32)
    full = jax.ShapeDtypeStruct((SUB, size.extent), F32)

    def exchange(left, right):
        up = [(i, i + 1) for i in range(count - 1)]
        down = [(i + 1, i) for i in range(count - 1)]
        return lax.ppermute(right, "dom", up), lax.ppermute(left, "dom", down)

    me = lax.axis_index("grp")
    first_row = me * size.rows
    place = jnp.stack([first_row // HALF, first_row % HALF]).astype(jnp.int32)
    spread = size.spread()
    keys, weights, bounds = pl.pallas_call(
        functools.partial(sort_kernel, size),
        out_shape=(
            jax.ShapeDtypeStruct(spread, jnp.int32),
            jax.ShapeDtypeStruct(spread, F32),
            jax.ShapeDtypeStruct((4, LANES), jnp.int32),
        ),
        in_specs=[smem, vmem],
        out_specs=(vmem,) * 3,
        scratch_shapes=[
            pltpu.VMEM((2, size.regs, SUB, LANES), jnp.int32),
            pltpu.VMEM((2, size.regs, SUB, LANES), F32),
        ],
        compiler_params=params,
        name="sort_edges",
    )(place, pay)
    edges = (bounds, keys, weights)
    edge_specs = [smem, vmem, vmem]
    scratch = [
        pltpu.VMEM((size.domain + size.windows[0], LANES), F32),
        pltpu.VMEM((size.extent + size.windows[1], LANES), F32),
        pltpu.VMEM((SUB, 16, size.parts * LANES), BF),
        pltpu.VMEM((SUB, 16, size.parts * LANES), BF),
    ]
    acc = pl.pallas_call(
        functools.partial(sketch_kernel, size),
        out_shape=(half, half),
        in_specs=edge_specs + [vmem],
        out_specs=(vmem, vmem),
        scratch_shapes=scratch,
        compiler_params=params,
        name="sketch",
    )(*edges, pay)
    got = exchange(*acc)
    *acc, v0, diag = pl.pallas_call(
        functools.partial(first_kernel, size),
        out_shape=(half, half, full, full),
        in_specs=edge_specs + [vmem] * 4,
        out_specs=(vmem,) * 4,
        scratch_shapes=scratch,
        compiler_params=params,
        name="operator_first",
    )(*edges, *acc, *got)
    got = exchange(*acc)
    *acc, v1 = pl.pallas_call(
        functools.partial(second_kernel, size),
        out_shape=(half, half, full),
        in_specs=edge_specs + [vmem] * 5,
        out_specs=(vmem,) * 3,
        scratch_shapes=scratch,
        compiler_params=params,
        name="operator_second",
    )(*edges, *acc, *got, diag)
    got = exchange(*acc)
    *acc, v2, moments = pl.pallas_call(
        functools.partial(third_kernel, size),
        out_shape=(half, half, full, jax.ShapeDtypeStruct((SUB, LANES), F32)),
        in_specs=edge_specs + [vmem] * 7,
        out_specs=(vmem,) * 4,
        scratch_shapes=scratch,
        compiler_params=params,
        name="operator_third",
    )(*edges, *acc, *got, diag, v0, v1)
    up = [(i, i + 1) for i in range(count - 1)]
    down = [(i + 1, i) for i in range(count - 1)]
    got_l = lax.ppermute(acc[1][:, size.reach :], "dom", up)
    got_r = lax.ppermute(acc[0][:, : size.reach], "dom", down)
    shared = total_over_dom(moments, count)
    out = pl.pallas_call(
        functools.partial(last_kernel, size),
        out_shape=jax.ShapeDtypeStruct((group, 2, SUB, size.verts), F32),
        in_specs=[vmem] * 9,
        out_specs=vmem,
        compiler_params=params,
        name="combine",
    )(shared, *acc, got_l, got_r, diag, v0, v1, v2)
    out = lax.all_to_all(out[:, :, : size.rows, :], "grp", 0, 0)
    return (out[:, 0].reshape(K, size.verts), out[:, 1].reshape(K, size.verts))


def solution(mesh):
    in_specs = (
        P(("dom", "grp")),
        P(("dom", "grp")),
        P(None, ("dom", "grp")),
        P(("dom", "grp")),
        P(("dom", "grp")),
    )
    out_specs = (P(None, ("dom", "grp")), P(None, ("dom", "grp")))
    return jax.shard_map(
        on_device, mesh=mesh, in_specs=in_specs, out_specs=out_specs, check_vma=False
    )
```

```python
import functools

import jax
import jax.numpy as jnp
from jax import lax
from jax.experimental import pallas as pl
from jax.experimental.pallas import tpu as pltpu
from jax.sharding import PartitionSpec as P

K = 24
HALF = 12
LANES = 128
SUB = 8
BF = jnp.bfloat16
F32 = jnp.float32


def row_of(block, r, count):
    return jnp.broadcast_to(block[r : r + 1, :], (count, LANES))


def bits_of(n):
    return (n - 1).bit_length()


class Sizes:
    def __init__(self, edev, verts, group):
        self.edev, self.verts, self.group = edev, verts, group
        self.domain = verts * group
        self.reach = self.domain // 2
        self.extent = self.domain + 2 * self.reach
        self.rows = K // group
        self.section = edev // LANES
        self.ground_rows = verts // LANES
        self.payload = -(-(5 * self.section + self.ground_rows) // SUB) * SUB
        self.regs = edev * group // (SUB * LANES)
        self.parts = self.regs * SUB // LANES
        self.strip = self.domain // 8
        self.windows = (self.strip, self.extent // 16 + 64)
        self.blocks = (2 * self.strip // LANES, -(-(self.windows[1] + LANES - 1) // LANES))
        self.tables = self.extent // LANES + max(self.blocks)

    def pack(self, heads, tails, signs):
        strip = heads // self.strip
        turned = jnp.where(strip % 2 == 1, self.extent - 1 - tails, tails)
        key = strip * self.extent + turned
        key = key * self.strip + heads % self.strip
        return (key << self.rows) | signs

    def unpack(self, key):
        key = jnp.right_shift(key, self.rows)
        low, key = key & (self.strip - 1), jnp.right_shift(key, bits_of(self.strip))
        turned, strip = key & (self.extent - 1), jnp.right_shift(key, bits_of(self.extent))
        tails = jnp.where(strip & 1 == 1, self.extent - 1 - turned, turned)
        return strip * self.strip + low, tails


def flip_mask(size, level):
    low = bits_of(size.regs)
    if level >= low + 10:
        return None
    if level < low + 3:
        place = lax.broadcasted_iota(jnp.int32, (SUB, LANES), 0)
        bit = level - low
    else:
        place = lax.broadcasted_iota(jnp.int32, (SUB, LANES), 1)
        bit = level - low - 3
    return -(jnp.right_shift(place, bit) & 1)


def partner(size, j):
    low = bits_of(size.regs)
    axis, bit = (0, j - low) if j < low + 3 else (1, j - low - 3)
    place = lax.broadcasted_iota(jnp.int32, (SUB, LANES), axis)
    lower = (jnp.right_shift(place, bit) & 1) == 0
    index = jnp.bitwise_xor(place, 1 << bit)
    return axis, index, lower


def sort_edges(size, keys, weights):
    low = bits_of(size.regs)
    levels = low + 10

    def between(group, stages):
        key = {v: keys[v] for v in group}
        weight = {v: weights[v] for v in group}
        for level, j in stages:
            for v in group:
                if v >> j & 1:
                    continue
                a, b = v, v | 1 << j
                if level < low and v >> level & 1:
                    a, b = b, a
                swap = key[a] > key[b]
                key[a], key[b] = jnp.where(swap, key[b], key[a]), jnp.where(swap, key[a], key[b])
                weight[a], weight[b] = (
                    jnp.where(swap, weight[b], weight[a]),
                    jnp.where(swap, weight[a], weight[b]),
                )
        for v in group:
            keys[v] = key[v]
            weights[v] = weight[v]

    def registers(level):
        top = min(level, low)
        if top > 3:
            for v in range(8):
                between(list(range(v, size.regs, 8)), [(level, j) for j in range(top - 1, 2, -1)])
        for v in range(0, size.regs, 8):
            between(list(range(v, v + 8)), [(level, j) for j in range(min(top, 3) - 1, -1, -1)])

    for v in range(0, size.regs, 8):
        between(list(range(v, v + 8)), [(level, j) for level in (1, 2, 3) for j in range(level - 1, -1, -1)])
    for level in range(4, low):
        registers(level)

    for level in range(low, levels + 1):
        before = flip_mask(size, level - 1) if level > low else None
        now = flip_mask(size, level)
        flip = now if before is None else before if now is None else jnp.bitwise_xor(before, now)
        stages = [partner(size, j) for j in range(level - 1, low - 1, -1)]

        def across(i, carry, flip=flip, stages=stages):
            group = [i * 8 + u for u in range(8)]
            key = [jnp.bitwise_xor(keys[v], flip) for v in group]
            weight = [weights[v] for v in group]
            for axis, index, lower in stages:
                for u in range(8):
                    k, w = key[u], weight[u]
                    other = jnp.take_along_axis(k, index, axis=axis, mode="promise_in_bounds")
                    other_w = jnp.take_along_axis(w, index, axis=axis, mode="promise_in_bounds")
                    best = jnp.where(lower, jnp.minimum(k, other), jnp.maximum(k, other))
                    weight[u] = jnp.where(best == k, w, other_w)
                    key[u] = best
            for u, v in enumerate(group):
                keys[v] = key[u]
                weights[v] = weight[u]
            return carry

        lax.fori_loop(0, size.regs // 8, across, 0)
        registers(level)


def sort_kernel(size, place, pay, key_out, weight_out, bounds, keys, weights):
    word, shift = place[0], place[1]
    per = size.section // SUB
    mask = (1 << size.rows) - 1

    def section(which, g, c):
        return pay[g, which * size.section + c * SUB : which * size.section + (c + 1) * SUB, :]

    for g in range(size.group):
        for c in range(per):
            heads = section(0, g, c).astype(jnp.int32)
            tails = section(1, g, c).astype(jnp.int32)
            signs = jnp.where(word == 0, section(2, g, c), section(3, g, c)).astype(jnp.int32)
            v = g * per + c
            keys[v] = size.pack(heads, tails, jnp.right_shift(signs, shift) & mask)
            weights[v] = section(4, g, c)
    sort_edges(size, keys, weights)
    ends = [size.unpack(keys[v]) for v in range(size.regs)]
    for which in range(2):
        least = functools.reduce(jnp.minimum, [end[which] for end in ends])
        most = functools.reduce(jnp.maximum, [end[which] for end in ends])
        bounds[2 * which : 2 * which + 1, :] = jnp.min(least, axis=0, keepdims=True)
        bounds[2 * which + 1 : 2 * which + 2, :] = jnp.max(most, axis=0, keepdims=True)
    for j in range(size.parts):
        here = range(j * 16, (j + 1) * 16)
        key_out[j] = jnp.concatenate([keys[v] for v in here], axis=0).T
        weight_out[j] = jnp.concatenate([weights[v] for v in here], axis=0).T


def halves_of(value):
    high = value.astype(BF).astype(F32)
    return jnp.concatenate([high, value - high], axis=0).astype(BF)


def scatter(size, which, own, bounds, i, held, acc):
    window = size.windows[which]
    iota = lax.broadcasted_iota(jnp.int32, (16, LANES), 0)
    rows = [(iota + 16 * m).astype(F32).astype(BF) for m in range(16)]
    zero, one = jnp.zeros((16, LANES), BF), jnp.ones((16, LANES), BF)

    def add(q, start):
        hot = []
        for j in range(size.parts):
            column = []
            for at in range(0, window, 256):
                local = own[j][q : q + 1, :] - (start + at)
                local = jnp.where((local >= 0) & (local < 256), local, 256).astype(F32)
                local = jnp.broadcast_to(local, (16, LANES)).astype(BF)
                count = min(256, window - at) // 16
                column += [jnp.where(local == rows[m], one, zero) for m in range(count)]
            hot.append(jnp.concatenate(column, axis=0))
        hot = jnp.concatenate(hot, axis=1)
        got = lax.dot_general(hot, held[q], (((1,), (1,)), ((), ())), preferred_element_type=F32)
        start = pl.multiple_of(start, SUB)
        acc[pl.ds(start, window), 0:16] += got

    def reach(q):
        start = bounds[2 * which, i * SUB + q] & -8
        return start, bounds[2 * which + 1, i * SUB + q] - start

    far = 0
    for q in range(SUB):
        start, span = reach(q)
        far = jnp.maximum(far, span)
        add(q, start)

    @pl.when(far >= window)
    def _():
        for q in range(SUB):
            start, span = reach(q)

            def step(m, carry, q=q, start=start):
                add(q, start + m * window)
                return carry

            lax.fori_loop(1, span // window + 1, step, 0)


def collect(size, acc_h, acc_t, out_l, out_r):
    shift = size.reach // LANES
    half = size.domain // LANES

    def turned(acc, a):
        value = acc[a * LANES : (a + 1) * LANES, :].T
        return value[0:8, :] + value[8:16, :]

    for a in range(size.extent // LANES):
        value = turned(acc_t, a)
        h = a - shift
        if 0 <= h < half:
            value += turned(acc_h, h)
        out, at = (out_l, a) if a < half else (out_r, a - half)
        out[:, at * LANES : (at + 1) * LANES] = value


def clear(acc_h, acc_t):
    acc_h[...] = jnp.zeros_like(acc_h)
    acc_t[...] = jnp.zeros_like(acc_t)


def block(ref, j, i):
    return ref[j, pl.ds(pl.multiple_of(i * SUB, SUB), SUB), :]


def spread_lanes(j):
    return slice(j * LANES, (j + 1) * LANES)


def sketch_kernel(size, bounds, keys, weights, pay, out_l, out_r, acc_h, acc_t, held_h, held_t, tables):
    sub = lax.broadcasted_iota(jnp.int32, (SUB, LANES), 0)
    is_sign = sub < size.rows
    clear(acc_h, acc_t)

    def step(i, carry):
        heads, tails = [], []
        for j in range(size.parts):
            key, weight = block(keys, j, i), block(weights, j, i)
            head, tail = size.unpack(key)
            heads.append(head)
            tails.append(tail)
            root = jnp.sqrt(weight)
            for q in range(SUB):
                bit = jnp.right_shift(row_of(key, q, SUB), sub) & 1
                signed = (2 * bit - 1).astype(F32) * row_of(root, q, SUB)
                last = jnp.where(sub == size.rows, row_of(weight, q, SUB), 0.0)
                held_h[q, :, spread_lanes(j)] = halves_of(jnp.where(is_sign, signed, last))
                held_t[q, :, spread_lanes(j)] = halves_of(jnp.where(is_sign, -signed, last))
        scatter(size, 0, heads, bounds, i, held_h, acc_h)
        scatter(size, 1, tails, bounds, i, held_t, acc_t)
        return carry

    lax.fori_loop(0, LANES // SUB, step, 0)
    collect(size, acc_h, acc_t, out_l, out_r)
    for g in range(size.group):
        for r in range(size.ground_rows):
            at = size.reach + g * size.verts + r * LANES
            out, at = (out_l, at) if at < size.domain else (out_r, at - size.domain)
            row = 5 * size.section + r
            value = jnp.broadcast_to(pay[g, row : row + 1, :], (SUB, LANES))
            out[:, at : at + LANES] += jnp.where(sub == size.rows, value, 0.0)


def gather(size, which, index, weight, bounds, i, held, tables):
    shift = size.reach // LANES if which == 0 else 0
    count = size.blocks[which]

    def first_of(q):
        return bounds[2 * which, i * SUB + q] // LANES

    def last_of(q):
        return bounds[2 * which + 1, i * SUB + q] // LANES

    def take(low, high, a, out):
        got = jnp.take_along_axis(tables[shift + a], low, axis=1, mode="promise_in_bounds")
        return jnp.where(high == a, got, out)

    def store(q, j, out):
        held[q, :, spread_lanes(j)] = halves_of(out * row_of(weight[j], q, SUB))

    more = 0
    for q in range(SUB):
        first = first_of(q)
        more = jnp.maximum(more, last_of(q) - first)
        for j in range(size.parts):
            low = row_of(index[j] % LANES, q, SUB)
            high = row_of(index[j] // LANES, q, SUB)
            out = jnp.zeros((SUB, LANES), F32)
            for a in range(count):
                out = take(low, high, first + a, out)
            store(q, j, out)

    @pl.when(more >= count)
    def _():
        for q in range(SUB):

            @pl.when(last_of(q) - first_of(q) >= count)
            def _(q=q):
                for j in range(size.parts):
                    low = row_of(index[j] % LANES, q, SUB)
                    high = row_of(index[j] // LANES, q, SUB)
                    out = lax.fori_loop(
                        first_of(q),
                        last_of(q) + 1,
                        lambda a, out: take(low, high, a, out),
                        jnp.zeros((SUB, LANES), F32),
                    )
                    store(q, j, out)


def operator_core(size, bounds, keys, weights, table, out_l, out_r, bufs):
    acc_h, acc_t, held_h, held_t, tables = bufs
    clear(acc_h, acc_t)
    for a in range(size.extent // LANES):
        tables[a] = table[:, a * LANES : (a + 1) * LANES]

    def step(i, carry):
        heads, tails, weight = [], [], []
        for j in range(size.parts):
            head, tail = size.unpack(block(keys, j, i))
            heads.append(head)
            tails.append(tail)
            weight.append(block(weights, j, i))
        gather(size, 1, tails, weight, bounds, i, held_h, tables)
        gather(size, 0, heads, weight, bounds, i, held_t, tables)
        scatter(size, 0, heads, bounds, i, held_h, acc_h)
        scatter(size, 1, tails, bounds, i, held_t, acc_t)
        return carry

    lax.fori_loop(0, LANES // SUB, step, 0)
    collect(size, acc_h, acc_t, out_l, out_r)


def halves(size, own_l, own_r, got_l, got_r):
    return ((0, own_l, got_l), (size.domain, own_r, got_r))


def first_kernel(size, bounds, keys, weights, own_l, own_r, got_l, got_r, out_l, out_r, v, diag, *bufs):
    sub = lax.broadcasted_iota(jnp.int32, (SUB, size.domain), 0)
    for at, own, got in halves(size, own_l, own_r, got_l, got_r):
        total = own[...] + got[...]
        spread = jnp.broadcast_to(total[size.rows : size.rows + 1, :], total.shape)
        safe = jnp.where(spread > 0.0, spread, 1.0)
        diag[:, at : at + size.domain] = safe
        v[:, at : at + size.domain] = jnp.where(sub < size.rows, total / safe, 0.0)
    operator_core(size, bounds, keys, weights, v, out_l, out_r, bufs)


def next_v(size, own_l, own_r, got_l, got_r, diag, v):
    for at, own, got in halves(size, own_l, own_r, got_l, got_r):
        v[:, at : at + size.domain] = (own[...] + got[...]) / diag[:, at : at + size.domain]


def second_kernel(size, bounds, keys, weights, own_l, own_r, got_l, got_r, diag, out_l, out_r, v, *bufs):
    next_v(size, own_l, own_r, got_l, got_r, diag, v)
    operator_core(size, bounds, keys, weights, v, out_l, out_r, bufs)


def third_kernel(size, bounds, keys, weights, own_l, own_r, got_l, got_r, diag, v0, v1, out_l, out_r, v2, moments, *bufs):
    next_v(size, own_l, own_r, got_l, got_r, diag, v2)
    operator_core(size, bounds, keys, weights, v2, out_l, out_r, bufs)
    lane = lax.broadcasted_iota(jnp.int32, (SUB, LANES), 1)
    middle = slice(size.reach, size.reach + size.domain)
    weighted = diag[:, middle] * v0[:, middle]
    other = diag[:, middle] * v1[:, middle]
    sums = [
        weighted * v0[:, middle],
        weighted * v1[:, middle],
        other * v1[:, middle],
        other * v2[:, middle],
        diag[:, middle] * v2[:, middle] * v2[:, middle],
        v2[:, : size.domain] * out_l[...] + v2[:, size.domain :] * out_r[...],
    ]
    out = jnp.zeros((SUB, LANES), F32)
    for k, value in enumerate(sums):
        out = jnp.where(lane == k, jnp.sum(value, axis=1, keepdims=True), out)
    moments[...] = out


def coefficients(mu):
    zero = jnp.zeros_like(mu[0])

    def inner(a, b):
        total = None
        for i, x in enumerate(a):
            for j, y in enumerate(b):
                term = mu[i + j] if x is None and y is None else mu[i + j] * (y if x is None else x if y is None else x * y)
                total = term if total is None else total + term
        return total

    def image(a):
        a = [jnp.ones_like(zero) if x is None else x for x in a] + [zero]
        return [a[0]] + [a[i] - a[i - 1] for i in range(1, len(a))]

    def ratio(top, bottom):
        return jnp.where(bottom > 0.0, top / jnp.where(bottom > 0.0, bottom, 1.0), 0.0)

    rho, pi, x = [jnp.ones_like(zero)], [jnp.ones_like(zero)], []
    gamma = inner(rho, rho)
    for step in range(3):
        moved = image(pi)
        alpha = ratio(gamma, inner(pi, moved))
        x = [(x[i] if i < len(x) else zero) + alpha * pi[i] for i in range(len(pi))]
        rho = [(rho[i] if i < len(rho) else zero) - alpha * moved[i] for i in range(len(moved))]
        if step < 2:
            following = inner(rho, rho)
            beta = ratio(following, gamma)
            pi = [rho[i] + (beta * pi[i] if i < len(pi) else zero) for i in range(len(rho))]
            gamma = following
    return x, rho


def last_kernel(size, moments, own_l, own_r, got_l, got_r, diag, v0, v1, v2, out):
    total = moments[...]
    mu = [jnp.broadcast_to(total[:, k : k + 1], (SUB, LANES)) for k in range(6)]
    x, rho = coefficients(mu)
    x = [value[:, :1] for value in x]
    rho = [value[:, :1] for value in rho]
    for g in range(size.group):
        at = size.reach + g * size.verts
        here = slice(at, at + size.verts)
        if at < size.domain:
            sums = own_l[:, here] + got_l[:, g * size.verts : (g + 1) * size.verts]
        else:
            back = at - size.domain
            inside = slice(back, back + size.verts)
            sums = own_r[:, inside] + got_r[:, inside]
        a, b, c, scale = v0[:, here], v1[:, here], v2[:, here], diag[:, here]
        out[g, 0] = x[0] * a + x[1] * b + x[2] * c
        out[g, 1] = scale * (rho[0] * a + rho[1] * b + rho[2] * c) + rho[3] * sums


def total_over_dom(value, count):
    if count & (count - 1):
        return jnp.sum(lax.all_gather(value, "dom"), axis=0)
    step = 1
    while step < count:
        value = value + lax.ppermute(value, "dom", [(i, i ^ step) for i in range(count)])
        step *= 2
    return value


def on_device(heads, tails, signs, edge_weights, ground):
    group = lax.axis_size("grp")
    count = lax.axis_size("dom")
    size = Sizes(heads.shape[0], ground.shape[0], group)
    vmem = pl.BlockSpec(memory_space=pltpu.VMEM)
    smem = pl.BlockSpec(memory_space=pltpu.SMEM)
    params = pltpu.CompilerParams(vmem_limit_bytes=48 * 1024 * 1024)

    def flat(value):
        return value.astype(F32).reshape(-1, LANES)

    parts = [flat(heads), flat(tails), flat(signs[0]), flat(signs[1]), flat(edge_weights), flat(ground)]
    used = sum(part.shape[0] for part in parts)
    parts.append(jnp.zeros((size.payload - used, LANES), F32))
    pay = lax.all_gather(jnp.concatenate(parts, axis=0), "grp")

    half = jax.ShapeDtypeStruct((SUB, size.domain), F32)
    full = jax.ShapeDtypeStruct((SUB, size.extent), F32)

    def exchange(left, right):
        up = [(i, i + 1) for i in range(count - 1)]
        down = [(i + 1, i) for i in range(count - 1)]
        return lax.ppermute(right, "dom", up), lax.ppermute(left, "dom", down)

    me = lax.axis_index("grp")
    first_row = me * size.rows
    place = jnp.stack([first_row // HALF, first_row % HALF]).astype(jnp.int32)
    spread = (size.parts, LANES, LANES)
    keys, weights, bounds = pl.pallas_call(
        functools.partial(sort_kernel, size),
        out_shape=(
            jax.ShapeDtypeStruct(spread, jnp.int32),
            jax.ShapeDtypeStruct(spread, F32),
            jax.ShapeDtypeStruct((4, LANES), jnp.int32),
        ),
        in_specs=[smem, vmem],
        out_specs=(vmem,) * 3,
        scratch_shapes=[
            pltpu.VMEM((size.regs, SUB, LANES), jnp.int32),
            pltpu.VMEM((size.regs, SUB, LANES), F32),
        ],
        compiler_params=params,
        name="sort_edges",
    )(place, pay)
    edges = (bounds, keys, weights)
    edge_specs = [smem, vmem, vmem]
    scratch = [
        pltpu.VMEM((size.domain + size.windows[0], LANES), F32),
        pltpu.VMEM((size.extent + size.windows[1], LANES), F32),
        pltpu.VMEM((SUB, 16, size.parts * LANES), BF),
        pltpu.VMEM((SUB, 16, size.parts * LANES), BF),
        pltpu.VMEM((size.tables, SUB, LANES), F32),
    ]
    acc = pl.pallas_call(
        functools.partial(sketch_kernel, size),
        out_shape=(half, half),
        in_specs=edge_specs + [vmem],
        out_specs=(vmem, vmem),
        scratch_shapes=scratch,
        compiler_params=params,
        name="sketch",
    )(*edges, pay)
    got = exchange(*acc)
    *acc, v0, diag = pl.pallas_call(
        functools.partial(first_kernel, size),
        out_shape=(half, half, full, full),
        in_specs=edge_specs + [vmem] * 4,
        out_specs=(vmem,) * 4,
        scratch_shapes=scratch,
        compiler_params=params,
        name="operator_first",
    )(*edges, *acc, *got)
    got = exchange(*acc)
    *acc, v1 = pl.pallas_call(
        functools.partial(second_kernel, size),
        out_shape=(half, half, full),
        in_specs=edge_specs + [vmem] * 5,
        out_specs=(vmem,) * 3,
        scratch_shapes=scratch,
        compiler_params=params,
        name="operator_second",
    )(*edges, *acc, *got, diag)
    got = exchange(*acc)
    *acc, v2, moments = pl.pallas_call(
        functools.partial(third_kernel, size),
        out_shape=(half, half, full, jax.ShapeDtypeStruct((SUB, LANES), F32)),
        in_specs=edge_specs + [vmem] * 7,
        out_specs=(vmem,) * 4,
        scratch_shapes=scratch,
        compiler_params=params,
        name="operator_third",
    )(*edges, *acc, *got, diag, v0, v1)
    up = [(i, i + 1) for i in range(count - 1)]
    down = [(i + 1, i) for i in range(count - 1)]
    got_l = lax.ppermute(acc[1][:, size.reach :], "dom", up)
    got_r = lax.ppermute(acc[0][:, : size.reach], "dom", down)
    shared = total_over_dom(moments, count)
    out = pl.pallas_call(
        functools.partial(last_kernel, size),
        out_shape=jax.ShapeDtypeStruct((group, 2, SUB, size.verts), F32),
        in_specs=[vmem] * 9,
        out_specs=vmem,
        compiler_params=params,
        name="combine",
    )(shared, *acc, got_l, got_r, diag, v0, v1, v2)
    out = lax.all_to_all(out[:, :, : size.rows, :], "grp", 0, 0)
    return (out[:, 0].reshape(K, size.verts), out[:, 1].reshape(K, size.verts))


def solution(mesh):
    in_specs = (
        P(("dom", "grp")),
        P(("dom", "grp")),
        P(None, ("dom", "grp")),
        P(("dom", "grp")),
        P(("dom", "grp")),
    )
    out_specs = (P(None, ("dom", "grp")), P(None, ("dom", "grp")))
    return jax.shard_map(
        on_device, mesh=mesh, in_specs=in_specs, out_specs=out_specs, check_vma=False
    )
```

```python
import functools

import jax
import jax.numpy as jnp
from jax import lax
from jax.experimental import pallas as pl
from jax.experimental.pallas import tpu as pltpu
from jax.sharding import PartitionSpec as P

K = 24
HALF = 12
LANES = 128
SUB = 8
WIDE = 256
BF = jnp.bfloat16
F32 = jnp.float32


def row_of(block, r, count):
    return jnp.broadcast_to(block[r : r + 1, :], (count, LANES))


def expand(values, index, buf_v, buf_o, lanes, highs):
    top = values.astype(BF).astype(F32)
    rest = values - top
    big = index // WIDE
    for a in range(highs):
        here = big == a
        pair = jnp.concatenate([jnp.where(here, top, 0.0), jnp.where(here, rest, 0.0)], axis=0)
        buf_v[a * 16 : (a + 1) * 16, lanes] = pair.astype(BF)
    small = index % WIDE - lax.broadcasted_iota(jnp.int32, (SUB, LANES), 0)
    for j in range(WIDE // 16):
        pair = [jnp.where(small == 16 * j + 8 * h, 1.0, 0.0) for h in range(2)]
        buf_o[j * 16 : (j + 1) * 16, lanes] = jnp.concatenate(pair, axis=0).astype(BF)


def product(buf_v, buf_o, acc):
    acc[...] += lax.dot_general(
        buf_v[...], buf_o[...], (((1,), (1,)), ((), ())), preferred_element_type=F32
    )


def pick(table, index, first, blocks):
    low = index % LANES
    high = index // LANES
    out = jnp.zeros((SUB, LANES), F32)
    for a in range(blocks):
        part = table[:, first + a * LANES : first + (a + 1) * LANES]
        got = jnp.take_along_axis(part, low, axis=1, mode="promise_in_bounds")
        out = jnp.where(high == a, got, out)
    return out


class Sizes:
    def __init__(self, edev, verts, group):
        self.edev, self.verts, self.group = edev, verts, group
        self.domain = verts * group
        self.reach = self.domain // 2
        self.extent = self.domain + 2 * self.reach
        self.rows = K // group
        self.section = edev // LANES
        self.ground_rows = verts // LANES
        self.payload = -(-(5 * self.section + self.ground_rows) // SUB) * SUB
        self.per_device = self.section // SUB
        self.chunks = self.per_device * group
        self.high_h = self.domain // WIDE
        self.high_t = self.extent // WIDE

    def scratch(self):
        span = SUB * LANES
        one = [
            pltpu.VMEM((self.high_h * 16, span), BF),
            pltpu.VMEM((WIDE, span), BF),
            pltpu.VMEM((self.high_t * 16, span), BF),
            pltpu.VMEM((WIDE, span), BF),
        ]
        return one + one + [
            pltpu.VMEM((self.high_h * 16, WIDE), F32),
            pltpu.VMEM((self.high_t * 16, WIDE), F32),
        ]

    def block(self, pay, i, which):
        start = pl.multiple_of(which * self.section + (i % self.per_device) * SUB, SUB)
        return pay[i // self.per_device, pl.ds(start, SUB), :]


def sweep(size, fill, bufs):
    set_a, set_b, acc_h, acc_t = bufs[0:4], bufs[4:8], bufs[8], bufs[9]
    acc_h[...] = jnp.zeros_like(acc_h)
    acc_t[...] = jnp.zeros_like(acc_t)

    def use(bufs):
        product(bufs[0], bufs[1], acc_h)
        product(bufs[2], bufs[3], acc_t)

    fill(0, set_a)

    def step(i, carry):
        fill(2 * i + 1, set_b)
        use(set_a)
        fill((2 * i + 2) % size.chunks, set_a)
        use(set_b)
        return carry

    lax.fori_loop(0, size.chunks // 2, step, 0)


def collect(size, bufs, out_l, out_r):
    acc_h, acc_t = bufs[8], bufs[9]
    shift = size.reach // WIDE
    half = size.domain // WIDE
    for a in range(size.high_t):
        value = acc_t[a * 16 : a * 16 + 8, :] + acc_t[a * 16 + 8 : a * 16 + 16, :]
        h = a - shift
        if 0 <= h < size.high_h:
            value += acc_h[h * 16 : h * 16 + 8, :] + acc_h[h * 16 + 8 : h * 16 + 16, :]
        out, at = (out_l, a) if a < half else (out_r, a - half)
        out[:, at * WIDE : (at + 1) * WIDE] = value


def sketch_kernel(size, place, pay, out_l, out_r, *bufs):
    sub = lax.broadcasted_iota(jnp.int32, (SUB, LANES), 0)
    word, shift = place[0], place[1]
    is_sign = sub < size.rows

    def fill(i, bufs):
        heads = size.block(pay, i, 0).astype(jnp.int32)
        tails = size.block(pay, i, 1).astype(jnp.int32)
        signs = jnp.where(word == 0, size.block(pay, i, 2), size.block(pay, i, 3)).astype(jnp.int32)
        weight = size.block(pay, i, 4)
        root = jnp.sqrt(weight)
        for r in range(SUB):
            bit = jnp.right_shift(row_of(signs, r, SUB), sub + shift) & 1
            signed = (2 * bit - 1).astype(F32) * row_of(root, r, SUB)
            last = jnp.where(sub == size.rows, row_of(weight, r, SUB), 0.0)
            lanes = slice(r * LANES, (r + 1) * LANES)
            expand(jnp.where(is_sign, signed, last), row_of(heads, r, SUB), bufs[0], bufs[1], lanes, size.high_h)
            expand(jnp.where(is_sign, -signed, last), row_of(tails, r, SUB), bufs[2], bufs[3], lanes, size.high_t)

    sweep(size, fill, bufs)
    collect(size, bufs, out_l, out_r)
    for g in range(size.group):
        for r in range(size.ground_rows):
            at = size.reach + g * size.verts + r * LANES
            out, at = (out_l, at) if at < size.domain else (out_r, at - size.domain)
            row = 5 * size.section + r
            value = jnp.broadcast_to(pay[g, row : row + 1, :], (SUB, LANES))
            out[:, at : at + LANES] += jnp.where(sub == size.rows, value, 0.0)


def operator_core(size, pay, table, out_l, out_r, bufs):

    def fill(i, bufs):
        heads = size.block(pay, i, 0).astype(jnp.int32)
        tails = size.block(pay, i, 1).astype(jnp.int32)
        weight = size.block(pay, i, 4)
        for r in range(SUB):
            lanes = slice(r * LANES, (r + 1) * LANES)
            w = row_of(weight, r, SUB)
            at_head = pick(table, row_of(heads, r, SUB), size.reach, size.domain // LANES)
            at_tail = pick(table, row_of(tails, r, SUB), 0, size.extent // LANES)
            expand(w * at_tail, row_of(heads, r, SUB), bufs[0], bufs[1], lanes, size.high_h)
            expand(w * at_head, row_of(tails, r, SUB), bufs[2], bufs[3], lanes, size.high_t)

    sweep(size, fill, bufs)
    collect(size, bufs, out_l, out_r)


def halves(size, own_l, own_r, got_l, got_r):
    return ((0, own_l, got_l), (size.domain, own_r, got_r))


def first_kernel(size, pay, own_l, own_r, got_l, got_r, out_l, out_r, v, diag, *bufs):
    sub = lax.broadcasted_iota(jnp.int32, (SUB, size.domain), 0)
    for at, own, got in halves(size, own_l, own_r, got_l, got_r):
        total = own[...] + got[...]
        spread = jnp.broadcast_to(total[size.rows : size.rows + 1, :], total.shape)
        safe = jnp.where(spread > 0.0, spread, 1.0)
        diag[:, at : at + size.domain] = safe
        v[:, at : at + size.domain] = jnp.where(sub < size.rows, total / safe, 0.0)
    operator_core(size, pay, v, out_l, out_r, bufs)


def next_v(size, own_l, own_r, got_l, got_r, diag, v):
    for at, own, got in halves(size, own_l, own_r, got_l, got_r):
        v[:, at : at + size.domain] = (own[...] + got[...]) / diag[:, at : at + size.domain]


def second_kernel(size, pay, own_l, own_r, got_l, got_r, diag, out_l, out_r, v, *bufs):
    next_v(size, own_l, own_r, got_l, got_r, diag, v)
    operator_core(size, pay, v, out_l, out_r, bufs)


def third_kernel(size, pay, own_l, own_r, got_l, got_r, diag, v0, v1, out_l, out_r, v2, moments, *bufs):
    next_v(size, own_l, own_r, got_l, got_r, diag, v2)
    operator_core(size, pay, v2, out_l, out_r, bufs)
    lane = lax.broadcasted_iota(jnp.int32, (SUB, LANES), 1)
    middle = slice(size.reach, size.reach + size.domain)
    weighted = diag[:, middle] * v0[:, middle]
    other = diag[:, middle] * v1[:, middle]
    sums = [
        weighted * v0[:, middle],
        weighted * v1[:, middle],
        other * v1[:, middle],
        other * v2[:, middle],
        diag[:, middle] * v2[:, middle] * v2[:, middle],
        v2[:, : size.domain] * out_l[...] + v2[:, size.domain :] * out_r[...],
    ]
    out = jnp.zeros((SUB, LANES), F32)
    for k, value in enumerate(sums):
        out = jnp.where(lane == k, jnp.sum(value, axis=1, keepdims=True), out)
    moments[...] = out


def coefficients(mu):
    zero = jnp.zeros_like(mu[0])

    def inner(a, b):
        total = None
        for i, x in enumerate(a):
            for j, y in enumerate(b):
                term = mu[i + j] if x is None and y is None else mu[i + j] * (y if x is None else x if y is None else x * y)
                total = term if total is None else total + term
        return total

    def image(a):
        a = [jnp.ones_like(zero) if x is None else x for x in a] + [zero]
        return [a[0]] + [a[i] - a[i - 1] for i in range(1, len(a))]

    def ratio(top, bottom):
        return jnp.where(bottom > 0.0, top / jnp.where(bottom > 0.0, bottom, 1.0), 0.0)

    rho, pi, x = [jnp.ones_like(zero)], [jnp.ones_like(zero)], []
    gamma = inner(rho, rho)
    for step in range(3):
        moved = image(pi)
        alpha = ratio(gamma, inner(pi, moved))
        x = [(x[i] if i < len(x) else zero) + alpha * pi[i] for i in range(len(pi))]
        rho = [(rho[i] if i < len(rho) else zero) - alpha * moved[i] for i in range(len(moved))]
        if step < 2:
            following = inner(rho, rho)
            beta = ratio(following, gamma)
            pi = [rho[i] + (beta * pi[i] if i < len(pi) else zero) for i in range(len(rho))]
            gamma = following
    return x, rho


def last_kernel(size, moments, own_l, own_r, got_l, got_r, diag, v0, v1, v2, out):
    total = moments[...]
    mu = [jnp.broadcast_to(total[:, k : k + 1], (SUB, LANES)) for k in range(6)]
    x, rho = coefficients(mu)
    x = [value[:, :1] for value in x]
    rho = [value[:, :1] for value in rho]
    for g in range(size.group):
        at = size.reach + g * size.verts
        here = slice(at, at + size.verts)
        if at < size.domain:
            sums = own_l[:, here] + got_l[:, g * size.verts : (g + 1) * size.verts]
        else:
            back = at - size.domain
            inside = slice(back, back + size.verts)
            sums = own_r[:, inside] + got_r[:, inside]
        a, b, c, scale = v0[:, here], v1[:, here], v2[:, here], diag[:, here]
        out[g, 0] = x[0] * a + x[1] * b + x[2] * c
        out[g, 1] = scale * (rho[0] * a + rho[1] * b + rho[2] * c) + rho[3] * sums


def total_over_dom(value, count):
    if count & (count - 1):
        return jnp.sum(lax.all_gather(value, "dom"), axis=0)
    step = 1
    while step < count:
        value = value + lax.ppermute(value, "dom", [(i, i ^ step) for i in range(count)])
        step *= 2
    return value


def on_device(heads, tails, signs, edge_weights, ground):
    group = lax.axis_size("grp")
    count = lax.axis_size("dom")
    size = Sizes(heads.shape[0], ground.shape[0], group)
    vmem = pl.BlockSpec(memory_space=pltpu.VMEM)
    smem = pl.BlockSpec(memory_space=pltpu.SMEM)
    params = pltpu.CompilerParams(vmem_limit_bytes=48 * 1024 * 1024)

    def flat(value):
        return value.astype(F32).reshape(-1, LANES)

    parts = [flat(heads), flat(tails), flat(signs[0]), flat(signs[1]), flat(edge_weights), flat(ground)]
    used = sum(part.shape[0] for part in parts)
    parts.append(jnp.zeros((size.payload - used, LANES), F32))
    pay = lax.all_gather(jnp.concatenate(parts, axis=0), "grp")

    half = jax.ShapeDtypeStruct((SUB, size.domain), F32)
    full = jax.ShapeDtypeStruct((SUB, size.extent), F32)

    def exchange(left, right):
        up = [(i, i + 1) for i in range(count - 1)]
        down = [(i + 1, i) for i in range(count - 1)]
        return lax.ppermute(right, "dom", up), lax.ppermute(left, "dom", down)

    me = lax.axis_index("grp")
    first_row = me * size.rows
    place = jnp.stack([first_row // HALF, first_row % HALF]).astype(jnp.int32)
    acc = pl.pallas_call(
        functools.partial(sketch_kernel, size),
        out_shape=(half, half),
        in_specs=[smem, vmem],
        out_specs=(vmem, vmem),
        scratch_shapes=size.scratch(),
        compiler_params=params,
        name="sketch",
    )(place, pay)
    got = exchange(*acc)
    *acc, v0, diag = pl.pallas_call(
        functools.partial(first_kernel, size),
        out_shape=(half, half, full, full),
        in_specs=[vmem] * 5,
        out_specs=(vmem,) * 4,
        scratch_shapes=size.scratch(),
        compiler_params=params,
        name="operator_first",
    )(pay, *acc, *got)
    got = exchange(*acc)
    *acc, v1 = pl.pallas_call(
        functools.partial(second_kernel, size),
        out_shape=(half, half, full),
        in_specs=[vmem] * 6,
        out_specs=(vmem,) * 3,
        scratch_shapes=size.scratch(),
        compiler_params=params,
        name="operator_second",
    )(pay, *acc, *got, diag)
    got = exchange(*acc)
    *acc, v2, moments = pl.pallas_call(
        functools.partial(third_kernel, size),
        out_shape=(half, half, full, jax.ShapeDtypeStruct((SUB, LANES), F32)),
        in_specs=[vmem] * 8,
        out_specs=(vmem,) * 4,
        scratch_shapes=size.scratch(),
        compiler_params=params,
        name="operator_third",
    )(pay, *acc, *got, diag, v0, v1)
    up = [(i, i + 1) for i in range(count - 1)]
    down = [(i + 1, i) for i in range(count - 1)]
    got_l = lax.ppermute(acc[1][:, size.reach :], "dom", up)
    got_r = lax.ppermute(acc[0][:, : size.reach], "dom", down)
    shared = total_over_dom(moments, count)
    out = pl.pallas_call(
        functools.partial(last_kernel, size),
        out_shape=jax.ShapeDtypeStruct((group, 2, SUB, size.verts), F32),
        in_specs=[vmem] * 9,
        out_specs=vmem,
        compiler_params=params,
        name="combine",
    )(shared, *acc, got_l, got_r, diag, v0, v1, v2)
    out = lax.all_to_all(out[:, :, : size.rows, :], "grp", 0, 0)
    return (out[:, 0].reshape(K, size.verts), out[:, 1].reshape(K, size.verts))


def solution(mesh):
    in_specs = (
        P(("dom", "grp")),
        P(("dom", "grp")),
        P(None, ("dom", "grp")),
        P(("dom", "grp")),
        P(("dom", "grp")),
    )
    out_specs = (P(None, ("dom", "grp")), P(None, ("dom", "grp")))
    return jax.shard_map(
        on_device, mesh=mesh, in_specs=in_specs, out_specs=out_specs, check_vma=False
    )
```

```python
import functools

import jax
import jax.numpy as jnp
from jax import lax
from jax.experimental import pallas as pl
from jax.experimental.pallas import tpu as pltpu
from jax.sharding import PartitionSpec as P

K = 24
HALF = 12
LANES = 128
SUB = 8
BF = jnp.bfloat16
F32 = jnp.float32


def row_of(block, r, count):
    return jnp.broadcast_to(block[r : r + 1, :], (count, LANES))


def bits_of(n):
    return (n - 1).bit_length()


class Sizes:
    def __init__(self, edev, verts, group):
        self.edev, self.verts, self.group = edev, verts, group
        self.domain = verts * group
        self.reach = self.domain // 2
        self.extent = self.domain + 2 * self.reach
        self.rows = K // group
        self.section = edev // LANES
        self.ground_rows = verts // LANES
        self.payload = -(-(5 * self.section + self.ground_rows) // SUB) * SUB
        self.regs = edev * group // (SUB * LANES)
        self.parts = self.regs * SUB // LANES
        self.strip = self.domain // 8
        self.windows = (self.strip, self.extent // 16 + 64)
        self.blocks = (2 * self.strip // LANES, -(-(self.windows[1] + LANES - 1) // LANES))
        self.tables = self.extent // LANES + max(self.blocks)

    def pack(self, heads, tails, signs):
        strip = heads // self.strip
        turned = jnp.where(strip % 2 == 1, self.extent - 1 - tails, tails)
        key = strip * self.extent + turned
        key = key * self.strip + heads % self.strip
        return (key << self.rows) | signs

    def unpack(self, key):
        key = jnp.right_shift(key, self.rows)
        low, key = key & (self.strip - 1), jnp.right_shift(key, bits_of(self.strip))
        turned, strip = key & (self.extent - 1), jnp.right_shift(key, bits_of(self.extent))
        tails = jnp.where(strip & 1 == 1, self.extent - 1 - turned, turned)
        return strip * self.strip + low, tails


def flip_mask(size, level):
    low = bits_of(size.regs)
    if level >= low + 10:
        return None
    if level < low + 3:
        place = lax.broadcasted_iota(jnp.int32, (SUB, LANES), 0)
        bit = level - low
    else:
        place = lax.broadcasted_iota(jnp.int32, (SUB, LANES), 1)
        bit = level - low - 3
    return -(jnp.right_shift(place, bit) & 1)


def partner(size, j):
    low = bits_of(size.regs)
    axis, bit = (0, j - low) if j < low + 3 else (1, j - low - 3)
    place = lax.broadcasted_iota(jnp.int32, (SUB, LANES), axis)
    lower = (jnp.right_shift(place, bit) & 1) == 0
    index = jnp.bitwise_xor(place, 1 << bit)
    return axis, index, lower


def sort_edges(size, keys, weights):
    low = bits_of(size.regs)
    levels = low + 10

    def between(group, stages):
        key = {v: keys[v] for v in group}
        weight = {v: weights[v] for v in group}
        for level, j in stages:
            for v in group:
                if v >> j & 1:
                    continue
                a, b = v, v | 1 << j
                if level < low and v >> level & 1:
                    a, b = b, a
                swap = key[a] > key[b]
                key[a], key[b] = jnp.where(swap, key[b], key[a]), jnp.where(swap, key[a], key[b])
                weight[a], weight[b] = (
                    jnp.where(swap, weight[b], weight[a]),
                    jnp.where(swap, weight[a], weight[b]),
                )
        for v in group:
            keys[v] = key[v]
            weights[v] = weight[v]

    def registers(level):
        top = min(level, low)
        if top > 3:
            for v in range(8):
                between(list(range(v, size.regs, 8)), [(level, j) for j in range(top - 1, 2, -1)])
        for v in range(0, size.regs, 8):
            between(list(range(v, v + 8)), [(level, j) for j in range(min(top, 3) - 1, -1, -1)])

    for v in range(0, size.regs, 8):
        between(list(range(v, v + 8)), [(level, j) for level in (1, 2, 3) for j in range(level - 1, -1, -1)])
    for level in range(4, low):
        registers(level)

    for level in range(low, levels + 1):
        before = flip_mask(size, level - 1) if level > low else None
        now = flip_mask(size, level)
        flip = now if before is None else before if now is None else jnp.bitwise_xor(before, now)
        stages = [partner(size, j) for j in range(level - 1, low - 1, -1)]

        def across(i, carry, flip=flip, stages=stages):
            group = [i * 8 + u for u in range(8)]
            key = [jnp.bitwise_xor(keys[v], flip) for v in group]
            weight = [weights[v] for v in group]
            for axis, index, lower in stages:
                for u in range(8):
                    k, w = key[u], weight[u]
                    other = jnp.take_along_axis(k, index, axis=axis, mode="promise_in_bounds")
                    other_w = jnp.take_along_axis(w, index, axis=axis, mode="promise_in_bounds")
                    best = jnp.where(lower, jnp.minimum(k, other), jnp.maximum(k, other))
                    weight[u] = jnp.where(best == k, w, other_w)
                    key[u] = best
            for u, v in enumerate(group):
                keys[v] = key[u]
                weights[v] = weight[u]
            return carry

        lax.fori_loop(0, size.regs // 8, across, 0)
        registers(level)


def sort_kernel(size, place, pay, key_out, weight_out, bounds, keys, weights):
    word, shift = place[0], place[1]
    per = size.section // SUB
    mask = (1 << size.rows) - 1

    def section(which, g, c):
        return pay[g, which * size.section + c * SUB : which * size.section + (c + 1) * SUB, :]

    for g in range(size.group):
        for c in range(per):
            heads = section(0, g, c).astype(jnp.int32)
            tails = section(1, g, c).astype(jnp.int32)
            signs = jnp.where(word == 0, section(2, g, c), section(3, g, c)).astype(jnp.int32)
            v = g * per + c
            keys[v] = size.pack(heads, tails, jnp.right_shift(signs, shift) & mask)
            weights[v] = section(4, g, c)
    sort_edges(size, keys, weights)
    ends = [size.unpack(keys[v]) for v in range(size.regs)]
    lane = lax.broadcasted_iota(jnp.int32, (1, LANES), 1)
    wide = jnp.zeros((1, LANES), jnp.int32)
    runs = jnp.full((1, LANES), LANES, jnp.int32)
    for which in range(2):
        least = functools.reduce(jnp.minimum, [end[which] for end in ends])
        most = functools.reduce(jnp.maximum, [end[which] for end in ends])
        least = jnp.min(least, axis=0, keepdims=True)
        most = jnp.max(most, axis=0, keepdims=True)
        bounds[2 * which : 2 * which + 1, :] = least
        bounds[2 * which + 1 : 2 * which + 2, :] = most
        wide = jnp.maximum(wide, most // LANES - least // LANES - size.blocks[which] + 1)
        runs = jnp.where(most - (least & -8) >= size.windows[which], lane, runs)
    for step in (1, 2, 4, 8, 16, 32, 64):
        after = jnp.where(lane + step < LANES, jnp.roll(runs, -step, axis=1), LANES)
        runs = jnp.minimum(runs, after)
    bounds[4:5, :] = runs
    bounds[5:6, :] = jnp.broadcast_to(jnp.max(wide, axis=1, keepdims=True), (1, LANES))
    for j in range(size.parts):
        here = range(j * 16, (j + 1) * 16)
        key_out[j] = jnp.concatenate([keys[v] for v in here], axis=0).T
        weight_out[j] = jnp.concatenate([weights[v] for v in here], axis=0).T


def halves_of(value):
    high = value.astype(BF).astype(F32)
    return jnp.concatenate([high, value - high], axis=0).astype(BF)


def window_add(size, which, own, start, pair, acc):
    window = size.windows[which]
    iota = lax.broadcasted_iota(jnp.int32, (16, LANES), 0)
    rows = [(iota + 16 * m).astype(F32).astype(BF) for m in range(16)]
    zero, one = jnp.zeros((16, LANES), BF), jnp.ones((16, LANES), BF)
    hot = []
    for j in range(size.parts):
        column = []
        for at in range(0, window, 256):
            local = jnp.broadcast_to(own[j], (16, LANES)) - (start + at).astype(F32)
            local = local.astype(BF)
            count = min(256, window - at) // 16
            column += [jnp.where(local == rows[m], one, zero) for m in range(count)]
        hot.append(jnp.concatenate(column, axis=0))
    hot = jnp.concatenate(hot, axis=1)
    got = lax.dot_general(hot, pair, (((1,), (1,)), ((), ())), preferred_element_type=F32)
    acc[pl.ds(pl.multiple_of(start, SUB), window), 0:16] += got


def scatter_all(size, bounds, keys, held, accs):
    per = 2

    def step(i, carry):
        for u in range(per):
            ends = [size.unpack(block(keys, j, i * per + u)) for j in range(size.parts)]
            for q in range(SUB):
                run = (i * per + u) * SUB + q
                for which in range(2):
                    own = [end[which][q : q + 1, :].astype(F32) for end in ends]
                    start = bounds[2 * which, run] & -8
                    window_add(size, which, own, start, held[which][run], accs[which])
        return carry

    lax.fori_loop(0, LANES // SUB // per, step, 0)

    def more(run):
        ends = [size.unpack(keys[j, pl.ds(run, 1), :]) for j in range(size.parts)]
        for which in range(2):
            own = [end[which].astype(F32) for end in ends]
            start = bounds[2 * which, run] & -8
            span = bounds[2 * which + 1, run] - start

            def one(m, carry, which=which, own=own, start=start):
                window_add(size, which, own, start + m * size.windows[which], held[which][run], accs[which])
                return carry

            lax.fori_loop(1, span // size.windows[which] + 1, one, 0)
        following = bounds[4, jnp.minimum(run + 1, LANES - 1)]
        return jnp.where(run + 1 < LANES, following, LANES)

    lax.while_loop(lambda run: run < LANES, more, bounds[4, 0])


def collect(size, acc_h, acc_t, out_l, out_r):
    shift = size.reach // LANES
    half = size.domain // LANES

    def turned(acc, a):
        value = acc[a * LANES : (a + 1) * LANES, :].T
        return value[0:8, :] + value[8:16, :]

    for a in range(size.extent // LANES):
        value = turned(acc_t, a)
        h = a - shift
        if 0 <= h < half:
            value += turned(acc_h, h)
        out, at = (out_l, a) if a < half else (out_r, a - half)
        out[:, at * LANES : (at + 1) * LANES] = value


def clear(acc_h, acc_t):
    acc_h[...] = jnp.zeros_like(acc_h)
    acc_t[...] = jnp.zeros_like(acc_t)


def block(ref, j, i):
    return ref[j, pl.ds(pl.multiple_of(i * SUB, SUB), SUB), :]


def spread_lanes(j):
    return slice(j * LANES, (j + 1) * LANES)


def sketch_kernel(size, bounds, keys, weights, pay, out_l, out_r, acc_h, acc_t, held_h, held_t, tables):
    sub = lax.broadcasted_iota(jnp.int32, (SUB, LANES), 0)
    is_sign = sub < size.rows
    clear(acc_h, acc_t)

    def step(i, carry):
        for j in range(size.parts):
            key, weight = block(keys, j, i), block(weights, j, i)
            root = jnp.sqrt(weight)
            for q in range(SUB):
                bit = jnp.right_shift(row_of(key, q, SUB), sub) & 1
                signed = (2 * bit - 1).astype(F32) * row_of(root, q, SUB)
                last = jnp.where(sub == size.rows, row_of(weight, q, SUB), 0.0)
                held_h[i * SUB + q, :, spread_lanes(j)] = halves_of(jnp.where(is_sign, signed, last))
                held_t[i * SUB + q, :, spread_lanes(j)] = halves_of(jnp.where(is_sign, -signed, last))
        return carry

    lax.fori_loop(0, LANES // SUB, step, 0)
    scatter_all(size, bounds, keys, (held_h, held_t), (acc_h, acc_t))
    collect(size, acc_h, acc_t, out_l, out_r)
    for g in range(size.group):
        for r in range(size.ground_rows):
            at = size.reach + g * size.verts + r * LANES
            out, at = (out_l, at) if at < size.domain else (out_r, at - size.domain)
            row = 5 * size.section + r
            value = jnp.broadcast_to(pay[g, row : row + 1, :], (SUB, LANES))
            out[:, at : at + LANES] += jnp.where(sub == size.rows, value, 0.0)


def gather_all(size, bounds, keys, weights, held, tables):

    def take(which, low, high, a, out):
        shift = size.reach // LANES if which == 0 else 0
        got = jnp.take_along_axis(tables[shift + a], low, axis=1, mode="promise_in_bounds")
        return jnp.where(high == a, got, out)

    nothing = jnp.zeros((SUB, LANES), F32)

    def step(i, carry):
        for j in range(size.parts):
            ends, weight = size.unpack(block(keys, j, i)), block(weights, j, i)
            for which in range(2):
                low, high = ends[which] % LANES, ends[which] // LANES
                for q in range(SUB):
                    run = i * SUB + q
                    first = bounds[2 * which, run] // LANES
                    out = nothing
                    for a in range(size.blocks[which]):
                        out = take(which, row_of(low, q, SUB), row_of(high, q, SUB), first + a, out)
                    held[1 - which][run, :, spread_lanes(j)] = halves_of(out * row_of(weight, q, SUB))
        return carry

    lax.fori_loop(0, LANES // SUB, step, 0)

    @pl.when(bounds[5, 0] > 0)
    def _():
        def whole(run, carry):
            for j in range(size.parts):
                ends = size.unpack(keys[j, pl.ds(run, 1), :])
                weight = jnp.broadcast_to(weights[j, pl.ds(run, 1), :], (SUB, LANES))
                for which in range(2):
                    end = jnp.broadcast_to(ends[which], (SUB, LANES))
                    out = lax.fori_loop(
                        bounds[2 * which, run] // LANES,
                        bounds[2 * which + 1, run] // LANES + 1,
                        lambda a, out, which=which, end=end: take(which, end % LANES, end // LANES, a, out),
                        nothing,
                    )
                    held[1 - which][run, :, spread_lanes(j)] = halves_of(out * weight)
            return carry

        lax.fori_loop(0, LANES, whole, 0)


def operator_core(size, bounds, keys, weights, table, out_l, out_r, bufs):
    acc_h, acc_t, held_h, held_t, tables = bufs
    clear(acc_h, acc_t)
    for a in range(size.extent // LANES):
        tables[a] = table[:, a * LANES : (a + 1) * LANES]
    gather_all(size, bounds, keys, weights, (held_h, held_t), tables)
    scatter_all(size, bounds, keys, (held_h, held_t), (acc_h, acc_t))
    collect(size, acc_h, acc_t, out_l, out_r)


def halves(size, own_l, own_r, got_l, got_r):
    return ((0, own_l, got_l), (size.domain, own_r, got_r))


def first_kernel(size, bounds, keys, weights, own_l, own_r, got_l, got_r, out_l, out_r, v, diag, *bufs):
    sub = lax.broadcasted_iota(jnp.int32, (SUB, size.domain), 0)
    for at, own, got in halves(size, own_l, own_r, got_l, got_r):
        total = own[...] + got[...]
        spread = jnp.broadcast_to(total[size.rows : size.rows + 1, :], total.shape)
        safe = jnp.where(spread > 0.0, spread, 1.0)
        diag[:, at : at + size.domain] = safe
        v[:, at : at + size.domain] = jnp.where(sub < size.rows, total / safe, 0.0)
    operator_core(size, bounds, keys, weights, v, out_l, out_r, bufs)


def next_v(size, own_l, own_r, got_l, got_r, diag, v):
    for at, own, got in halves(size, own_l, own_r, got_l, got_r):
        v[:, at : at + size.domain] = (own[...] + got[...]) / diag[:, at : at + size.domain]


def second_kernel(size, bounds, keys, weights, own_l, own_r, got_l, got_r, diag, out_l, out_r, v, *bufs):
    next_v(size, own_l, own_r, got_l, got_r, diag, v)
    operator_core(size, bounds, keys, weights, v, out_l, out_r, bufs)


def third_kernel(size, bounds, keys, weights, own_l, own_r, got_l, got_r, diag, v0, v1, out_l, out_r, v2, moments, *bufs):
    next_v(size, own_l, own_r, got_l, got_r, diag, v2)
    operator_core(size, bounds, keys, weights, v2, out_l, out_r, bufs)
    lane = lax.broadcasted_iota(jnp.int32, (SUB, LANES), 1)
    middle = slice(size.reach, size.reach + size.domain)
    weighted = diag[:, middle] * v0[:, middle]
    other = diag[:, middle] * v1[:, middle]
    sums = [
        weighted * v0[:, middle],
        weighted * v1[:, middle],
        other * v1[:, middle],
        other * v2[:, middle],
        diag[:, middle] * v2[:, middle] * v2[:, middle],
        v2[:, : size.domain] * out_l[...] + v2[:, size.domain :] * out_r[...],
    ]
    out = jnp.zeros((SUB, LANES), F32)
    for k, value in enumerate(sums):
        out = jnp.where(lane == k, jnp.sum(value, axis=1, keepdims=True), out)
    moments[...] = out


def coefficients(mu):
    zero = jnp.zeros_like(mu[0])

    def inner(a, b):
        total = None
        for i, x in enumerate(a):
            for j, y in enumerate(b):
                term = mu[i + j] if x is None and y is None else mu[i + j] * (y if x is None else x if y is None else x * y)
                total = term if total is None else total + term
        return total

    def image(a):
        a = [jnp.ones_like(zero) if x is None else x for x in a] + [zero]
        return [a[0]] + [a[i] - a[i - 1] for i in range(1, len(a))]

    def ratio(top, bottom):
        return jnp.where(bottom > 0.0, top / jnp.where(bottom > 0.0, bottom, 1.0), 0.0)

    rho, pi, x = [jnp.ones_like(zero)], [jnp.ones_like(zero)], []
    gamma = inner(rho, rho)
    for step in range(3):
        moved = image(pi)
        alpha = ratio(gamma, inner(pi, moved))
        x = [(x[i] if i < len(x) else zero) + alpha * pi[i] for i in range(len(pi))]
        rho = [(rho[i] if i < len(rho) else zero) - alpha * moved[i] for i in range(len(moved))]
        if step < 2:
            following = inner(rho, rho)
            beta = ratio(following, gamma)
            pi = [rho[i] + (beta * pi[i] if i < len(pi) else zero) for i in range(len(rho))]
            gamma = following
    return x, rho


def last_kernel(size, moments, own_l, own_r, got_l, got_r, diag, v0, v1, v2, out):
    total = moments[...]
    mu = [jnp.broadcast_to(total[:, k : k + 1], (SUB, LANES)) for k in range(6)]
    x, rho = coefficients(mu)
    x = [value[:, :1] for value in x]
    rho = [value[:, :1] for value in rho]
    for g in range(size.group):
        at = size.reach + g * size.verts
        here = slice(at, at + size.verts)
        if at < size.domain:
            sums = own_l[:, here] + got_l[:, g * size.verts : (g + 1) * size.verts]
        else:
            back = at - size.domain
            inside = slice(back, back + size.verts)
            sums = own_r[:, inside] + got_r[:, inside]
        a, b, c, scale = v0[:, here], v1[:, here], v2[:, here], diag[:, here]
        out[g, 0] = x[0] * a + x[1] * b + x[2] * c
        out[g, 1] = scale * (rho[0] * a + rho[1] * b + rho[2] * c) + rho[3] * sums


def total_over_dom(value, count):
    if count & (count - 1):
        return jnp.sum(lax.all_gather(value, "dom"), axis=0)
    step = 1
    while step < count:
        value = value + lax.ppermute(value, "dom", [(i, i ^ step) for i in range(count)])
        step *= 2
    return value


def on_device(heads, tails, signs, edge_weights, ground):
    group = lax.axis_size("grp")
    count = lax.axis_size("dom")
    size = Sizes(heads.shape[0], ground.shape[0], group)
    vmem = pl.BlockSpec(memory_space=pltpu.VMEM)
    smem = pl.BlockSpec(memory_space=pltpu.SMEM)
    params = pltpu.CompilerParams(vmem_limit_bytes=48 * 1024 * 1024)

    def flat(value):
        return value.astype(F32).reshape(-1, LANES)

    parts = [flat(heads), flat(tails), flat(signs[0]), flat(signs[1]), flat(edge_weights), flat(ground)]
    used = sum(part.shape[0] for part in parts)
    parts.append(jnp.zeros((size.payload - used, LANES), F32))
    pay = lax.all_gather(jnp.concatenate(parts, axis=0), "grp")

    half = jax.ShapeDtypeStruct((SUB, size.domain), F32)
    full = jax.ShapeDtypeStruct((SUB, size.extent), F32)

    def exchange(left, right):
        up = [(i, i + 1) for i in range(count - 1)]
        down = [(i + 1, i) for i in range(count - 1)]
        return lax.ppermute(right, "dom", up), lax.ppermute(left, "dom", down)

    me = lax.axis_index("grp")
    first_row = me * size.rows
    place = jnp.stack([first_row // HALF, first_row % HALF]).astype(jnp.int32)
    spread = (size.parts, LANES, LANES)
    keys, weights, bounds = pl.pallas_call(
        functools.partial(sort_kernel, size),
        out_shape=(
            jax.ShapeDtypeStruct(spread, jnp.int32),
            jax.ShapeDtypeStruct(spread, F32),
            jax.ShapeDtypeStruct((SUB, LANES), jnp.int32),
        ),
        in_specs=[smem, vmem],
        out_specs=(vmem,) * 3,
        scratch_shapes=[
            pltpu.VMEM((size.regs, SUB, LANES), jnp.int32),
            pltpu.VMEM((size.regs, SUB, LANES), F32),
        ],
        compiler_params=params,
        name="sort_edges",
    )(place, pay)
    edges = (bounds, keys, weights)
    edge_specs = [smem, vmem, vmem]
    scratch = [
        pltpu.VMEM((size.domain + size.windows[0], LANES), F32),
        pltpu.VMEM((size.extent + size.windows[1], LANES), F32),
        pltpu.VMEM((LANES, 16, size.parts * LANES), BF),
        pltpu.VMEM((LANES, 16, size.parts * LANES), BF),
        pltpu.VMEM((size.tables, SUB, LANES), F32),
    ]
    acc = pl.pallas_call(
        functools.partial(sketch_kernel, size),
        out_shape=(half, half),
        in_specs=edge_specs + [vmem],
        out_specs=(vmem, vmem),
        scratch_shapes=scratch,
        compiler_params=params,
        name="sketch",
    )(*edges, pay)
    got = exchange(*acc)
    *acc, v0, diag = pl.pallas_call(
        functools.partial(first_kernel, size),
        out_shape=(half, half, full, full),
        in_specs=edge_specs + [vmem] * 4,
        out_specs=(vmem,) * 4,
        scratch_shapes=scratch,
        compiler_params=params,
        name="operator_first",
    )(*edges, *acc, *got)
    got = exchange(*acc)
    *acc, v1 = pl.pallas_call(
        functools.partial(second_kernel, size),
        out_shape=(half, half, full),
        in_specs=edge_specs + [vmem] * 5,
        out_specs=(vmem,) * 3,
        scratch_shapes=scratch,
        compiler_params=params,
        name="operator_second",
    )(*edges, *acc, *got, diag)
    got = exchange(*acc)
    *acc, v2, moments = pl.pallas_call(
        functools.partial(third_kernel, size),
        out_shape=(half, half, full, jax.ShapeDtypeStruct((SUB, LANES), F32)),
        in_specs=edge_specs + [vmem] * 7,
        out_specs=(vmem,) * 4,
        scratch_shapes=scratch,
        compiler_params=params,
        name="operator_third",
    )(*edges, *acc, *got, diag, v0, v1)
    up = [(i, i + 1) for i in range(count - 1)]
    down = [(i + 1, i) for i in range(count - 1)]
    got_l = lax.ppermute(acc[1][:, size.reach :], "dom", up)
    got_r = lax.ppermute(acc[0][:, : size.reach], "dom", down)
    shared = total_over_dom(moments, count)
    out = pl.pallas_call(
        functools.partial(last_kernel, size),
        out_shape=jax.ShapeDtypeStruct((group, 2, SUB, size.verts), F32),
        in_specs=[vmem] * 9,
        out_specs=vmem,
        compiler_params=params,
        name="combine",
    )(shared, *acc, got_l, got_r, diag, v0, v1, v2)
    out = lax.all_to_all(out[:, :, : size.rows, :], "grp", 0, 0)
    return (out[:, 0].reshape(K, size.verts), out[:, 1].reshape(K, size.verts))


def solution(mesh):
    in_specs = (
        P(("dom", "grp")),
        P(("dom", "grp")),
        P(None, ("dom", "grp")),
        P(("dom", "grp")),
        P(("dom", "grp")),
    )
    out_specs = (P(None, ("dom", "grp")), P(None, ("dom", "grp")))
    return jax.shard_map(
        on_device, mesh=mesh, in_specs=in_specs, out_specs=out_specs, check_vma=False
    )
```

```python
import functools

import jax
import jax.numpy as jnp
from jax import lax
from jax.experimental import pallas as pl
from jax.experimental.pallas import tpu as pltpu
from jax.sharding import PartitionSpec as P

K = 24
HALF = 12
LANES = 128
SUB = 8
BF = jnp.bfloat16
F32 = jnp.float32


def row_of(block, r, count):
    return jnp.broadcast_to(block[r : r + 1, :], (count, LANES))


def bits_of(n):
    return (n - 1).bit_length()


class Sizes:
    def __init__(self, edev, verts, group):
        self.edev, self.verts, self.group = edev, verts, group
        self.domain = verts * group
        self.reach = self.domain // 2
        self.extent = self.domain + 2 * self.reach
        self.rows = K // group
        self.section = edev // LANES
        self.ground_rows = verts // LANES
        self.payload = -(-(5 * self.section + self.ground_rows) // SUB) * SUB
        self.regs = edev * group // (SUB * LANES)
        self.parts = self.regs * SUB // LANES
        self.strip = self.domain // 8
        self.blocks = (self.strip // LANES, self.extent // 16 // LANES + 1)
        self.most = (2 * self.blocks[0], self.blocks[1] + 1)
        self.listed = 16

    def padded(self, which):
        return (self.domain, self.extent)[which] // LANES + self.most[which]

    def pack(self, heads, tails, signs):
        strip = heads // self.strip
        turned = jnp.where(strip % 2 == 1, self.extent - 1 - tails, tails)
        key = strip * self.extent + turned
        key = key * self.strip + heads % self.strip
        return (key << self.rows) | signs

    def unpack(self, key):
        key = jnp.right_shift(key, self.rows)
        low, key = key & (self.strip - 1), jnp.right_shift(key, bits_of(self.strip))
        turned, strip = key & (self.extent - 1), jnp.right_shift(key, bits_of(self.extent))
        tails = jnp.where(strip & 1 == 1, self.extent - 1 - turned, turned)
        return strip * self.strip + low, tails


def flip_mask(size, level):
    low = bits_of(size.regs)
    if level >= low + 10:
        return None
    if level < low + 3:
        place = lax.broadcasted_iota(jnp.int32, (SUB, LANES), 0)
        bit = level - low
    else:
        place = lax.broadcasted_iota(jnp.int32, (SUB, LANES), 1)
        bit = level - low - 3
    return -(jnp.right_shift(place, bit) & 1)


def partner(size, j):
    low = bits_of(size.regs)
    axis, bit = (0, j - low) if j < low + 3 else (1, j - low - 3)
    place = lax.broadcasted_iota(jnp.int32, (SUB, LANES), axis)
    lower = (jnp.right_shift(place, bit) & 1) == 0
    index = jnp.bitwise_xor(place, 1 << bit)
    return axis, index, lower


def sort_edges(size, keys, weights):
    low = bits_of(size.regs)
    levels = low + 10

    def between(group, stages):
        key = {v: keys[v] for v in group}
        weight = {v: weights[v] for v in group}
        for level, j in stages:
            for v in group:
                if v >> j & 1:
                    continue
                a, b = v, v | 1 << j
                if level < low and v >> level & 1:
                    a, b = b, a
                swap = key[a] > key[b]
                key[a], key[b] = jnp.where(swap, key[b], key[a]), jnp.where(swap, key[a], key[b])
                weight[a], weight[b] = (
                    jnp.where(swap, weight[b], weight[a]),
                    jnp.where(swap, weight[a], weight[b]),
                )
        for v in group:
            keys[v] = key[v]
            weights[v] = weight[v]

    def registers(level):
        top = min(level, low)
        if top > 3:
            for v in range(8):
                between(list(range(v, size.regs, 8)), [(level, j) for j in range(top - 1, 2, -1)])
        for v in range(0, size.regs, 8):
            between(list(range(v, v + 8)), [(level, j) for j in range(min(top, 3) - 1, -1, -1)])

    for v in range(0, size.regs, 8):
        between(list(range(v, v + 8)), [(level, j) for level in (1, 2, 3) for j in range(level - 1, -1, -1)])
    for level in range(4, low):
        registers(level)

    for level in range(low, levels + 1):
        before = flip_mask(size, level - 1) if level > low else None
        now = flip_mask(size, level)
        flip = now if before is None else before if now is None else jnp.bitwise_xor(before, now)
        stages = [partner(size, j) for j in range(level - 1, low - 1, -1)]

        def across(i, carry, flip=flip, stages=stages):
            group = [i * 8 + u for u in range(8)]
            key = [jnp.bitwise_xor(keys[v], flip) for v in group]
            weight = [weights[v] for v in group]
            for axis, index, lower in stages:
                for u in range(8):
                    k, w = key[u], weight[u]
                    other = jnp.take_along_axis(k, index, axis=axis, mode="promise_in_bounds")
                    other_w = jnp.take_along_axis(w, index, axis=axis, mode="promise_in_bounds")
                    best = jnp.where(lower, jnp.minimum(k, other), jnp.maximum(k, other))
                    weight[u] = jnp.where(best == k, w, other_w)
                    key[u] = best
            for u, v in enumerate(group):
                keys[v] = key[u]
                weights[v] = weight[u]
            return carry

        lax.fori_loop(0, size.regs // 8, across, 0)
        registers(level)


def sort_kernel(size, place, pay, key_out, heads_out, tails_out, weight_out, bounds, keys, weights):
    word, shift = place[0], place[1]
    per = size.section // SUB
    mask = (1 << size.rows) - 1

    def section(which, g, c):
        return pay[g, which * size.section + c * SUB : which * size.section + (c + 1) * SUB, :]

    for g in range(size.group):
        for c in range(per):
            heads = section(0, g, c).astype(jnp.int32)
            tails = section(1, g, c).astype(jnp.int32)
            signs = jnp.where(word == 0, section(2, g, c), section(3, g, c)).astype(jnp.int32)
            v = g * per + c
            keys[v] = size.pack(heads, tails, jnp.right_shift(signs, shift) & mask)
            weights[v] = section(4, g, c)
    sort_edges(size, keys, weights)
    ends = [size.unpack(keys[v]) for v in range(size.regs)]
    lane = lax.broadcasted_iota(jnp.int32, (1, LANES), 1)
    far = rare = lane < 0
    for which in range(2):
        least = functools.reduce(jnp.minimum, [end[which] for end in ends])
        most = functools.reduce(jnp.maximum, [end[which] for end in ends])
        least = jnp.min(least, axis=0, keepdims=True) // LANES
        most = jnp.max(most, axis=0, keepdims=True) // LANES
        bounds[2 * which : 2 * which + 1, :] = least
        bounds[2 * which + 1 : 2 * which + 2, :] = most
        far = far | (most - least >= size.blocks[which])
        rare = rare | (most - least >= size.most[which])
    runs = jnp.where(far, lane, LANES)
    count = jnp.sum(far.astype(F32), axis=1, keepdims=True)
    rare = jnp.max(jnp.where(rare, 1.0, 0.0), axis=1, keepdims=True)
    rare = jnp.maximum(rare, jnp.where(count > size.listed, 1.0, 0.0)).astype(jnp.int32)
    for step in (1, 2, 4, 8, 16, 32, 64):
        after = jnp.where(lane + step < LANES, jnp.roll(runs, -step, axis=1), LANES)
        runs = jnp.minimum(runs, after)
    bounds[4:5, :] = runs
    bounds[5:6, :] = jnp.broadcast_to(rare, (1, LANES))
    for j in range(size.parts):
        here = range(j * 16, (j + 1) * 16)
        key = jnp.concatenate([keys[v] for v in here], axis=0).T
        key_out[j] = key
        heads_out[j], tails_out[j] = size.unpack(key)
        weight_out[j] = jnp.concatenate([weights[v] for v in here], axis=0).T


def halves_of(value):
    high = value.astype(BF).astype(F32)
    return jnp.concatenate([high, value - high], axis=0).astype(BF)


def row(ref, j, run, count):
    return jnp.broadcast_to(ref[j, pl.ds(run, 1), :], (count, LANES))


def next_far(bounds, run):
    following = bounds[4, jnp.minimum(run + 1, LANES - 1)]
    return jnp.where(run + 1 < LANES, following, LANES)


def window_add(size, index, run, first, begin, end, pair, acc, valid=True):
    iota = lax.broadcasted_iota(jnp.int32, (16, LANES), 0)
    rows = [(iota + 16 * m).astype(F32).astype(BF) for m in range(16)]
    zero, one = jnp.zeros((16, LANES), BF), jnp.ones((16, LANES), BF)
    start = (first + begin) * LANES
    if valid is not True:
        start = jnp.where(valid, start, -(1 << 20))
    window = (end - begin) * LANES
    hot = []
    for j in range(size.parts):
        column = []
        for at in range(0, window, 256):
            local = (row(index, j, run, 16) - (start + at)).astype(F32).astype(BF)
            count = min(256, window - at) // 16
            column += [jnp.where(local == rows[m], one, zero) for m in range(count)]
        hot.append(jnp.concatenate(column, axis=0))
    hot = jnp.concatenate(hot, axis=1)
    got = lax.dot_general(pair, hot, (((1,), (1,)), ((), ())), preferred_element_type=F32)
    for b in range(end - begin):
        acc[first + begin + b] += got[:, b * LANES : (b + 1) * LANES]


def scatter_all(size, bounds, ends, held, accs):
    per = 16

    def step(i, carry):
        for q in range(per):
            run = i * per + q
            for which in range(2):
                first = bounds[2 * which, run]
                window_add(size, ends[which], run, first, 0, size.blocks[which], held[which][run], accs[which])
        return carry

    lax.fori_loop(0, LANES // per, step, 0)

    @pl.when(bounds[5, 0] == 0)
    def _():
        def four(i, run):
            for _ in range(4):
                valid, here = run < LANES, jnp.minimum(run, LANES - 1)
                for which in range(2):
                    first = bounds[2 * which, here]
                    window_add(
                        size, ends[which], here, first, size.blocks[which], size.most[which],
                        held[which][here], accs[which], valid,
                    )
                run = jnp.where(valid, next_far(bounds, here), LANES)
            return run

        lax.fori_loop(0, size.listed // 4, four, bounds[4, 0])

    @pl.when(bounds[5, 0] != 0)
    def _():
        def more(run):
            for which in range(2):
                def one(a, carry, which=which):
                    window_add(size, ends[which], run, a, 0, 1, held[which][run], accs[which])
                    return carry

                first, last = bounds[2 * which, run], bounds[2 * which + 1, run]
                lax.fori_loop(first + size.blocks[which], last + 1, one, 0)
            return next_far(bounds, run)

        lax.while_loop(lambda run: run < LANES, more, bounds[4, 0])


def collect(size, acc_h, acc_t, out_l, out_r):
    shift = size.reach // LANES
    half = size.domain // LANES
    for a in range(size.extent // LANES):
        value = acc_t[a, 0:8] + acc_t[a, 8:16]
        h = a - shift
        if 0 <= h < half:
            value += acc_h[h, 0:8] + acc_h[h, 8:16]
        out, at = (out_l, a) if a < half else (out_r, a - half)
        out[:, at * LANES : (at + 1) * LANES] = value


def clear(acc_h, acc_t):
    acc_h[...] = jnp.zeros_like(acc_h)
    acc_t[...] = jnp.zeros_like(acc_t)


def spread_lanes(j):
    return slice(j * LANES, (j + 1) * LANES)


def sketch_kernel(size, bounds, keys, heads, tails, weights, pay, out_l, out_r, acc_h, acc_t, held_h, held_t, tables):
    sub = lax.broadcasted_iota(jnp.int32, (SUB, LANES), 0)
    is_sign = sub < size.rows
    clear(acc_h, acc_t)

    def step(i, carry):
        for j in range(size.parts):
            for q in range(SUB):
                run = i * SUB + q
                weight = row(weights, j, run, SUB)
                bit = jnp.right_shift(row(keys, j, run, SUB), sub) & 1
                signed = (2 * bit - 1).astype(F32) * jnp.sqrt(weight)
                last = jnp.where(sub == size.rows, weight, 0.0)
                held_h[run, :, spread_lanes(j)] = halves_of(jnp.where(is_sign, signed, last))
                held_t[run, :, spread_lanes(j)] = halves_of(jnp.where(is_sign, -signed, last))
        return carry

    lax.fori_loop(0, LANES // SUB, step, 0)
    scatter_all(size, bounds, (heads, tails), (held_h, held_t), (acc_h, acc_t))
    collect(size, acc_h, acc_t, out_l, out_r)
    for g in range(size.group):
        for r in range(size.ground_rows):
            at = size.reach + g * size.verts + r * LANES
            out, at = (out_l, at) if at < size.domain else (out_r, at - size.domain)
            line = 5 * size.section + r
            value = jnp.broadcast_to(pay[g, line : line + 1, :], (SUB, LANES))
            out[:, at : at + LANES] += jnp.where(sub == size.rows, value, 0.0)


def gather_all(size, bounds, ends, weights, held, tables):

    def take(which, low, high, a, out):
        shift = size.reach // LANES if which == 0 else 0
        got = jnp.take_along_axis(tables[shift + a], low, axis=1, mode="promise_in_bounds")
        return jnp.where(high == a, got, out)

    nothing = jnp.zeros((SUB, LANES), F32)

    def one(run, counts):
        for j in range(size.parts):
            weight = row(weights, j, run, SUB)
            for which in range(2):
                index = row(ends[which], j, run, SUB)
                first = bounds[2 * which, run]
                low, high = index % LANES, index // LANES
                if counts is None:
                    out = lax.fori_loop(
                        first, bounds[2 * which + 1, run] + 1,
                        lambda a, out: take(which, low, high, a, out), nothing,
                    )
                else:
                    out = nothing
                    for a in range(counts[which]):
                        out = take(which, low, high, first + a, out)
                held[1 - which][run, :, spread_lanes(j)] = halves_of(out * weight)

    def step(i, carry):
        for q in range(SUB):
            one(i * SUB + q, size.blocks)
        return carry

    lax.fori_loop(0, LANES // SUB, step, 0)

    @pl.when(bounds[5, 0] == 0)
    def _():
        def four(i, run):
            for _ in range(4):
                here = jnp.minimum(run, LANES - 1)
                one(here, size.most)
                run = jnp.where(run < LANES, next_far(bounds, here), LANES)
            return run

        lax.fori_loop(0, size.listed // 4, four, bounds[4, 0])

    @pl.when(bounds[5, 0] != 0)
    def _():
        def more(run):
            one(run, None)
            return next_far(bounds, run)

        lax.while_loop(lambda run: run < LANES, more, bounds[4, 0])


def operator_core(size, bounds, heads, tails, weights, table, out_l, out_r, bufs):
    acc_h, acc_t, held_h, held_t, tables = bufs
    clear(acc_h, acc_t)
    for a in range(size.extent // LANES):
        tables[a] = table[:, a * LANES : (a + 1) * LANES]
    ends = (heads, tails)
    gather_all(size, bounds, ends, weights, (held_h, held_t), tables)
    scatter_all(size, bounds, ends, (held_h, held_t), (acc_h, acc_t))
    collect(size, acc_h, acc_t, out_l, out_r)


def halves(size, own_l, own_r, got_l, got_r):
    return ((0, own_l, got_l), (size.domain, own_r, got_r))


def first_kernel(size, bounds, heads, tails, weights, own_l, own_r, got_l, got_r, out_l, out_r, v, diag, *bufs):
    sub = lax.broadcasted_iota(jnp.int32, (SUB, size.domain), 0)
    for at, own, got in halves(size, own_l, own_r, got_l, got_r):
        total = own[...] + got[...]
        spread = jnp.broadcast_to(total[size.rows : size.rows + 1, :], total.shape)
        safe = jnp.where(spread > 0.0, spread, 1.0)
        diag[:, at : at + size.domain] = safe
        v[:, at : at + size.domain] = jnp.where(sub < size.rows, total / safe, 0.0)
    operator_core(size, bounds, heads, tails, weights, v, out_l, out_r, bufs)


def next_v(size, own_l, own_r, got_l, got_r, diag, v):
    for at, own, got in halves(size, own_l, own_r, got_l, got_r):
        v[:, at : at + size.domain] = (own[...] + got[...]) / diag[:, at : at + size.domain]


def second_kernel(size, bounds, heads, tails, weights, own_l, own_r, got_l, got_r, diag, out_l, out_r, v, *bufs):
    next_v(size, own_l, own_r, got_l, got_r, diag, v)
    operator_core(size, bounds, heads, tails, weights, v, out_l, out_r, bufs)


def third_kernel(size, bounds, heads, tails, weights, own_l, own_r, got_l, got_r, diag, v0, v1, out_l, out_r, v2, moments, *bufs):
    next_v(size, own_l, own_r, got_l, got_r, diag, v2)
    operator_core(size, bounds, heads, tails, weights, v2, out_l, out_r, bufs)
    lane = lax.broadcasted_iota(jnp.int32, (SUB, LANES), 1)
    middle = slice(size.reach, size.reach + size.domain)
    weighted = diag[:, middle] * v0[:, middle]
    other = diag[:, middle] * v1[:, middle]
    sums = [
        weighted * v0[:, middle],
        weighted * v1[:, middle],
        other * v1[:, middle],
        other * v2[:, middle],
        diag[:, middle] * v2[:, middle] * v2[:, middle],
        v2[:, : size.domain] * out_l[...] + v2[:, size.domain :] * out_r[...],
    ]
    out = jnp.zeros((SUB, LANES), F32)
    for k, value in enumerate(sums):
        out = jnp.where(lane == k, jnp.sum(value, axis=1, keepdims=True), out)
    moments[...] = out


def coefficients(mu):
    zero = jnp.zeros_like(mu[0])

    def inner(a, b):
        total = None
        for i, x in enumerate(a):
            for j, y in enumerate(b):
                term = mu[i + j] if x is None and y is None else mu[i + j] * (y if x is None else x if y is None else x * y)
                total = term if total is None else total + term
        return total

    def image(a):
        a = [jnp.ones_like(zero) if x is None else x for x in a] + [zero]
        return [a[0]] + [a[i] - a[i - 1] for i in range(1, len(a))]

    def ratio(top, bottom):
        return jnp.where(bottom > 0.0, top / jnp.where(bottom > 0.0, bottom, 1.0), 0.0)

    rho, pi, x = [jnp.ones_like(zero)], [jnp.ones_like(zero)], []
    gamma = inner(rho, rho)
    for step in range(3):
        moved = image(pi)
        alpha = ratio(gamma, inner(pi, moved))
        x = [(x[i] if i < len(x) else zero) + alpha * pi[i] for i in range(len(pi))]
        rho = [(rho[i] if i < len(rho) else zero) - alpha * moved[i] for i in range(len(moved))]
        if step < 2:
            following = inner(rho, rho)
            beta = ratio(following, gamma)
            pi = [rho[i] + (beta * pi[i] if i < len(pi) else zero) for i in range(len(rho))]
            gamma = following
    return x, rho


def last_kernel(size, moments, own_l, own_r, got_l, got_r, diag, v0, v1, v2, out):
    total = moments[...]
    mu = [jnp.broadcast_to(total[:, k : k + 1], (SUB, LANES)) for k in range(6)]
    x, rho = coefficients(mu)
    x = [value[:, :1] for value in x]
    rho = [value[:, :1] for value in rho]
    for g in range(size.group):
        at = size.reach + g * size.verts
        here = slice(at, at + size.verts)
        if at < size.domain:
            sums = own_l[:, here] + got_l[:, g * size.verts : (g + 1) * size.verts]
        else:
            back = at - size.domain
            inside = slice(back, back + size.verts)
            sums = own_r[:, inside] + got_r[:, inside]
        a, b, c, scale = v0[:, here], v1[:, here], v2[:, here], diag[:, here]
        out[g, 0] = x[0] * a + x[1] * b + x[2] * c
        out[g, 1] = scale * (rho[0] * a + rho[1] * b + rho[2] * c) + rho[3] * sums


def total_over_dom(value, count):
    if count & (count - 1):
        return jnp.sum(lax.all_gather(value, "dom"), axis=0)
    step = 1
    while step < count:
        value = value + lax.ppermute(value, "dom", [(i, i ^ step) for i in range(count)])
        step *= 2
    return value


def on_device(heads, tails, signs, edge_weights, ground):
    group = lax.axis_size("grp")
    count = lax.axis_size("dom")
    size = Sizes(heads.shape[0], ground.shape[0], group)
    vmem = pl.BlockSpec(memory_space=pltpu.VMEM)
    smem = pl.BlockSpec(memory_space=pltpu.SMEM)
    params = pltpu.CompilerParams(vmem_limit_bytes=48 * 1024 * 1024)

    def flat(value):
        return value.astype(F32).reshape(-1, LANES)

    parts = [flat(heads), flat(tails), flat(signs[0]), flat(signs[1]), flat(edge_weights), flat(ground)]
    used = sum(part.shape[0] for part in parts)
    parts.append(jnp.zeros((size.payload - used, LANES), F32))
    pay = lax.all_gather(jnp.concatenate(parts, axis=0), "grp")

    half = jax.ShapeDtypeStruct((SUB, size.domain), F32)
    full = jax.ShapeDtypeStruct((SUB, size.extent), F32)

    def exchange(left, right):
        up = [(i, i + 1) for i in range(count - 1)]
        down = [(i + 1, i) for i in range(count - 1)]
        return lax.ppermute(right, "dom", up), lax.ppermute(left, "dom", down)

    me = lax.axis_index("grp")
    first_row = me * size.rows
    place = jnp.stack([first_row // HALF, first_row % HALF]).astype(jnp.int32)
    spread = (size.parts, LANES, LANES)
    keys, heads, tails, weights, bounds = pl.pallas_call(
        functools.partial(sort_kernel, size),
        out_shape=(
            jax.ShapeDtypeStruct(spread, jnp.int32),
            jax.ShapeDtypeStruct(spread, jnp.int32),
            jax.ShapeDtypeStruct(spread, jnp.int32),
            jax.ShapeDtypeStruct(spread, F32),
            jax.ShapeDtypeStruct((SUB, LANES), jnp.int32),
        ),
        in_specs=[smem, vmem],
        out_specs=(vmem,) * 5,
        scratch_shapes=[
            pltpu.VMEM((size.regs, SUB, LANES), jnp.int32),
            pltpu.VMEM((size.regs, SUB, LANES), F32),
        ],
        compiler_params=params,
        name="sort_edges",
    )(place, pay)
    edges = (bounds, heads, tails, weights)
    edge_specs = [smem, vmem, vmem, vmem]
    scratch = [
        pltpu.VMEM((size.padded(0), 16, LANES), F32),
        pltpu.VMEM((size.padded(1), 16, LANES), F32),
        pltpu.VMEM((LANES, 16, size.parts * LANES), BF),
        pltpu.VMEM((LANES, 16, size.parts * LANES), BF),
        pltpu.VMEM((size.padded(1) + size.most[0], SUB, LANES), F32),
    ]
    acc = pl.pallas_call(
        functools.partial(sketch_kernel, size),
        out_shape=(half, half),
        in_specs=edge_specs + [vmem] * 2,
        out_specs=(vmem, vmem),
        scratch_shapes=scratch,
        compiler_params=params,
        name="sketch",
    )(bounds, keys, heads, tails, weights, pay)
    got = exchange(*acc)
    *acc, v0, diag = pl.pallas_call(
        functools.partial(first_kernel, size),
        out_shape=(half, half, full, full),
        in_specs=edge_specs + [vmem] * 4,
        out_specs=(vmem,) * 4,
        scratch_shapes=scratch,
        compiler_params=params,
        name="operator_first",
    )(*edges, *acc, *got)
    got = exchange(*acc)
    *acc, v1 = pl.pallas_call(
        functools.partial(second_kernel, size),
        out_shape=(half, half, full),
        in_specs=edge_specs + [vmem] * 5,
        out_specs=(vmem,) * 3,
        scratch_shapes=scratch,
        compiler_params=params,
        name="operator_second",
    )(*edges, *acc, *got, diag)
    got = exchange(*acc)
    *acc, v2, moments = pl.pallas_call(
        functools.partial(third_kernel, size),
        out_shape=(half, half, full, jax.ShapeDtypeStruct((SUB, LANES), F32)),
        in_specs=edge_specs + [vmem] * 7,
        out_specs=(vmem,) * 4,
        scratch_shapes=scratch,
        compiler_params=params,
        name="operator_third",
    )(*edges, *acc, *got, diag, v0, v1)
    up = [(i, i + 1) for i in range(count - 1)]
    down = [(i + 1, i) for i in range(count - 1)]
    got_l = lax.ppermute(acc[1][:, size.reach :], "dom", up)
    got_r = lax.ppermute(acc[0][:, : size.reach], "dom", down)
    shared = total_over_dom(moments, count)
    out = pl.pallas_call(
        functools.partial(last_kernel, size),
        out_shape=jax.ShapeDtypeStruct((group, 2, SUB, size.verts), F32),
        in_specs=[vmem] * 9,
        out_specs=vmem,
        compiler_params=params,
        name="combine",
    )(shared, *acc, got_l, got_r, diag, v0, v1, v2)
    out = lax.all_to_all(out[:, :, : size.rows, :], "grp", 0, 0)
    return (out[:, 0].reshape(K, size.verts), out[:, 1].reshape(K, size.verts))


def solution(mesh):
    in_specs = (
        P(("dom", "grp")),
        P(("dom", "grp")),
        P(None, ("dom", "grp")),
        P(("dom", "grp")),
        P(("dom", "grp")),
    )
    out_specs = (P(None, ("dom", "grp")), P(None, ("dom", "grp")))
    return jax.shard_map(
        on_device, mesh=mesh, in_specs=in_specs, out_specs=out_specs, check_vma=False
    )
```

```python
import functools

import jax
import jax.numpy as jnp
from jax import lax
from jax.experimental import pallas as pl
from jax.experimental.pallas import tpu as pltpu
from jax.sharding import PartitionSpec as P

K = 24
HALF = 12
LANES = 128
SUB = 8
BF = jnp.bfloat16
F32 = jnp.float32


def row_of(block, r, count):
    return jnp.broadcast_to(block[r : r + 1, :], (count, LANES))


def bits_of(n):
    return (n - 1).bit_length()


class Sizes:
    def __init__(self, edev, verts, group):
        self.edev, self.verts, self.group = edev, verts, group
        self.domain = verts * group
        self.reach = self.domain // 2
        self.extent = self.domain + 2 * self.reach
        self.rows = K // group
        self.section = edev // LANES
        self.ground_rows = verts // LANES
        self.payload = -(-(5 * self.section + self.ground_rows) // SUB) * SUB
        self.regs = edev * group // (SUB * LANES)
        self.parts = self.regs * SUB // LANES
        self.strip = self.domain // 8
        self.blocks = (self.strip // LANES, self.extent // 16 // LANES + 1)
        self.most = (2 * self.blocks[0], self.blocks[1] + 1)

    def padded(self, which):
        return (self.domain, self.extent)[which] // LANES + self.most[which]

    def pack(self, heads, tails, signs):
        strip = heads // self.strip
        turned = jnp.where(strip % 2 == 1, self.extent - 1 - tails, tails)
        key = strip * self.extent + turned
        key = key * self.strip + heads % self.strip
        return (key << self.rows) | signs

    def unpack(self, key):
        key = jnp.right_shift(key, self.rows)
        low, key = key & (self.strip - 1), jnp.right_shift(key, bits_of(self.strip))
        turned, strip = key & (self.extent - 1), jnp.right_shift(key, bits_of(self.extent))
        tails = jnp.where(strip & 1 == 1, self.extent - 1 - turned, turned)
        return strip * self.strip + low, tails


def flip_mask(size, level):
    low = bits_of(size.regs)
    if level >= low + 10:
        return None
    if level < low + 3:
        place = lax.broadcasted_iota(jnp.int32, (SUB, LANES), 0)
        bit = level - low
    else:
        place = lax.broadcasted_iota(jnp.int32, (SUB, LANES), 1)
        bit = level - low - 3
    return -(jnp.right_shift(place, bit) & 1)


def partner(size, j):
    low = bits_of(size.regs)
    axis, bit = (0, j - low) if j < low + 3 else (1, j - low - 3)
    place = lax.broadcasted_iota(jnp.int32, (SUB, LANES), axis)
    lower = (jnp.right_shift(place, bit) & 1) == 0
    index = jnp.bitwise_xor(place, 1 << bit)
    return axis, index, lower


def sort_edges(size, keys, weights):
    low = bits_of(size.regs)
    levels = low + 10

    def between(group, stages):
        key = {v: keys[v] for v in group}
        weight = {v: weights[v] for v in group}
        for level, j in stages:
            for v in group:
                if v >> j & 1:
                    continue
                a, b = v, v | 1 << j
                if level < low and v >> level & 1:
                    a, b = b, a
                swap = key[a] > key[b]
                key[a], key[b] = jnp.where(swap, key[b], key[a]), jnp.where(swap, key[a], key[b])
                weight[a], weight[b] = (
                    jnp.where(swap, weight[b], weight[a]),
                    jnp.where(swap, weight[a], weight[b]),
                )
        for v in group:
            keys[v] = key[v]
            weights[v] = weight[v]

    def registers(level):
        top = min(level, low)
        if top > 3:
            for v in range(8):
                between(list(range(v, size.regs, 8)), [(level, j) for j in range(top - 1, 2, -1)])
        for v in range(0, size.regs, 8):
            between(list(range(v, v + 8)), [(level, j) for j in range(min(top, 3) - 1, -1, -1)])

    for v in range(0, size.regs, 8):
        between(list(range(v, v + 8)), [(level, j) for level in (1, 2, 3) for j in range(level - 1, -1, -1)])
    for level in range(4, low):
        registers(level)

    for level in range(low, levels + 1):
        before = flip_mask(size, level - 1) if level > low else None
        now = flip_mask(size, level)
        flip = now if before is None else before if now is None else jnp.bitwise_xor(before, now)
        stages = [partner(size, j) for j in range(level - 1, low - 1, -1)]

        def across(i, carry, flip=flip, stages=stages):
            group = [i * 8 + u for u in range(8)]
            key = [jnp.bitwise_xor(keys[v], flip) for v in group]
            weight = [weights[v] for v in group]
            for axis, index, lower in stages:
                for u in range(8):
                    k, w = key[u], weight[u]
                    other = jnp.take_along_axis(k, index, axis=axis, mode="promise_in_bounds")
                    other_w = jnp.take_along_axis(w, index, axis=axis, mode="promise_in_bounds")
                    best = jnp.where(lower, jnp.minimum(k, other), jnp.maximum(k, other))
                    weight[u] = jnp.where(best == k, w, other_w)
                    key[u] = best
            for u, v in enumerate(group):
                keys[v] = key[u]
                weights[v] = weight[u]
            return carry

        lax.fori_loop(0, size.regs // 8, across, 0)
        registers(level)


def sort_kernel(size, place, pay, key_out, heads_out, tails_out, weight_out, bounds, keys, weights):
    word, shift = place[0], place[1]
    per = size.section // SUB
    mask = (1 << size.rows) - 1

    def section(which, g, c):
        return pay[g, which * size.section + c * SUB : which * size.section + (c + 1) * SUB, :]

    for g in range(size.group):
        for c in range(per):
            heads = section(0, g, c).astype(jnp.int32)
            tails = section(1, g, c).astype(jnp.int32)
            signs = jnp.where(word == 0, section(2, g, c), section(3, g, c)).astype(jnp.int32)
            v = g * per + c
            keys[v] = size.pack(heads, tails, jnp.right_shift(signs, shift) & mask)
            weights[v] = section(4, g, c)
    sort_edges(size, keys, weights)
    ends = [size.unpack(keys[v]) for v in range(size.regs)]
    lane = lax.broadcasted_iota(jnp.int32, (1, LANES), 1)
    far = rare = lane < 0
    for which in range(2):
        least = functools.reduce(jnp.minimum, [end[which] for end in ends])
        most = functools.reduce(jnp.maximum, [end[which] for end in ends])
        least = jnp.min(least, axis=0, keepdims=True) // LANES
        most = jnp.max(most, axis=0, keepdims=True) // LANES
        bounds[2 * which : 2 * which + 1, :] = least
        bounds[2 * which + 1 : 2 * which + 2, :] = most
        far = far | (most - least >= size.blocks[which])
        rare = rare | (most - least >= size.most[which])
    runs = jnp.where(far, lane, LANES)
    count = jnp.sum(far.astype(F32), axis=1, keepdims=True)
    rare = jnp.max(jnp.where(rare, 1.0, 0.0), axis=1, keepdims=True)
    rare, count = rare.astype(jnp.int32), count.astype(jnp.int32)
    for step in (1, 2, 4, 8, 16, 32, 64):
        after = jnp.where(lane + step < LANES, jnp.roll(runs, -step, axis=1), LANES)
        runs = jnp.minimum(runs, after)
    bounds[4:5, :] = runs
    bounds[5:6, :] = jnp.broadcast_to(rare, (1, LANES))
    bounds[6:7, :] = jnp.broadcast_to(count, (1, LANES))
    for j in range(size.parts):
        here = range(j * 16, (j + 1) * 16)
        key = jnp.concatenate([keys[v] for v in here], axis=0).T
        key_out[j] = key
        heads_out[j], tails_out[j] = size.unpack(key)
        weight_out[j] = jnp.concatenate([weights[v] for v in here], axis=0).T


def halves_of(value):
    high = value.astype(BF).astype(F32)
    return jnp.concatenate([high, value - high], axis=0).astype(BF)


def row(ref, j, run, count):
    return jnp.broadcast_to(ref[j, pl.ds(run, 1), :], (count, LANES))


def next_far(bounds, run):
    following = bounds[4, jnp.minimum(run + 1, LANES - 1)]
    return jnp.where(run + 1 < LANES, following, LANES)


def window_add(size, index, run, first, begin, end, pair, acc, valid=True):
    iota = lax.broadcasted_iota(jnp.int32, (16, LANES), 0)
    rows = [(iota + 16 * m).astype(F32).astype(BF) for m in range(16)]
    zero, one = jnp.zeros((16, LANES), BF), jnp.ones((16, LANES), BF)
    start = (first + begin) * LANES
    if valid is not True:
        start = jnp.where(valid, start, -(1 << 20))
    window = (end - begin) * LANES
    hot = []
    for j in range(size.parts):
        column = []
        for at in range(0, window, 256):
            local = (row(index, j, run, 16) - (start + at)).astype(F32).astype(BF)
            count = min(256, window - at) // 16
            column += [jnp.where(local == rows[m], one, zero) for m in range(count)]
        hot.append(jnp.concatenate(column, axis=0))
    hot = jnp.concatenate(hot, axis=1)
    got = lax.dot_general(pair, hot, (((1,), (1,)), ((), ())), preferred_element_type=F32)
    for b in range(end - begin):
        acc[first + begin + b] += got[:, b * LANES : (b + 1) * LANES]


def sweep(size, bounds, ends, make, make_far, accs, bufs):
    def fill(buf, base):
        for q in range(SUB):
            for which, pair in enumerate(make(base + q)):
                buf[which, q] = pair

    def use(buf, base):
        for q in range(SUB):
            for which in range(2):
                first = bounds[2 * which, base + q]
                window_add(size, ends[which], base + q, first, 0, size.blocks[which], buf[which, q], accs[which])

    fill(bufs[0], 0)

    def step(i, carry):
        base = i * 2 * SUB
        use(bufs[0], base)
        fill(bufs[1], base + SUB)
        use(bufs[1], base + SUB)
        fill(bufs[0], (base + 2 * SUB) % LANES)
        return carry

    lax.fori_loop(0, LANES // (2 * SUB), step, 0)

    @pl.when(bounds[5, 0] == 0)
    def _():
        def four(i, run):
            for _ in range(4):
                valid, here = run < LANES, jnp.minimum(run, LANES - 1)
                full, beyond = make_far(here, False)
                for which in range(2):
                    first = bounds[2 * which, here]
                    near, most = size.blocks[which], size.most[which]
                    window_add(size, ends[which], here, first, near, most, full[which], accs[which], valid)
                    if beyond is not None:
                        window_add(size, ends[which], here, first, 0, near, beyond[which], accs[which], valid)
                run = jnp.where(valid, next_far(bounds, here), LANES)
            return run

        lax.fori_loop(0, (bounds[6, 0] + 3) // 4, four, bounds[4, 0])

    @pl.when(bounds[5, 0] != 0)
    def _():
        def more(run):
            full, beyond = make_far(run, True)
            for which in range(2):
                def one(a, carry, which=which):
                    window_add(size, ends[which], run, a, 0, 1, full[which], accs[which])
                    return carry

                first, last = bounds[2 * which, run], bounds[2 * which + 1, run]
                lax.fori_loop(first + size.blocks[which], last + 1, one, 0)
                if beyond is not None:
                    window_add(size, ends[which], run, first, 0, size.blocks[which], beyond[which], accs[which])
            return next_far(bounds, run)

        lax.while_loop(lambda run: run < LANES, more, bounds[4, 0])


def collect(size, acc_h, acc_t, out_l, out_r):
    shift = size.reach // LANES
    half = size.domain // LANES
    for a in range(size.extent // LANES):
        value = acc_t[a, 0:8] + acc_t[a, 8:16]
        h = a - shift
        if 0 <= h < half:
            value += acc_h[h, 0:8] + acc_h[h, 8:16]
        out, at = (out_l, a) if a < half else (out_r, a - half)
        out[:, at * LANES : (at + 1) * LANES] = value


def clear(acc_h, acc_t):
    acc_h[...] = jnp.zeros_like(acc_h)
    acc_t[...] = jnp.zeros_like(acc_t)


def sketch_kernel(size, bounds, keys, heads, tails, weights, pay, out_l, out_r, acc_h, acc_t, buf_a, buf_b, tables):
    sub = lax.broadcasted_iota(jnp.int32, (SUB, LANES), 0)
    is_sign = sub < size.rows
    clear(acc_h, acc_t)

    def make(run):
        pairs = [[], []]
        for j in range(size.parts):
            weight = row(weights, j, run, SUB)
            bit = jnp.right_shift(row(keys, j, run, SUB), sub) & 1
            signed = (2 * bit - 1).astype(F32) * jnp.sqrt(weight)
            last = jnp.where(sub == size.rows, weight, 0.0)
            pairs[0].append(halves_of(jnp.where(is_sign, signed, last)))
            pairs[1].append(halves_of(jnp.where(is_sign, -signed, last)))
        return [jnp.concatenate(pair, axis=1) for pair in pairs]

    sweep(size, bounds, (heads, tails), make, lambda run, every: (make(run), None), (acc_h, acc_t), (buf_a, buf_b))
    collect(size, acc_h, acc_t, out_l, out_r)
    for g in range(size.group):
        for r in range(size.ground_rows):
            at = size.reach + g * size.verts + r * LANES
            out, at = (out_l, at) if at < size.domain else (out_r, at - size.domain)
            line = 5 * size.section + r
            value = jnp.broadcast_to(pay[g, line : line + 1, :], (SUB, LANES))
            out[:, at : at + LANES] += jnp.where(sub == size.rows, value, 0.0)


def operator_core(size, bounds, heads, tails, weights, table, out_l, out_r, bufs):
    acc_h, acc_t, buf_a, buf_b, tables = bufs
    clear(acc_h, acc_t)
    for a in range(size.extent // LANES):
        tables[a] = table[:, a * LANES : (a + 1) * LANES]
    ends = (heads, tails)

    def take(which, low, high, a, out):
        shift = size.reach // LANES if which == 0 else 0
        got = jnp.take_along_axis(tables[shift + a], low, axis=1, mode="promise_in_bounds")
        return jnp.where(high == a, got, out)

    nothing = jnp.zeros((SUB, LANES), F32)

    def gathered(run, blocks):
        pairs = [[], []]
        for j in range(size.parts):
            weight = row(weights, j, run, SUB)
            for which in range(2):
                index = row(ends[which], j, run, SUB)
                first, (begin, end) = bounds[2 * which, run], blocks[which]
                low, high = index % LANES, index // LANES
                if end is None:
                    out = lax.fori_loop(
                        first + begin, bounds[2 * which + 1, run] + 1,
                        lambda a, out: take(which, low, high, a, out), nothing,
                    )
                else:
                    out = nothing
                    for a in range(begin, end):
                        out = take(which, low, high, first + a, out)
                pairs[1 - which].append(halves_of(out * weight))
        return [jnp.concatenate(pair, axis=1) for pair in pairs]

    def make(run):
        return gathered(run, [(0, size.blocks[which]) for which in range(2)])

    def make_far(run, every):
        ends_at = [None, None] if every else size.most
        return (
            gathered(run, [(0, ends_at[which]) for which in range(2)]),
            gathered(run, [(size.blocks[which], ends_at[which]) for which in range(2)]),
        )

    sweep(size, bounds, ends, make, make_far, (acc_h, acc_t), (buf_a, buf_b))
    collect(size, acc_h, acc_t, out_l, out_r)


def halves(size, own_l, own_r, got_l, got_r):
    return ((0, own_l, got_l), (size.domain, own_r, got_r))


def first_kernel(size, bounds, heads, tails, weights, own_l, own_r, got_l, got_r, out_l, out_r, v, diag, *bufs):
    sub = lax.broadcasted_iota(jnp.int32, (SUB, size.domain), 0)
    for at, own, got in halves(size, own_l, own_r, got_l, got_r):
        total = own[...] + got[...]
        spread = jnp.broadcast_to(total[size.rows : size.rows + 1, :], total.shape)
        safe = jnp.where(spread > 0.0, spread, 1.0)
        diag[:, at : at + size.domain] = safe
        v[:, at : at + size.domain] = jnp.where(sub < size.rows, total / safe, 0.0)
    operator_core(size, bounds, heads, tails, weights, v, out_l, out_r, bufs)


def next_v(size, own_l, own_r, got_l, got_r, diag, v):
    for at, own, got in halves(size, own_l, own_r, got_l, got_r):
        v[:, at : at + size.domain] = (own[...] + got[...]) / diag[:, at : at + size.domain]


def second_kernel(size, bounds, heads, tails, weights, own_l, own_r, got_l, got_r, diag, out_l, out_r, v, *bufs):
    next_v(size, own_l, own_r, got_l, got_r, diag, v)
    operator_core(size, bounds, heads, tails, weights, v, out_l, out_r, bufs)


def third_kernel(size, bounds, heads, tails, weights, own_l, own_r, got_l, got_r, diag, v0, v1, out_l, out_r, v2, moments, *bufs):
    next_v(size, own_l, own_r, got_l, got_r, diag, v2)
    operator_core(size, bounds, heads, tails, weights, v2, out_l, out_r, bufs)
    lane = lax.broadcasted_iota(jnp.int32, (SUB, LANES), 1)
    middle = slice(size.reach, size.reach + size.domain)
    weighted = diag[:, middle] * v0[:, middle]
    other = diag[:, middle] * v1[:, middle]
    sums = [
        weighted * v0[:, middle],
        weighted * v1[:, middle],
        other * v1[:, middle],
        other * v2[:, middle],
        diag[:, middle] * v2[:, middle] * v2[:, middle],
        v2[:, : size.domain] * out_l[...] + v2[:, size.domain :] * out_r[...],
    ]
    out = jnp.zeros((SUB, LANES), F32)
    for k, value in enumerate(sums):
        out = jnp.where(lane == k, jnp.sum(value, axis=1, keepdims=True), out)
    moments[...] = out


def coefficients(mu):
    zero = jnp.zeros_like(mu[0])

    def inner(a, b):
        total = None
        for i, x in enumerate(a):
            for j, y in enumerate(b):
                term = mu[i + j] if x is None and y is None else mu[i + j] * (y if x is None else x if y is None else x * y)
                total = term if total is None else total + term
        return total

    def image(a):
        a = [jnp.ones_like(zero) if x is None else x for x in a] + [zero]
        return [a[0]] + [a[i] - a[i - 1] for i in range(1, len(a))]

    def ratio(top, bottom):
        return jnp.where(bottom > 0.0, top / jnp.where(bottom > 0.0, bottom, 1.0), 0.0)

    rho, pi, x = [jnp.ones_like(zero)], [jnp.ones_like(zero)], []
    gamma = inner(rho, rho)
    for step in range(3):
        moved = image(pi)
        alpha = ratio(gamma, inner(pi, moved))
        x = [(x[i] if i < len(x) else zero) + alpha * pi[i] for i in range(len(pi))]
        rho = [(rho[i] if i < len(rho) else zero) - alpha * moved[i] for i in range(len(moved))]
        if step < 2:
            following = inner(rho, rho)
            beta = ratio(following, gamma)
            pi = [rho[i] + (beta * pi[i] if i < len(pi) else zero) for i in range(len(rho))]
            gamma = following
    return x, rho


def last_kernel(size, moments, own_l, own_r, got_l, got_r, diag, v0, v1, v2, out):
    total = moments[...]
    mu = [jnp.broadcast_to(total[:, k : k + 1], (SUB, LANES)) for k in range(6)]
    x, rho = coefficients(mu)
    x = [value[:, :1] for value in x]
    rho = [value[:, :1] for value in rho]
    for g in range(size.group):
        at = size.reach + g * size.verts
        here = slice(at, at + size.verts)
        if at < size.domain:
            sums = own_l[:, here] + got_l[:, g * size.verts : (g + 1) * size.verts]
        else:
            back = at - size.domain
            inside = slice(back, back + size.verts)
            sums = own_r[:, inside] + got_r[:, inside]
        a, b, c, scale = v0[:, here], v1[:, here], v2[:, here], diag[:, here]
        out[g, 0] = x[0] * a + x[1] * b + x[2] * c
        out[g, 1] = scale * (rho[0] * a + rho[1] * b + rho[2] * c) + rho[3] * sums


def total_over_dom(value, count):
    if count & (count - 1):
        return jnp.sum(lax.all_gather(value, "dom"), axis=0)
    step = 1
    while step < count:
        value = value + lax.ppermute(value, "dom", [(i, i ^ step) for i in range(count)])
        step *= 2
    return value


def on_device(heads, tails, signs, edge_weights, ground):
    group = lax.axis_size("grp")
    count = lax.axis_size("dom")
    size = Sizes(heads.shape[0], ground.shape[0], group)
    vmem = pl.BlockSpec(memory_space=pltpu.VMEM)
    smem = pl.BlockSpec(memory_space=pltpu.SMEM)
    params = pltpu.CompilerParams(vmem_limit_bytes=48 * 1024 * 1024)

    def flat(value):
        return value.astype(F32).reshape(-1, LANES)

    parts = [flat(heads), flat(tails), flat(signs[0]), flat(signs[1]), flat(edge_weights), flat(ground)]
    used = sum(part.shape[0] for part in parts)
    parts.append(jnp.zeros((size.payload - used, LANES), F32))
    pay = lax.all_gather(jnp.concatenate(parts, axis=0), "grp")

    half = jax.ShapeDtypeStruct((SUB, size.domain), F32)
    full = jax.ShapeDtypeStruct((SUB, size.extent), F32)

    def exchange(left, right):
        up = [(i, i + 1) for i in range(count - 1)]
        down = [(i + 1, i) for i in range(count - 1)]
        return lax.ppermute(right, "dom", up), lax.ppermute(left, "dom", down)

    me = lax.axis_index("grp")
    first_row = me * size.rows
    place = jnp.stack([first_row // HALF, first_row % HALF]).astype(jnp.int32)
    spread = (size.parts, LANES, LANES)
    keys, heads, tails, weights, bounds = pl.pallas_call(
        functools.partial(sort_kernel, size),
        out_shape=(
            jax.ShapeDtypeStruct(spread, jnp.int32),
            jax.ShapeDtypeStruct(spread, jnp.int32),
            jax.ShapeDtypeStruct(spread, jnp.int32),
            jax.ShapeDtypeStruct(spread, F32),
            jax.ShapeDtypeStruct((SUB, LANES), jnp.int32),
        ),
        in_specs=[smem, vmem],
        out_specs=(vmem,) * 5,
        scratch_shapes=[
            pltpu.VMEM((size.regs, SUB, LANES), jnp.int32),
            pltpu.VMEM((size.regs, SUB, LANES), F32),
        ],
        compiler_params=params,
        name="sort_edges",
    )(place, pay)
    edges = (bounds, heads, tails, weights)
    edge_specs = [smem, vmem, vmem, vmem]
    scratch = [
        pltpu.VMEM((size.padded(0), 16, LANES), F32),
        pltpu.VMEM((size.padded(1), 16, LANES), F32),
        pltpu.VMEM((2, SUB, 16, size.parts * LANES), BF),
        pltpu.VMEM((2, SUB, 16, size.parts * LANES), BF),
        pltpu.VMEM((size.padded(1) + size.most[0], SUB, LANES), F32),
    ]
    acc = pl.pallas_call(
        functools.partial(sketch_kernel, size),
        out_shape=(half, half),
        in_specs=edge_specs + [vmem] * 2,
        out_specs=(vmem, vmem),
        scratch_shapes=scratch,
        compiler_params=params,
        name="sketch",
    )(bounds, keys, heads, tails, weights, pay)
    got = exchange(*acc)
    *acc, v0, diag = pl.pallas_call(
        functools.partial(first_kernel, size),
        out_shape=(half, half, full, full),
        in_specs=edge_specs + [vmem] * 4,
        out_specs=(vmem,) * 4,
        scratch_shapes=scratch,
        compiler_params=params,
        name="operator_first",
    )(*edges, *acc, *got)
    got = exchange(*acc)
    *acc, v1 = pl.pallas_call(
        functools.partial(second_kernel, size),
        out_shape=(half, half, full),
        in_specs=edge_specs + [vmem] * 5,
        out_specs=(vmem,) * 3,
        scratch_shapes=scratch,
        compiler_params=params,
        name="operator_second",
    )(*edges, *acc, *got, diag)
    got = exchange(*acc)
    *acc, v2, moments = pl.pallas_call(
        functools.partial(third_kernel, size),
        out_shape=(half, half, full, jax.ShapeDtypeStruct((SUB, LANES), F32)),
        in_specs=edge_specs + [vmem] * 7,
        out_specs=(vmem,) * 4,
        scratch_shapes=scratch,
        compiler_params=params,
        name="operator_third",
    )(*edges, *acc, *got, diag, v0, v1)
    up = [(i, i + 1) for i in range(count - 1)]
    down = [(i + 1, i) for i in range(count - 1)]
    got_l = lax.ppermute(acc[1][:, size.reach :], "dom", up)
    got_r = lax.ppermute(acc[0][:, : size.reach], "dom", down)
    shared = total_over_dom(moments, count)
    out = pl.pallas_call(
        functools.partial(last_kernel, size),
        out_shape=jax.ShapeDtypeStruct((group, 2, SUB, size.verts), F32),
        in_specs=[vmem] * 9,
        out_specs=vmem,
        compiler_params=params,
        name="combine",
    )(shared, *acc, got_l, got_r, diag, v0, v1, v2)
    out = lax.all_to_all(out[:, :, : size.rows, :], "grp", 0, 0)
    return (out[:, 0].reshape(K, size.verts), out[:, 1].reshape(K, size.verts))


def solution(mesh):
    in_specs = (
        P(("dom", "grp")),
        P(("dom", "grp")),
        P(None, ("dom", "grp")),
        P(("dom", "grp")),
        P(("dom", "grp")),
    )
    out_specs = (P(None, ("dom", "grp")), P(None, ("dom", "grp")))
    return jax.shard_map(
        on_device, mesh=mesh, in_specs=in_specs, out_specs=out_specs, check_vma=False
    )
```

```python
import functools

import jax
import jax.numpy as jnp
from jax import lax
from jax.experimental import pallas as pl
from jax.experimental.pallas import tpu as pltpu
from jax.sharding import PartitionSpec as P

K = 24
HALF = 12
LANES = 128
SUB = 8
BF = jnp.bfloat16
F32 = jnp.float32


def row_of(block, r, count):
    return jnp.broadcast_to(block[r : r + 1, :], (count, LANES))


def bits_of(n):
    return (n - 1).bit_length()


class Sizes:
    def __init__(self, edev, verts, group):
        self.edev, self.verts, self.group = edev, verts, group
        self.domain = verts * group
        self.reach = self.domain // 2
        self.extent = self.domain + 2 * self.reach
        self.rows = K // group
        self.section = edev // LANES
        self.ground_rows = verts // LANES
        self.payload = -(-(5 * self.section + self.ground_rows) // SUB) * SUB
        self.regs = edev * group // (SUB * LANES)
        self.parts = self.regs * SUB // LANES
        self.strip = self.domain // 8
        self.blocks = (self.strip // LANES, self.extent // 16 // LANES + 2)
        self.most = (2 * self.blocks[0], self.blocks[1])
        self.window = self.extent // 16 + 64

    def padded(self, which):
        return (self.domain, self.extent)[which] // LANES + self.most[which]

    def pack(self, heads, tails, signs):
        strip = heads // self.strip
        turned = jnp.where(strip % 2 == 1, self.extent - 1 - tails, tails)
        key = strip * self.extent + turned
        key = key * self.strip + heads % self.strip
        return (key << self.rows) | signs

    def unpack(self, key):
        key = jnp.right_shift(key, self.rows)
        low, key = key & (self.strip - 1), jnp.right_shift(key, bits_of(self.strip))
        turned, strip = key & (self.extent - 1), jnp.right_shift(key, bits_of(self.extent))
        tails = jnp.where(strip & 1 == 1, self.extent - 1 - turned, turned)
        return strip * self.strip + low, tails


def flip_mask(size, level):
    low = bits_of(size.regs)
    if level >= low + 10:
        return None
    if level < low + 3:
        place = lax.broadcasted_iota(jnp.int32, (SUB, LANES), 0)
        bit = level - low
    else:
        place = lax.broadcasted_iota(jnp.int32, (SUB, LANES), 1)
        bit = level - low - 3
    return -(jnp.right_shift(place, bit) & 1)


def partner(size, j):
    low = bits_of(size.regs)
    axis, bit = (0, j - low) if j < low + 3 else (1, j - low - 3)
    place = lax.broadcasted_iota(jnp.int32, (SUB, LANES), axis)
    lower = (jnp.right_shift(place, bit) & 1) == 0
    index = jnp.bitwise_xor(place, 1 << bit)
    return axis, index, lower


def sort_edges(size, keys, weights):
    low = bits_of(size.regs)
    levels = low + 10

    def between(group, stages):
        key = {v: keys[v] for v in group}
        weight = {v: weights[v] for v in group}
        for level, j in stages:
            for v in group:
                if v >> j & 1:
                    continue
                a, b = v, v | 1 << j
                if level < low and v >> level & 1:
                    a, b = b, a
                swap = key[a] > key[b]
                key[a], key[b] = jnp.where(swap, key[b], key[a]), jnp.where(swap, key[a], key[b])
                weight[a], weight[b] = (
                    jnp.where(swap, weight[b], weight[a]),
                    jnp.where(swap, weight[a], weight[b]),
                )
        for v in group:
            keys[v] = key[v]
            weights[v] = weight[v]

    def registers(level):
        top = min(level, low)
        if top > 3:
            for v in range(8):
                between(list(range(v, size.regs, 8)), [(level, j) for j in range(top - 1, 2, -1)])
        for v in range(0, size.regs, 8):
            between(list(range(v, v + 8)), [(level, j) for j in range(min(top, 3) - 1, -1, -1)])

    for v in range(0, size.regs, 8):
        between(list(range(v, v + 8)), [(level, j) for level in (1, 2, 3) for j in range(level - 1, -1, -1)])
    for level in range(4, low):
        registers(level)

    for level in range(low, levels + 1):
        before = flip_mask(size, level - 1) if level > low else None
        now = flip_mask(size, level)
        flip = now if before is None else before if now is None else jnp.bitwise_xor(before, now)
        stages = [partner(size, j) for j in range(level - 1, low - 1, -1)]

        def across(i, carry, flip=flip, stages=stages):
            group = [i * 8 + u for u in range(8)]
            key = [jnp.bitwise_xor(keys[v], flip) for v in group]
            weight = [weights[v] for v in group]
            for axis, index, lower in stages:
                for u in range(8):
                    k, w = key[u], weight[u]
                    other = jnp.take_along_axis(k, index, axis=axis, mode="promise_in_bounds")
                    other_w = jnp.take_along_axis(w, index, axis=axis, mode="promise_in_bounds")
                    best = jnp.where(lower, jnp.minimum(k, other), jnp.maximum(k, other))
                    weight[u] = jnp.where(best == k, w, other_w)
                    key[u] = best
            for u, v in enumerate(group):
                keys[v] = key[u]
                weights[v] = weight[u]
            return carry

        lax.fori_loop(0, size.regs // 8, across, 0)
        registers(level)


def sort_kernel(size, place, pay, key_out, heads_out, tails_out, weight_out, bounds, keys, weights):
    word, shift = place[0], place[1]
    per = size.section // SUB
    mask = (1 << size.rows) - 1

    def section(which, g, c):
        return pay[g, which * size.section + c * SUB : which * size.section + (c + 1) * SUB, :]

    for g in range(size.group):
        for c in range(per):
            heads = section(0, g, c).astype(jnp.int32)
            tails = section(1, g, c).astype(jnp.int32)
            signs = jnp.where(word == 0, section(2, g, c), section(3, g, c)).astype(jnp.int32)
            v = g * per + c
            keys[v] = size.pack(heads, tails, jnp.right_shift(signs, shift) & mask)
            weights[v] = section(4, g, c)
    sort_edges(size, keys, weights)
    ends = [size.unpack(keys[v]) for v in range(size.regs)]
    lane = lax.broadcasted_iota(jnp.int32, (1, LANES), 1)
    far = rare = lane < 0
    for which in range(2):
        least = functools.reduce(jnp.minimum, [end[which] for end in ends])
        most = functools.reduce(jnp.maximum, [end[which] for end in ends])
        least = jnp.min(least, axis=0, keepdims=True)
        most = jnp.max(most, axis=0, keepdims=True)
        bounds[2 * which : 2 * which + 1, :] = least
        bounds[2 * which + 1 : 2 * which + 2, :] = most
        if which == 1:
            far = far | (most - (least & -8) >= size.window)
            rare = rare | (most - (least & -8) >= size.window)
        least, most = least // LANES, most // LANES
        far = far | (most - least >= size.blocks[which])
        rare = rare | (most - least >= size.most[which])
    runs = jnp.where(far, lane, LANES)
    count = jnp.sum(far.astype(F32), axis=1, keepdims=True)
    rare = jnp.max(jnp.where(rare, 1.0, 0.0), axis=1, keepdims=True)
    rare, count = rare.astype(jnp.int32), count.astype(jnp.int32)
    for step in (1, 2, 4, 8, 16, 32, 64):
        after = jnp.where(lane + step < LANES, jnp.roll(runs, -step, axis=1), LANES)
        runs = jnp.minimum(runs, after)
    bounds[4:5, :] = runs
    bounds[5:6, :] = jnp.broadcast_to(rare, (1, LANES))
    bounds[6:7, :] = jnp.broadcast_to(count, (1, LANES))
    for j in range(size.parts):
        here = range(j * 16, (j + 1) * 16)
        key = jnp.concatenate([keys[v] for v in here], axis=0).T
        key_out[j] = key
        heads_out[j], tails_out[j] = size.unpack(key)
        weight_out[j] = jnp.concatenate([weights[v] for v in here], axis=0).T


def halves_of(value):
    high = value.astype(BF).astype(F32)
    return jnp.concatenate([high, value - high], axis=0).astype(BF)


def row(ref, j, run, count):
    return jnp.broadcast_to(ref[j, pl.ds(run, 1), :], (count, LANES))


def next_far(bounds, run):
    following = bounds[4, jnp.minimum(run + 1, LANES - 1)]
    return jnp.where(run + 1 < LANES, following, LANES)


def one_hot(size, index, run, start, window):
    iota = lax.broadcasted_iota(jnp.int32, (16, LANES), 0)
    rows = [(iota + 16 * m).astype(F32).astype(BF) for m in range(16)]
    zero, one = jnp.zeros((16, LANES), BF), jnp.ones((16, LANES), BF)
    hot = []
    for j in range(size.parts):
        column = []
        for at in range(0, window, 256):
            local = (row(index, j, run, 16) - (start + at)).astype(F32).astype(BF)
            count = min(256, window - at) // 16
            column += [jnp.where(local == rows[m], one, zero) for m in range(count)]
        hot.append(jnp.concatenate(column, axis=0))
    return jnp.concatenate(hot, axis=1)


def times(left, right):
    return lax.dot_general(left, right, (((1,), (1,)), ((), ())), preferred_element_type=F32)


def add_blocks(size, heads, run, first, begin, end, pair, acc, valid=True):
    start = (first + begin) * LANES
    if valid is not True:
        start = jnp.where(valid, start, -(1 << 20))
    got = times(pair, one_hot(size, heads, run, start, (end - begin) * LANES))
    for b in range(end - begin):
        acc[first + begin + b] += got[:, b * LANES : (b + 1) * LANES]


def add_rows(size, tails, run, start, pair, acc, valid=True):
    start = pl.multiple_of(start, SUB)
    from_ = start if valid is True else jnp.where(valid, start, -(1 << 20))
    acc[pl.ds(start, size.window), 0:16] += times(one_hot(size, tails, run, from_, size.window), pair)


def first_block(bounds, which, run):
    return bounds[2 * which, run] // LANES


def last_block(bounds, which, run):
    return bounds[2 * which + 1, run] // LANES


def first_row(bounds, run):
    return bounds[2, run] & -8


def sweep(size, bounds, ends, make, make_far, accs, bufs):
    def fill(buf, base):
        for q in range(SUB):
            for which, pair in enumerate(make(base + q)):
                buf[which, q] = pair

    heads, tails = ends
    acc_h, acc_t = accs

    def use(buf, base):
        for q in range(SUB):
            run = base + q
            add_blocks(size, heads, run, first_block(bounds, 0, run), 0, size.blocks[0], buf[0, q], acc_h)
            add_rows(size, tails, run, first_row(bounds, run), buf[1, q], acc_t)

    fill(bufs[0], 0)

    def step(i, carry):
        base = i * 2 * SUB
        use(bufs[0], base)
        fill(bufs[1], base + SUB)
        use(bufs[1], base + SUB)
        fill(bufs[0], (base + 2 * SUB) % LANES)
        return carry

    lax.fori_loop(0, LANES // (2 * SUB), step, 0)

    @pl.when(bounds[5, 0] == 0)
    def _():
        def four(i, run):
            for _ in range(4):
                valid, here = run < LANES, jnp.minimum(run, LANES - 1)
                full, beyond = make_far(here, False)
                first = first_block(bounds, 0, here)
                add_blocks(size, heads, here, first, size.blocks[0], size.most[0], full[0], acc_h, valid)
                if beyond is not None:
                    add_rows(size, tails, here, first_row(bounds, here), beyond[1], acc_t, valid)
                run = jnp.where(valid, next_far(bounds, here), LANES)
            return run

        lax.fori_loop(0, (bounds[6, 0] + 3) // 4, four, bounds[4, 0])

    @pl.when(bounds[5, 0] != 0)
    def _():
        def more(run):
            full, beyond = make_far(run, True)
            first, start = first_block(bounds, 0, run), first_row(bounds, run)

            def block(a, carry):
                add_blocks(size, heads, run, a, 0, 1, full[0], acc_h)
                return carry

            def window(m, carry):
                add_rows(size, tails, run, start + m * size.window, full[1], acc_t)
                return carry

            lax.fori_loop(first + size.blocks[0], last_block(bounds, 0, run) + 1, block, 0)
            lax.fori_loop(1, (bounds[3, run] - start) // size.window + 1, window, 0)
            if beyond is not None:
                add_blocks(size, heads, run, first, 0, size.blocks[0], beyond[0], acc_h)
                add_rows(size, tails, run, start, beyond[1], acc_t)
            return next_far(bounds, run)

        lax.while_loop(lambda run: run < LANES, more, bounds[4, 0])


def collect(size, acc_h, acc_t, out_l, out_r):
    shift = size.reach // LANES
    half = size.domain // LANES
    for a in range(size.extent // LANES):
        value = acc_t[a * LANES : (a + 1) * LANES, :].T
        value = value[0:8, :] + value[8:16, :]
        h = a - shift
        if 0 <= h < half:
            value += acc_h[h, 0:8] + acc_h[h, 8:16]
        out, at = (out_l, a) if a < half else (out_r, a - half)
        out[:, at * LANES : (at + 1) * LANES] = value


def clear(acc_h, acc_t):
    acc_h[...] = jnp.zeros_like(acc_h)
    acc_t[...] = jnp.zeros_like(acc_t)


def sketch_kernel(size, bounds, keys, heads, tails, weights, pay, out_l, out_r, acc_h, acc_t, buf_a, buf_b, tables):
    sub = lax.broadcasted_iota(jnp.int32, (SUB, LANES), 0)
    is_sign = sub < size.rows
    clear(acc_h, acc_t)

    def make(run):
        pairs = [[], []]
        for j in range(size.parts):
            weight = row(weights, j, run, SUB)
            bit = jnp.right_shift(row(keys, j, run, SUB), sub) & 1
            signed = (2 * bit - 1).astype(F32) * jnp.sqrt(weight)
            last = jnp.where(sub == size.rows, weight, 0.0)
            pairs[0].append(halves_of(jnp.where(is_sign, signed, last)))
            pairs[1].append(halves_of(jnp.where(is_sign, -signed, last)))
        return [jnp.concatenate(pair, axis=1) for pair in pairs]

    sweep(size, bounds, (heads, tails), make, lambda run, every: (make(run), None), (acc_h, acc_t), (buf_a, buf_b))
    collect(size, acc_h, acc_t, out_l, out_r)
    for g in range(size.group):
        for r in range(size.ground_rows):
            at = size.reach + g * size.verts + r * LANES
            out, at = (out_l, at) if at < size.domain else (out_r, at - size.domain)
            line = 5 * size.section + r
            value = jnp.broadcast_to(pay[g, line : line + 1, :], (SUB, LANES))
            out[:, at : at + LANES] += jnp.where(sub == size.rows, value, 0.0)


def operator_core(size, bounds, heads, tails, weights, table, out_l, out_r, bufs):
    acc_h, acc_t, buf_a, buf_b, tables = bufs
    clear(acc_h, acc_t)
    for a in range(size.extent // LANES):
        tables[a] = table[:, a * LANES : (a + 1) * LANES]
    ends = (heads, tails)

    def take(which, low, high, a, out):
        shift = size.reach // LANES if which == 0 else 0
        got = jnp.take_along_axis(tables[shift + a], low, axis=1, mode="promise_in_bounds")
        return jnp.where(high == a, got, out)

    nothing = jnp.zeros((SUB, LANES), F32)

    def gathered(run, blocks):
        pairs = [[], []]
        for j in range(size.parts):
            weight = row(weights, j, run, SUB)
            for which in range(2):
                index = row(ends[which], j, run, SUB)
                first, (begin, end) = first_block(bounds, which, run), blocks[which]
                low, high = index % LANES, index // LANES
                if end is None:
                    out = lax.fori_loop(
                        first + begin, last_block(bounds, which, run) + 1,
                        lambda a, out: take(which, low, high, a, out), nothing,
                    )
                else:
                    out = nothing
                    for a in range(begin, end):
                        out = take(which, low, high, first + a, out)
                pairs[1 - which].append(halves_of(out * weight))
        return [jnp.concatenate(pair, axis=1) for pair in pairs]

    def make(run):
        return gathered(run, [(0, size.blocks[which]) for which in range(2)])

    def make_far(run, every):
        ends_at = [None, None] if every else size.most
        return (
            gathered(run, [(0, ends_at[which]) for which in range(2)]),
            gathered(run, [(size.blocks[which], ends_at[which]) for which in range(2)]),
        )

    sweep(size, bounds, ends, make, make_far, (acc_h, acc_t), (buf_a, buf_b))
    collect(size, acc_h, acc_t, out_l, out_r)


def halves(size, own_l, own_r, got_l, got_r):
    return ((0, own_l, got_l), (size.domain, own_r, got_r))


def first_kernel(size, bounds, heads, tails, weights, own_l, own_r, got_l, got_r, out_l, out_r, v, diag, *bufs):
    sub = lax.broadcasted_iota(jnp.int32, (SUB, size.domain), 0)
    for at, own, got in halves(size, own_l, own_r, got_l, got_r):
        total = own[...] + got[...]
        spread = jnp.broadcast_to(total[size.rows : size.rows + 1, :], total.shape)
        safe = jnp.where(spread > 0.0, spread, 1.0)
        diag[:, at : at + size.domain] = safe
        v[:, at : at + size.domain] = jnp.where(sub < size.rows, total / safe, 0.0)
    operator_core(size, bounds, heads, tails, weights, v, out_l, out_r, bufs)


def next_v(size, own_l, own_r, got_l, got_r, diag, v):
    for at, own, got in halves(size, own_l, own_r, got_l, got_r):
        v[:, at : at + size.domain] = (own[...] + got[...]) / diag[:, at : at + size.domain]


def second_kernel(size, bounds, heads, tails, weights, own_l, own_r, got_l, got_r, diag, out_l, out_r, v, *bufs):
    next_v(size, own_l, own_r, got_l, got_r, diag, v)
    operator_core(size, bounds, heads, tails, weights, v, out_l, out_r, bufs)


def third_kernel(size, bounds, heads, tails, weights, own_l, own_r, got_l, got_r, diag, v0, v1, out_l, out_r, v2, moments, *bufs):
    next_v(size, own_l, own_r, got_l, got_r, diag, v2)
    operator_core(size, bounds, heads, tails, weights, v2, out_l, out_r, bufs)
    lane = lax.broadcasted_iota(jnp.int32, (SUB, LANES), 1)
    middle = slice(size.reach, size.reach + size.domain)
    weighted = diag[:, middle] * v0[:, middle]
    other = diag[:, middle] * v1[:, middle]
    sums = [
        weighted * v0[:, middle],
        weighted * v1[:, middle],
        other * v1[:, middle],
        other * v2[:, middle],
        diag[:, middle] * v2[:, middle] * v2[:, middle],
        v2[:, : size.domain] * out_l[...] + v2[:, size.domain :] * out_r[...],
    ]
    out = jnp.zeros((SUB, LANES), F32)
    for k, value in enumerate(sums):
        out = jnp.where(lane == k, jnp.sum(value, axis=1, keepdims=True), out)
    moments[...] = out


def coefficients(mu):
    zero = jnp.zeros_like(mu[0])

    def inner(a, b):
        total = None
        for i, x in enumerate(a):
            for j, y in enumerate(b):
                term = mu[i + j] if x is None and y is None else mu[i + j] * (y if x is None else x if y is None else x * y)
                total = term if total is None else total + term
        return total

    def image(a):
        a = [jnp.ones_like(zero) if x is None else x for x in a] + [zero]
        return [a[0]] + [a[i] - a[i - 1] for i in range(1, len(a))]

    def ratio(top, bottom):
        return jnp.where(bottom > 0.0, top / jnp.where(bottom > 0.0, bottom, 1.0), 0.0)

    rho, pi, x = [jnp.ones_like(zero)], [jnp.ones_like(zero)], []
    gamma = inner(rho, rho)
    for step in range(3):
        moved = image(pi)
        alpha = ratio(gamma, inner(pi, moved))
        x = [(x[i] if i < len(x) else zero) + alpha * pi[i] for i in range(len(pi))]
        rho = [(rho[i] if i < len(rho) else zero) - alpha * moved[i] for i in range(len(moved))]
        if step < 2:
            following = inner(rho, rho)
            beta = ratio(following, gamma)
            pi = [rho[i] + (beta * pi[i] if i < len(pi) else zero) for i in range(len(rho))]
            gamma = following
    return x, rho


def last_kernel(size, moments, own_l, own_r, got_l, got_r, diag, v0, v1, v2, out):
    total = moments[...]
    mu = [jnp.broadcast_to(total[:, k : k + 1], (SUB, LANES)) for k in range(6)]
    x, rho = coefficients(mu)
    x = [value[:, :1] for value in x]
    rho = [value[:, :1] for value in rho]
    for g in range(size.group):
        at = size.reach + g * size.verts
        here = slice(at, at + size.verts)
        if at < size.domain:
            sums = own_l[:, here] + got_l[:, g * size.verts : (g + 1) * size.verts]
        else:
            back = at - size.domain
            inside = slice(back, back + size.verts)
            sums = own_r[:, inside] + got_r[:, inside]
        a, b, c, scale = v0[:, here], v1[:, here], v2[:, here], diag[:, here]
        out[g, 0] = x[0] * a + x[1] * b + x[2] * c
        out[g, 1] = scale * (rho[0] * a + rho[1] * b + rho[2] * c) + rho[3] * sums


def total_over_dom(value, count):
    if count & (count - 1):
        return jnp.sum(lax.all_gather(value, "dom"), axis=0)
    step = 1
    while step < count:
        value = value + lax.ppermute(value, "dom", [(i, i ^ step) for i in range(count)])
        step *= 2
    return value


def on_device(heads, tails, signs, edge_weights, ground):
    group = lax.axis_size("grp")
    count = lax.axis_size("dom")
    size = Sizes(heads.shape[0], ground.shape[0], group)
    vmem = pl.BlockSpec(memory_space=pltpu.VMEM)
    smem = pl.BlockSpec(memory_space=pltpu.SMEM)
    params = pltpu.CompilerParams(vmem_limit_bytes=48 * 1024 * 1024)

    def flat(value):
        return value.astype(F32).reshape(-1, LANES)

    parts = [flat(heads), flat(tails), flat(signs[0]), flat(signs[1]), flat(edge_weights), flat(ground)]
    used = sum(part.shape[0] for part in parts)
    parts.append(jnp.zeros((size.payload - used, LANES), F32))
    pay = lax.all_gather(jnp.concatenate(parts, axis=0), "grp")

    half = jax.ShapeDtypeStruct((SUB, size.domain), F32)
    full = jax.ShapeDtypeStruct((SUB, size.extent), F32)

    def exchange(left, right):
        up = [(i, i + 1) for i in range(count - 1)]
        down = [(i + 1, i) for i in range(count - 1)]
        return lax.ppermute(right, "dom", up), lax.ppermute(left, "dom", down)

    me = lax.axis_index("grp")
    first_row = me * size.rows
    place = jnp.stack([first_row // HALF, first_row % HALF]).astype(jnp.int32)
    spread = (size.parts, LANES, LANES)
    keys, heads, tails, weights, bounds = pl.pallas_call(
        functools.partial(sort_kernel, size),
        out_shape=(
            jax.ShapeDtypeStruct(spread, jnp.int32),
            jax.ShapeDtypeStruct(spread, jnp.int32),
            jax.ShapeDtypeStruct(spread, jnp.int32),
            jax.ShapeDtypeStruct(spread, F32),
            jax.ShapeDtypeStruct((SUB, LANES), jnp.int32),
        ),
        in_specs=[smem, vmem],
        out_specs=(vmem,) * 5,
        scratch_shapes=[
            pltpu.VMEM((size.regs, SUB, LANES), jnp.int32),
            pltpu.VMEM((size.regs, SUB, LANES), F32),
        ],
        compiler_params=params,
        name="sort_edges",
    )(place, pay)
    edges = (bounds, heads, tails, weights)
    edge_specs = [smem, vmem, vmem, vmem]
    scratch = [
        pltpu.VMEM((size.padded(0), 16, LANES), F32),
        pltpu.VMEM((size.extent + size.window, LANES), F32),
        pltpu.VMEM((2, SUB, 16, size.parts * LANES), BF),
        pltpu.VMEM((2, SUB, 16, size.parts * LANES), BF),
        pltpu.VMEM((size.padded(1) + size.most[0], SUB, LANES), F32),
    ]
    acc = pl.pallas_call(
        functools.partial(sketch_kernel, size),
        out_shape=(half, half),
        in_specs=edge_specs + [vmem] * 2,
        out_specs=(vmem, vmem),
        scratch_shapes=scratch,
        compiler_params=params,
        name="sketch",
    )(bounds, keys, heads, tails, weights, pay)
    got = exchange(*acc)
    *acc, v0, diag = pl.pallas_call(
        functools.partial(first_kernel, size),
        out_shape=(half, half, full, full),
        in_specs=edge_specs + [vmem] * 4,
        out_specs=(vmem,) * 4,
        scratch_shapes=scratch,
        compiler_params=params,
        name="operator_first",
    )(*edges, *acc, *got)
    got = exchange(*acc)
    *acc, v1 = pl.pallas_call(
        functools.partial(second_kernel, size),
        out_shape=(half, half, full),
        in_specs=edge_specs + [vmem] * 5,
        out_specs=(vmem,) * 3,
        scratch_shapes=scratch,
        compiler_params=params,
        name="operator_second",
    )(*edges, *acc, *got, diag)
    got = exchange(*acc)
    *acc, v2, moments = pl.pallas_call(
        functools.partial(third_kernel, size),
        out_shape=(half, half, full, jax.ShapeDtypeStruct((SUB, LANES), F32)),
        in_specs=edge_specs + [vmem] * 7,
        out_specs=(vmem,) * 4,
        scratch_shapes=scratch,
        compiler_params=params,
        name="operator_third",
    )(*edges, *acc, *got, diag, v0, v1)
    up = [(i, i + 1) for i in range(count - 1)]
    down = [(i + 1, i) for i in range(count - 1)]
    got_l = lax.ppermute(acc[1][:, size.reach :], "dom", up)
    got_r = lax.ppermute(acc[0][:, : size.reach], "dom", down)
    shared = total_over_dom(moments, count)
    out = pl.pallas_call(
        functools.partial(last_kernel, size),
        out_shape=jax.ShapeDtypeStruct((group, 2, SUB, size.verts), F32),
        in_specs=[vmem] * 9,
        out_specs=vmem,
        compiler_params=params,
        name="combine",
    )(shared, *acc, got_l, got_r, diag, v0, v1, v2)
    out = lax.all_to_all(out[:, :, : size.rows, :], "grp", 0, 0)
    return (out[:, 0].reshape(K, size.verts), out[:, 1].reshape(K, size.verts))


def solution(mesh):
    in_specs = (
        P(("dom", "grp")),
        P(("dom", "grp")),
        P(None, ("dom", "grp")),
        P(("dom", "grp")),
        P(("dom", "grp")),
    )
    out_specs = (P(None, ("dom", "grp")), P(None, ("dom", "grp")))
    return jax.shard_map(
        on_device, mesh=mesh, in_specs=in_specs, out_specs=out_specs, check_vma=False
    )
```

```python
import functools

import jax
import jax.numpy as jnp
from jax import lax
from jax.experimental import pallas as pl
from jax.experimental.pallas import tpu as pltpu
from jax.sharding import PartitionSpec as P

K = 24
HALF = 12
LANES = 128
SUB = 8
BF = jnp.bfloat16
F32 = jnp.float32


def row_of(block, r, count):
    return jnp.broadcast_to(block[r : r + 1, :], (count, LANES))


def bits_of(n):
    return (n - 1).bit_length()


class Sizes:
    def __init__(self, edev, verts, group):
        self.edev, self.verts, self.group = edev, verts, group
        self.domain = verts * group
        self.reach = self.domain // 2
        self.extent = self.domain + 2 * self.reach
        self.rows = K // group
        self.section = edev // LANES
        self.ground_rows = verts // LANES
        self.payload = -(-(5 * self.section + self.ground_rows) // SUB) * SUB
        self.regs = edev * group // (SUB * LANES)
        self.parts = self.regs * SUB // LANES
        self.strip = self.domain // 8
        self.blocks = (self.strip // LANES, self.extent // 16 // LANES + 2)
        self.most = (2 * self.blocks[0], self.blocks[1])
        self.window = self.extent // 16 + 64
        self.further = self.extent // 64

    def padded(self, which):
        return (self.domain, self.extent)[which] // LANES + self.most[which]

    def pack(self, heads, tails, signs):
        strip = heads // self.strip
        turned = jnp.where(strip % 2 == 1, self.extent - 1 - tails, tails)
        key = strip * self.extent + turned
        key = key * self.strip + heads % self.strip
        return (key << self.rows) | signs

    def unpack(self, key):
        key = jnp.right_shift(key, self.rows)
        low, key = key & (self.strip - 1), jnp.right_shift(key, bits_of(self.strip))
        turned, strip = key & (self.extent - 1), jnp.right_shift(key, bits_of(self.extent))
        tails = jnp.where(strip & 1 == 1, self.extent - 1 - turned, turned)
        return strip * self.strip + low, tails


def flip_mask(size, level):
    low = bits_of(size.regs)
    if level >= low + 10:
        return None
    if level < low + 3:
        place = lax.broadcasted_iota(jnp.int32, (SUB, LANES), 0)
        bit = level - low
    else:
        place = lax.broadcasted_iota(jnp.int32, (SUB, LANES), 1)
        bit = level - low - 3
    return -(jnp.right_shift(place, bit) & 1)


def partner(size, j):
    low = bits_of(size.regs)
    axis, bit = (0, j - low) if j < low + 3 else (1, j - low - 3)
    place = lax.broadcasted_iota(jnp.int32, (SUB, LANES), axis)
    lower = (jnp.right_shift(place, bit) & 1) == 0
    index = jnp.bitwise_xor(place, 1 << bit)
    return axis, index, lower


def sort_edges(size, keys, weights):
    low = bits_of(size.regs)
    levels = low + 10

    def between(group, stages):
        key = {v: keys[v] for v in group}
        weight = {v: weights[v] for v in group}
        for level, j in stages:
            for v in group:
                if v >> j & 1:
                    continue
                a, b = v, v | 1 << j
                if level < low and v >> level & 1:
                    a, b = b, a
                swap = key[a] > key[b]
                key[a], key[b] = jnp.where(swap, key[b], key[a]), jnp.where(swap, key[a], key[b])
                weight[a], weight[b] = (
                    jnp.where(swap, weight[b], weight[a]),
                    jnp.where(swap, weight[a], weight[b]),
                )
        for v in group:
            keys[v] = key[v]
            weights[v] = weight[v]

    def registers(level):
        top = min(level, low)
        if top > 3:
            for v in range(8):
                between(list(range(v, size.regs, 8)), [(level, j) for j in range(top - 1, 2, -1)])
        for v in range(0, size.regs, 8):
            between(list(range(v, v + 8)), [(level, j) for j in range(min(top, 3) - 1, -1, -1)])

    for v in range(0, size.regs, 8):
        between(list(range(v, v + 8)), [(level, j) for level in (1, 2, 3) for j in range(level - 1, -1, -1)])
    for level in range(4, low):
        registers(level)

    for level in range(low, levels + 1):
        before = flip_mask(size, level - 1) if level > low else None
        now = flip_mask(size, level)
        flip = now if before is None else before if now is None else jnp.bitwise_xor(before, now)
        stages = [partner(size, j) for j in range(level - 1, low - 1, -1)]

        wide = min(32, size.regs)

        def across(i, carry, flip=flip, stages=stages):
            group = [i * wide + u for u in range(wide)]
            key = [jnp.bitwise_xor(keys[v], flip) for v in group]
            weight = [weights[v] for v in group]
            for axis, index, lower in stages:
                for u in range(wide):
                    k, w = key[u], weight[u]
                    other = jnp.take_along_axis(k, index, axis=axis, mode="promise_in_bounds")
                    other_w = jnp.take_along_axis(w, index, axis=axis, mode="promise_in_bounds")
                    best = jnp.where(lower, jnp.minimum(k, other), jnp.maximum(k, other))
                    weight[u] = jnp.where(best == k, w, other_w)
                    key[u] = best
            for u, v in enumerate(group):
                keys[v] = key[u]
                weights[v] = weight[u]
            return carry

        lax.fori_loop(0, size.regs // wide, across, 0)
        registers(level)


def sort_kernel(size, place, pay, key_out, heads_out, tails_out, weight_out, bounds, keys, weights):
    word, shift = place[0], place[1]
    per = size.section // SUB
    mask = (1 << size.rows) - 1

    def section(which, g, c):
        return pay[g, which * size.section + c * SUB : which * size.section + (c + 1) * SUB, :]

    for g in range(size.group):
        for c in range(per):
            heads = section(0, g, c).astype(jnp.int32)
            tails = section(1, g, c).astype(jnp.int32)
            signs = jnp.where(word == 0, section(2, g, c), section(3, g, c)).astype(jnp.int32)
            v = g * per + c
            keys[v] = size.pack(heads, tails, jnp.right_shift(signs, shift) & mask)
            weights[v] = section(4, g, c)
    sort_edges(size, keys, weights)
    ends = [size.unpack(keys[v]) for v in range(size.regs)]
    lane = lax.broadcasted_iota(jnp.int32, (1, LANES), 1)
    far = rare = lane < 0
    for which in range(2):
        least = functools.reduce(jnp.minimum, [end[which] for end in ends])
        most = functools.reduce(jnp.maximum, [end[which] for end in ends])
        least = jnp.min(least, axis=0, keepdims=True)
        most = jnp.max(most, axis=0, keepdims=True)
        bounds[2 * which : 2 * which + 1, :] = least
        bounds[2 * which + 1 : 2 * which + 2, :] = most
        if which == 1:
            far = far | (most - (least & -8) >= size.window)
            rare = rare | (most - (least & -8) >= size.window + size.further)
        least, most = least // LANES, most // LANES
        far = far | (most - least >= size.blocks[which])
        rare = rare | (most - least >= size.most[which])
    runs = jnp.where(far, lane, LANES)
    count = jnp.sum(far.astype(F32), axis=1, keepdims=True)
    rare = jnp.max(jnp.where(rare, 1.0, 0.0), axis=1, keepdims=True)
    rare, count = rare.astype(jnp.int32), count.astype(jnp.int32)
    for step in (1, 2, 4, 8, 16, 32, 64):
        after = jnp.where(lane + step < LANES, jnp.roll(runs, -step, axis=1), LANES)
        runs = jnp.minimum(runs, after)
    bounds[4:5, :] = runs
    bounds[5:6, :] = jnp.broadcast_to(rare, (1, LANES))
    bounds[6:7, :] = jnp.broadcast_to(count, (1, LANES))
    for j in range(size.parts):
        here = range(j * 16, (j + 1) * 16)
        key = jnp.concatenate([keys[v] for v in here], axis=0).T
        key_out[j] = key
        heads_out[j], tails_out[j] = size.unpack(key)
        weight_out[j] = jnp.concatenate([weights[v] for v in here], axis=0).T


def halves_of(value):
    high = value.astype(BF).astype(F32)
    return jnp.concatenate([high, value - high], axis=0).astype(BF)


def row(ref, j, run, count):
    return jnp.broadcast_to(ref[j, pl.ds(run, 1), :], (count, LANES))


def next_far(bounds, run):
    following = bounds[4, jnp.minimum(run + 1, LANES - 1)]
    return jnp.where(run + 1 < LANES, following, LANES)


def one_hot(size, index, run, start, window):
    iota = lax.broadcasted_iota(jnp.int32, (16, LANES), 0)
    rows = [(iota + 16 * m).astype(F32).astype(BF) for m in range(16)]
    zero, one = jnp.zeros((16, LANES), BF), jnp.ones((16, LANES), BF)
    hot = []
    for j in range(size.parts):
        column = []
        for at in range(0, window, 256):
            local = (row(index, j, run, 16) - (start + at)).astype(F32).astype(BF)
            count = min(256, window - at) // 16
            column += [jnp.where(local == rows[m], one, zero) for m in range(count)]
        hot.append(jnp.concatenate(column, axis=0))
    return jnp.concatenate(hot, axis=1)


def times(left, right):
    return lax.dot_general(left, right, (((1,), (1,)), ((), ())), preferred_element_type=F32)


def add_blocks(size, heads, run, first, begin, end, pair, acc, valid=True):
    start = (first + begin) * LANES
    if valid is not True:
        start = jnp.where(valid, start, -(1 << 20))
    got = times(pair, one_hot(size, heads, run, start, (end - begin) * LANES))
    for b in range(end - begin):
        acc[first + begin + b] += got[:, b * LANES : (b + 1) * LANES]


def add_rows(size, tails, run, start, window, pair, acc, valid=True):
    start = pl.multiple_of(start, SUB)
    from_ = start if valid is True else jnp.where(valid, start, -(1 << 20))
    acc[pl.ds(start, window), 0:16] += times(one_hot(size, tails, run, from_, window), pair)


def first_block(bounds, which, run):
    return bounds[2 * which, run] // LANES


def last_block(bounds, which, run):
    return bounds[2 * which + 1, run] // LANES


def first_row(bounds, run):
    return bounds[2, run] & -8


def sweep(size, bounds, ends, make, make_far, accs, bufs):
    def fill(buf, base):
        for q in range(SUB):
            for which, pair in enumerate(make(base + q)):
                buf[which, q] = pair

    heads, tails = ends
    acc_h, acc_t = accs

    def use(buf, base):
        for q in range(SUB):
            run = base + q
            add_blocks(size, heads, run, first_block(bounds, 0, run), 0, size.blocks[0], buf[0, q], acc_h)
            add_rows(size, tails, run, first_row(bounds, run), size.window, buf[1, q], acc_t)

    fill(bufs[0], 0)

    def step(i, carry):
        base = i * 2 * SUB
        use(bufs[0], base)
        fill(bufs[1], base + SUB)
        use(bufs[1], base + SUB)
        fill(bufs[0], (base + 2 * SUB) % LANES)
        return carry

    lax.fori_loop(0, LANES // (2 * SUB), step, 0)

    @pl.when(bounds[5, 0] == 0)
    def _():
        def four(i, run):
            for _ in range(4):
                valid, here = run < LANES, jnp.minimum(run, LANES - 1)
                full, beyond = make_far(here, False)
                first = first_block(bounds, 0, here)
                add_blocks(size, heads, here, first, size.blocks[0], size.most[0], full[0], acc_h, valid)
                start = first_row(bounds, here)
                add_rows(size, tails, here, start + size.window, size.further, full[1], acc_t, valid)
                if beyond is not None:
                    add_rows(size, tails, here, start, size.window, beyond[1], acc_t, valid)
                run = jnp.where(valid, next_far(bounds, here), LANES)
            return run

        lax.fori_loop(0, (bounds[6, 0] + 3) // 4, four, bounds[4, 0])

    @pl.when(bounds[5, 0] != 0)
    def _():
        def more(run):
            full, beyond = make_far(run, True)
            first, start = first_block(bounds, 0, run), first_row(bounds, run)

            def block(a, carry):
                add_blocks(size, heads, run, a, 0, 1, full[0], acc_h)
                return carry

            def window(m, carry):
                add_rows(size, tails, run, start + m * size.window, size.window, full[1], acc_t)
                return carry

            lax.fori_loop(first + size.blocks[0], last_block(bounds, 0, run) + 1, block, 0)
            lax.fori_loop(1, (bounds[3, run] - start) // size.window + 1, window, 0)
            if beyond is not None:
                add_blocks(size, heads, run, first, 0, size.blocks[0], beyond[0], acc_h)
                add_rows(size, tails, run, start, size.window, beyond[1], acc_t)
            return next_far(bounds, run)

        lax.while_loop(lambda run: run < LANES, more, bounds[4, 0])


def collect(size, acc_h, acc_t, out_l, out_r):
    shift = size.reach // LANES
    half = size.domain // LANES
    for a in range(size.extent // LANES):
        value = acc_t[a * LANES : (a + 1) * LANES, :].T
        value = value[0:8, :] + value[8:16, :]
        h = a - shift
        if 0 <= h < half:
            value += acc_h[h, 0:8] + acc_h[h, 8:16]
        out, at = (out_l, a) if a < half else (out_r, a - half)
        out[:, at * LANES : (at + 1) * LANES] = value


def clear(acc_h, acc_t):
    acc_h[...] = jnp.zeros_like(acc_h)
    acc_t[...] = jnp.zeros_like(acc_t)


def sketch_kernel(size, bounds, keys, heads, tails, weights, pay, out_l, out_r, acc_h, acc_t, buf_a, buf_b, tables):
    sub = lax.broadcasted_iota(jnp.int32, (SUB, LANES), 0)
    is_sign = sub < size.rows
    clear(acc_h, acc_t)

    def make(run):
        pairs = [[], []]
        for j in range(size.parts):
            weight = row(weights, j, run, SUB)
            bit = jnp.right_shift(row(keys, j, run, SUB), sub) & 1
            signed = (2 * bit - 1).astype(F32) * jnp.sqrt(weight)
            last = jnp.where(sub == size.rows, weight, 0.0)
            pairs[0].append(halves_of(jnp.where(is_sign, signed, last)))
            pairs[1].append(halves_of(jnp.where(is_sign, -signed, last)))
        return [jnp.concatenate(pair, axis=1) for pair in pairs]

    sweep(size, bounds, (heads, tails), make, lambda run, every: (make(run), None), (acc_h, acc_t), (buf_a, buf_b))
    collect(size, acc_h, acc_t, out_l, out_r)
    for g in range(size.group):
        for r in range(size.ground_rows):
            at = size.reach + g * size.verts + r * LANES
            out, at = (out_l, at) if at < size.domain else (out_r, at - size.domain)
            line = 5 * size.section + r
            value = jnp.broadcast_to(pay[g, line : line + 1, :], (SUB, LANES))
            out[:, at : at + LANES] += jnp.where(sub == size.rows, value, 0.0)


def operator_core(size, bounds, heads, tails, weights, table, out_l, out_r, bufs):
    acc_h, acc_t, buf_a, buf_b, tables = bufs
    clear(acc_h, acc_t)
    for a in range(size.extent // LANES):
        tables[a] = table[:, a * LANES : (a + 1) * LANES]
    ends = (heads, tails)

    def take(which, low, high, a, out):
        shift = size.reach // LANES if which == 0 else 0
        got = jnp.take_along_axis(tables[shift + a], low, axis=1, mode="promise_in_bounds")
        return jnp.where(high == a, got, out)

    nothing = jnp.zeros((SUB, LANES), F32)

    def gathered(run, blocks):
        pairs = [[], []]
        for j in range(size.parts):
            weight = row(weights, j, run, SUB)
            for which in range(2):
                index = row(ends[which], j, run, SUB)
                first, (begin, end) = first_block(bounds, which, run), blocks[which]
                low, high = index % LANES, index // LANES
                if end is None:
                    out = lax.fori_loop(
                        first + begin, last_block(bounds, which, run) + 1,
                        lambda a, out: take(which, low, high, a, out), nothing,
                    )
                else:
                    out = nothing
                    for a in range(begin, end):
                        out = take(which, low, high, first + a, out)
                pairs[1 - which].append(halves_of(out * weight))
        return [jnp.concatenate(pair, axis=1) for pair in pairs]

    def make(run):
        return gathered(run, [(0, size.blocks[which]) for which in range(2)])

    def make_far(run, every):
        ends_at = [None, None] if every else size.most
        return (
            gathered(run, [(0, ends_at[which]) for which in range(2)]),
            gathered(run, [(size.blocks[which], ends_at[which]) for which in range(2)]),
        )

    sweep(size, bounds, ends, make, make_far, (acc_h, acc_t), (buf_a, buf_b))
    collect(size, acc_h, acc_t, out_l, out_r)


def halves(size, own_l, own_r, got_l, got_r):
    return ((0, own_l, got_l), (size.domain, own_r, got_r))


def first_kernel(size, bounds, heads, tails, weights, own_l, own_r, got_l, got_r, out_l, out_r, v, diag, *bufs):
    sub = lax.broadcasted_iota(jnp.int32, (SUB, size.domain), 0)
    for at, own, got in halves(size, own_l, own_r, got_l, got_r):
        total = own[...] + got[...]
        spread = jnp.broadcast_to(total[size.rows : size.rows + 1, :], total.shape)
        safe = jnp.where(spread > 0.0, spread, 1.0)
        diag[:, at : at + size.domain] = safe
        v[:, at : at + size.domain] = jnp.where(sub < size.rows, total / safe, 0.0)
    operator_core(size, bounds, heads, tails, weights, v, out_l, out_r, bufs)


def next_v(size, own_l, own_r, got_l, got_r, diag, v):
    for at, own, got in halves(size, own_l, own_r, got_l, got_r):
        v[:, at : at + size.domain] = (own[...] + got[...]) / diag[:, at : at + size.domain]


def second_kernel(size, bounds, heads, tails, weights, own_l, own_r, got_l, got_r, diag, out_l, out_r, v, *bufs):
    next_v(size, own_l, own_r, got_l, got_r, diag, v)
    operator_core(size, bounds, heads, tails, weights, v, out_l, out_r, bufs)


def third_kernel(size, bounds, heads, tails, weights, own_l, own_r, got_l, got_r, diag, v0, v1, out_l, out_r, v2, moments, *bufs):
    next_v(size, own_l, own_r, got_l, got_r, diag, v2)
    operator_core(size, bounds, heads, tails, weights, v2, out_l, out_r, bufs)
    lane = lax.broadcasted_iota(jnp.int32, (SUB, LANES), 1)
    middle = slice(size.reach, size.reach + size.domain)
    weighted = diag[:, middle] * v0[:, middle]
    other = diag[:, middle] * v1[:, middle]
    sums = [
        weighted * v0[:, middle],
        weighted * v1[:, middle],
        other * v1[:, middle],
        other * v2[:, middle],
        diag[:, middle] * v2[:, middle] * v2[:, middle],
        v2[:, : size.domain] * out_l[...] + v2[:, size.domain :] * out_r[...],
    ]
    out = jnp.zeros((SUB, LANES), F32)
    for k, value in enumerate(sums):
        out = jnp.where(lane == k, jnp.sum(value, axis=1, keepdims=True), out)
    moments[...] = out


def coefficients(mu):
    zero = jnp.zeros_like(mu[0])

    def inner(a, b):
        total = None
        for i, x in enumerate(a):
            for j, y in enumerate(b):
                term = mu[i + j] if x is None and y is None else mu[i + j] * (y if x is None else x if y is None else x * y)
                total = term if total is None else total + term
        return total

    def image(a):
        a = [jnp.ones_like(zero) if x is None else x for x in a] + [zero]
        return [a[0]] + [a[i] - a[i - 1] for i in range(1, len(a))]

    def ratio(top, bottom):
        return jnp.where(bottom > 0.0, top / jnp.where(bottom > 0.0, bottom, 1.0), 0.0)

    rho, pi, x = [jnp.ones_like(zero)], [jnp.ones_like(zero)], []
    gamma = inner(rho, rho)
    for step in range(3):
        moved = image(pi)
        alpha = ratio(gamma, inner(pi, moved))
        x = [(x[i] if i < len(x) else zero) + alpha * pi[i] for i in range(len(pi))]
        rho = [(rho[i] if i < len(rho) else zero) - alpha * moved[i] for i in range(len(moved))]
        if step < 2:
            following = inner(rho, rho)
            beta = ratio(following, gamma)
            pi = [rho[i] + (beta * pi[i] if i < len(pi) else zero) for i in range(len(rho))]
            gamma = following
    return x, rho


def last_kernel(size, moments, own_l, own_r, got_l, got_r, diag, v0, v1, v2, out):
    total = moments[...]
    mu = [jnp.broadcast_to(total[:, k : k + 1], (SUB, LANES)) for k in range(6)]
    x, rho = coefficients(mu)
    x = [value[:, :1] for value in x]
    rho = [value[:, :1] for value in rho]
    for g in range(size.group):
        at = size.reach + g * size.verts
        here = slice(at, at + size.verts)
        if at < size.domain:
            sums = own_l[:, here] + got_l[:, g * size.verts : (g + 1) * size.verts]
        else:
            back = at - size.domain
            inside = slice(back, back + size.verts)
            sums = own_r[:, inside] + got_r[:, inside]
        a, b, c, scale = v0[:, here], v1[:, here], v2[:, here], diag[:, here]
        out[g, 0] = x[0] * a + x[1] * b + x[2] * c
        out[g, 1] = scale * (rho[0] * a + rho[1] * b + rho[2] * c) + rho[3] * sums


def total_over_dom(value, count):
    if count & (count - 1):
        return jnp.sum(lax.all_gather(value, "dom"), axis=0)
    step = 1
    while step < count:
        value = value + lax.ppermute(value, "dom", [(i, i ^ step) for i in range(count)])
        step *= 2
    return value


def on_device(heads, tails, signs, edge_weights, ground):
    group = lax.axis_size("grp")
    count = lax.axis_size("dom")
    size = Sizes(heads.shape[0], ground.shape[0], group)
    vmem = pl.BlockSpec(memory_space=pltpu.VMEM)
    smem = pl.BlockSpec(memory_space=pltpu.SMEM)
    params = pltpu.CompilerParams(vmem_limit_bytes=48 * 1024 * 1024)

    def flat(value):
        return value.astype(F32).reshape(-1, LANES)

    parts = [flat(heads), flat(tails), flat(signs[0]), flat(signs[1]), flat(edge_weights), flat(ground)]
    used = sum(part.shape[0] for part in parts)
    parts.append(jnp.zeros((size.payload - used, LANES), F32))
    pay = lax.all_gather(jnp.concatenate(parts, axis=0), "grp")

    half = jax.ShapeDtypeStruct((SUB, size.domain), F32)
    full = jax.ShapeDtypeStruct((SUB, size.extent), F32)

    def exchange(left, right):
        up = [(i, i + 1) for i in range(count - 1)]
        down = [(i + 1, i) for i in range(count - 1)]
        return lax.ppermute(right, "dom", up), lax.ppermute(left, "dom", down)

    me = lax.axis_index("grp")
    first_row = me * size.rows
    place = jnp.stack([first_row // HALF, first_row % HALF]).astype(jnp.int32)
    spread = (size.parts, LANES, LANES)
    keys, heads, tails, weights, bounds = pl.pallas_call(
        functools.partial(sort_kernel, size),
        out_shape=(
            jax.ShapeDtypeStruct(spread, jnp.int32),
            jax.ShapeDtypeStruct(spread, jnp.int32),
            jax.ShapeDtypeStruct(spread, jnp.int32),
            jax.ShapeDtypeStruct(spread, F32),
            jax.ShapeDtypeStruct((SUB, LANES), jnp.int32),
        ),
        in_specs=[smem, vmem],
        out_specs=(vmem,) * 5,
        scratch_shapes=[
            pltpu.VMEM((size.regs, SUB, LANES), jnp.int32),
            pltpu.VMEM((size.regs, SUB, LANES), F32),
        ],
        compiler_params=params,
        name="sort_edges",
    )(place, pay)
    edges = (bounds, heads, tails, weights)
    edge_specs = [smem, vmem, vmem, vmem]
    scratch = [
        pltpu.VMEM((size.padded(0), 16, LANES), F32),
        pltpu.VMEM((size.extent + size.window + size.further, LANES), F32),
        pltpu.VMEM((2, SUB, 16, size.parts * LANES), BF),
        pltpu.VMEM((2, SUB, 16, size.parts * LANES), BF),
        pltpu.VMEM((size.padded(1) + size.most[0], SUB, LANES), F32),
    ]
    acc = pl.pallas_call(
        functools.partial(sketch_kernel, size),
        out_shape=(half, half),
        in_specs=edge_specs + [vmem] * 2,
        out_specs=(vmem, vmem),
        scratch_shapes=scratch,
        compiler_params=params,
        name="sketch",
    )(bounds, keys, heads, tails, weights, pay)
    got = exchange(*acc)
    *acc, v0, diag = pl.pallas_call(
        functools.partial(first_kernel, size),
        out_shape=(half, half, full, full),
        in_specs=edge_specs + [vmem] * 4,
        out_specs=(vmem,) * 4,
        scratch_shapes=scratch,
        compiler_params=params,
        name="operator_first",
    )(*edges, *acc, *got)
    got = exchange(*acc)
    *acc, v1 = pl.pallas_call(
        functools.partial(second_kernel, size),
        out_shape=(half, half, full),
        in_specs=edge_specs + [vmem] * 5,
        out_specs=(vmem,) * 3,
        scratch_shapes=scratch,
        compiler_params=params,
        name="operator_second",
    )(*edges, *acc, *got, diag)
    got = exchange(*acc)
    *acc, v2, moments = pl.pallas_call(
        functools.partial(third_kernel, size),
        out_shape=(half, half, full, jax.ShapeDtypeStruct((SUB, LANES), F32)),
        in_specs=edge_specs + [vmem] * 7,
        out_specs=(vmem,) * 4,
        scratch_shapes=scratch,
        compiler_params=params,
        name="operator_third",
    )(*edges, *acc, *got, diag, v0, v1)
    up = [(i, i + 1) for i in range(count - 1)]
    down = [(i + 1, i) for i in range(count - 1)]
    got_l = lax.ppermute(acc[1][:, size.reach :], "dom", up)
    got_r = lax.ppermute(acc[0][:, : size.reach], "dom", down)
    shared = total_over_dom(moments, count)
    out = pl.pallas_call(
        functools.partial(last_kernel, size),
        out_shape=jax.ShapeDtypeStruct((group, 2, SUB, size.verts), F32),
        in_specs=[vmem] * 9,
        out_specs=vmem,
        compiler_params=params,
        name="combine",
    )(shared, *acc, got_l, got_r, diag, v0, v1, v2)
    out = lax.all_to_all(out[:, :, : size.rows, :], "grp", 0, 0)
    return (out[:, 0].reshape(K, size.verts), out[:, 1].reshape(K, size.verts))


def solution(mesh):
    in_specs = (
        P(("dom", "grp")),
        P(("dom", "grp")),
        P(None, ("dom", "grp")),
        P(("dom", "grp")),
        P(("dom", "grp")),
    )
    out_specs = (P(None, ("dom", "grp")), P(None, ("dom", "grp")))
    return jax.shard_map(
        on_device, mesh=mesh, in_specs=in_specs, out_specs=out_specs, check_vma=False
    )
```

```python
import functools

import jax
import jax.numpy as jnp
from jax import lax
from jax.experimental import pallas as pl
from jax.experimental.pallas import tpu as pltpu
from jax.sharding import PartitionSpec as P

K = 24
HALF = 12
LANES = 128
SUB = 8
BF = jnp.bfloat16
F32 = jnp.float32


def row_of(block, r, count):
    return jnp.broadcast_to(block[r : r + 1, :], (count, LANES))


def bits_of(n):
    return (n - 1).bit_length()


class Sizes:
    def __init__(self, edev, verts, group):
        self.edev, self.verts, self.group = edev, verts, group
        self.domain = verts * group
        self.reach = self.domain // 2
        self.extent = self.domain + 2 * self.reach
        self.rows = K // group
        self.section = edev // LANES
        self.ground_rows = verts // LANES
        self.payload = -(-(5 * self.section + self.ground_rows) // SUB) * SUB
        self.regs = edev * group // (SUB * LANES)
        self.parts = self.regs * SUB // LANES
        self.strip = self.domain // 8
        self.blocks = (self.strip // LANES, self.extent // 16 // LANES + 2)
        self.most = (2 * self.blocks[0], self.blocks[1])
        self.window = self.extent // 16 + 64
        self.further = self.extent // 64

    def padded(self, which):
        return (self.domain, self.extent)[which] // LANES + self.most[which]

    def pack(self, heads, tails, signs):
        strip = heads // self.strip
        turned = jnp.where(strip % 2 == 1, self.extent - 1 - tails, tails)
        key = strip * self.extent + turned
        key = key * self.strip + heads % self.strip
        return (key << self.rows) | signs

    def unpack(self, key):
        key = jnp.right_shift(key, self.rows)
        low, key = key & (self.strip - 1), jnp.right_shift(key, bits_of(self.strip))
        turned, strip = key & (self.extent - 1), jnp.right_shift(key, bits_of(self.extent))
        tails = jnp.where(strip & 1 == 1, self.extent - 1 - turned, turned)
        return strip * self.strip + low, tails


def flip_mask(size, level):
    low = bits_of(size.regs)
    if level >= low + 10:
        return None
    if level < low + 3:
        place = lax.broadcasted_iota(jnp.int32, (SUB, LANES), 0)
        bit = level - low
    else:
        place = lax.broadcasted_iota(jnp.int32, (SUB, LANES), 1)
        bit = level - low - 3
    return -(jnp.right_shift(place, bit) & 1)


def partner(size, j):
    low = bits_of(size.regs)
    axis, bit = (0, j - low) if j < low + 3 else (1, j - low - 3)
    place = lax.broadcasted_iota(jnp.int32, (SUB, LANES), axis)
    lower = (jnp.right_shift(place, bit) & 1) == 0
    index = jnp.bitwise_xor(place, 1 << bit)
    return axis, index, lower


def sort_edges(size, keys, weights):
    low = bits_of(size.regs)
    levels = low + 10

    def between(group, stages):
        key = {v: keys[v] for v in group}
        weight = {v: weights[v] for v in group}
        for level, j in stages:
            for v in group:
                if v >> j & 1:
                    continue
                a, b = v, v | 1 << j
                if level < low and v >> level & 1:
                    a, b = b, a
                swap = key[a] > key[b]
                key[a], key[b] = jnp.where(swap, key[b], key[a]), jnp.where(swap, key[a], key[b])
                weight[a], weight[b] = (
                    jnp.where(swap, weight[b], weight[a]),
                    jnp.where(swap, weight[a], weight[b]),
                )
        for v in group:
            keys[v] = key[v]
            weights[v] = weight[v]

    def registers(level):
        top = min(level, low)
        if top > 3:
            for v in range(8):
                between(list(range(v, size.regs, 8)), [(level, j) for j in range(top - 1, 2, -1)])
        for v in range(0, size.regs, 8):
            between(list(range(v, v + 8)), [(level, j) for j in range(min(top, 3) - 1, -1, -1)])

    for v in range(0, size.regs, 8):
        between(list(range(v, v + 8)), [(level, j) for level in (1, 2, 3) for j in range(level - 1, -1, -1)])
    for level in range(4, low):
        registers(level)

    for level in range(low, levels + 1):
        before = flip_mask(size, level - 1) if level > low else None
        now = flip_mask(size, level)
        flip = now if before is None else before if now is None else jnp.bitwise_xor(before, now)
        stages = [partner(size, j) for j in range(level - 1, low - 1, -1)]

        wide = min(32, size.regs)

        def across(i, carry, flip=flip, stages=stages):
            group = [i * wide + u for u in range(wide)]
            key = [jnp.bitwise_xor(keys[v], flip) for v in group]
            weight = [weights[v] for v in group]
            for axis, index, lower in stages:
                for u in range(wide):
                    k, w = key[u], weight[u]
                    other = jnp.take_along_axis(k, index, axis=axis, mode="promise_in_bounds")
                    other_w = jnp.take_along_axis(w, index, axis=axis, mode="promise_in_bounds")
                    best = jnp.where(lower, jnp.minimum(k, other), jnp.maximum(k, other))
                    weight[u] = jnp.where(best == k, w, other_w)
                    key[u] = best
            for u, v in enumerate(group):
                keys[v] = key[u]
                weights[v] = weight[u]
            return carry

        lax.fori_loop(0, size.regs // wide, across, 0)
        registers(level)


def sort_kernel(size, place, pay, key_out, heads_out, tails_out, weight_out, bounds, keys, weights):
    word, shift = place[0], place[1]
    per = size.section // SUB
    mask = (1 << size.rows) - 1

    def section(which, g, c):
        return pay[g, which * size.section + c * SUB : which * size.section + (c + 1) * SUB, :]

    for g in range(size.group):
        for c in range(per):
            heads = section(0, g, c).astype(jnp.int32)
            tails = section(1, g, c).astype(jnp.int32)
            signs = jnp.where(word == 0, section(2, g, c), section(3, g, c)).astype(jnp.int32)
            v = g * per + c
            keys[v] = size.pack(heads, tails, jnp.right_shift(signs, shift) & mask)
            weights[v] = section(4, g, c)
    sort_edges(size, keys, weights)
    ends = [size.unpack(keys[v]) for v in range(size.regs)]
    lane = lax.broadcasted_iota(jnp.int32, (1, LANES), 1)
    far = rare = lane < 0
    for which in range(2):
        least = functools.reduce(jnp.minimum, [end[which] for end in ends])
        most = functools.reduce(jnp.maximum, [end[which] for end in ends])
        least = jnp.min(least, axis=0, keepdims=True)
        most = jnp.max(most, axis=0, keepdims=True)
        bounds[2 * which : 2 * which + 1, :] = least
        bounds[2 * which + 1 : 2 * which + 2, :] = most
        if which == 1:
            far = far | (most - (least & -8) >= size.window)
            rare = rare | (most - (least & -8) >= size.window + size.further)
        least, most = least // LANES, most // LANES
        far = far | (most - least >= size.blocks[which])
        rare = rare | (most - least >= size.most[which])
    runs = jnp.where(far, lane, LANES)
    count = jnp.sum(far.astype(F32), axis=1, keepdims=True)
    rare = jnp.max(jnp.where(rare, 1.0, 0.0), axis=1, keepdims=True)
    rare, count = rare.astype(jnp.int32), count.astype(jnp.int32)
    for step in (1, 2, 4, 8, 16, 32, 64):
        after = jnp.where(lane + step < LANES, jnp.roll(runs, -step, axis=1), LANES)
        runs = jnp.minimum(runs, after)
    bounds[4:5, :] = runs
    bounds[5:6, :] = jnp.broadcast_to(rare, (1, LANES))
    bounds[6:7, :] = jnp.broadcast_to(count, (1, LANES))
    for j in range(size.parts):
        here = range(j * 16, (j + 1) * 16)
        key = jnp.concatenate([keys[v] for v in here], axis=0).T
        key_out[j] = key
        heads_out[j], tails_out[j] = size.unpack(key)
        weight_out[j] = jnp.concatenate([weights[v] for v in here], axis=0).T


def halves_of(value):
    high = value.astype(BF).astype(F32)
    return jnp.concatenate([high, value - high], axis=0).astype(BF)


def row(ref, j, run, count):
    return jnp.broadcast_to(ref[j, pl.ds(run, 1), :], (count, LANES))


def next_far(bounds, run):
    following = bounds[4, jnp.minimum(run + 1, LANES - 1)]
    return jnp.where(run + 1 < LANES, following, LANES)


def one_hot(size, index, run, start, window):
    iota = lax.broadcasted_iota(jnp.int32, (16, LANES), 0)
    rows = [(iota + 16 * m).astype(F32).astype(BF) for m in range(16)]
    zero, one = jnp.zeros((16, LANES), BF), jnp.ones((16, LANES), BF)
    hot = []
    for j in range(size.parts):
        column = []
        for at in range(0, window, 256):
            local = (row(index, j, run, 16) - (start + at)).astype(F32).astype(BF)
            count = min(256, window - at) // 16
            column += [jnp.where(local == rows[m], one, zero) for m in range(count)]
        hot.append(jnp.concatenate(column, axis=0))
    return jnp.concatenate(hot, axis=1)


def times(left, right):
    return lax.dot_general(left, right, (((1,), (1,)), ((), ())), preferred_element_type=F32)


def add_blocks(size, heads, run, first, begin, end, pair, acc, valid=True):
    start = (first + begin) * LANES
    if valid is not True:
        start = jnp.where(valid, start, -(1 << 20))
    got = times(pair, one_hot(size, heads, run, start, (end - begin) * LANES))
    for b in range(end - begin):
        acc[first + begin + b] += got[:, b * LANES : (b + 1) * LANES]


def add_rows(size, tails, run, start, window, pair, acc, valid=True):
    start = pl.multiple_of(start, SUB)
    from_ = start if valid is True else jnp.where(valid, start, -(1 << 20))
    acc[pl.ds(start, window), 0:16] += times(one_hot(size, tails, run, from_, window), pair)


def first_block(bounds, which, run):
    return bounds[2 * which, run] // LANES


def last_block(bounds, which, run):
    return bounds[2 * which + 1, run] // LANES


def first_row(bounds, run):
    return bounds[2, run] & -8


def sweep(size, bounds, ends, make, make_far, accs, bufs):
    def fill(buf, base):
        for q in range(SUB):
            for which, pair in enumerate(make(base + q)):
                buf[which, q] = pair

    heads, tails = ends
    acc_h, acc_t = accs

    def use(buf, base):
        for q in range(SUB):
            run = base + q
            add_blocks(size, heads, run, first_block(bounds, 0, run), 0, size.blocks[0], buf[0, q], acc_h)
            add_rows(size, tails, run, first_row(bounds, run), size.window, buf[1, q], acc_t)

    fill(bufs[0], 0)

    def step(i, carry):
        base = i * 2 * SUB
        use(bufs[0], base)
        fill(bufs[1], base + SUB)
        use(bufs[1], base + SUB)
        fill(bufs[0], (base + 2 * SUB) % LANES)
        return carry

    lax.fori_loop(0, LANES // (2 * SUB), step, 0)

    @pl.when(bounds[5, 0] == 0)
    def _():
        def four(i, run):
            for _ in range(4):
                valid, here = run < LANES, jnp.minimum(run, LANES - 1)
                full, beyond = make_far(here, False)
                first = first_block(bounds, 0, here)
                add_blocks(size, heads, here, first, size.blocks[0], size.most[0], full[0], acc_h, valid)
                start = first_row(bounds, here)
                add_rows(size, tails, here, start + size.window, size.further, full[1], acc_t, valid)
                if beyond is not None:
                    add_rows(size, tails, here, start, size.window, beyond[1], acc_t, valid)
                run = jnp.where(valid, next_far(bounds, here), LANES)
            return run

        lax.fori_loop(0, (bounds[6, 0] + 3) // 4, four, bounds[4, 0])

    @pl.when(bounds[5, 0] != 0)
    def _():
        def more(run):
            full, beyond = make_far(run, True)
            first, start = first_block(bounds, 0, run), first_row(bounds, run)

            def block(a, carry):
                add_blocks(size, heads, run, a, 0, 1, full[0], acc_h)
                return carry

            def window(m, carry):
                add_rows(size, tails, run, start + m * size.window, size.window, full[1], acc_t)
                return carry

            lax.fori_loop(first + size.blocks[0], last_block(bounds, 0, run) + 1, block, 0)
            lax.fori_loop(1, (bounds[3, run] - start) // size.window + 1, window, 0)
            if beyond is not None:
                add_blocks(size, heads, run, first, 0, size.blocks[0], beyond[0], acc_h)
                add_rows(size, tails, run, start, size.window, beyond[1], acc_t)
            return next_far(bounds, run)

        lax.while_loop(lambda run: run < LANES, more, bounds[4, 0])


def collect(size, acc_h, acc_t, out_l, out_r):
    shift = size.reach // LANES
    half = size.domain // LANES
    for a in range(size.extent // LANES):
        value = acc_t[a * LANES : (a + 1) * LANES, :].T
        value = value[0:8, :] + value[8:16, :]
        h = a - shift
        if 0 <= h < half:
            value += acc_h[h, 0:8] + acc_h[h, 8:16]
        out, at = (out_l, a) if a < half else (out_r, a - half)
        out[:, at * LANES : (at + 1) * LANES] = value


def clear(acc_h, acc_t):
    acc_h[...] = jnp.zeros_like(acc_h)
    acc_t[...] = jnp.zeros_like(acc_t)


def sketch_kernel(size, bounds, keys, heads, tails, weights, pay, out_l, out_r, acc_h, acc_t, buf_a, buf_b, tables):
    sub = lax.broadcasted_iota(jnp.int32, (SUB, LANES), 0)
    is_sign = sub < size.rows
    clear(acc_h, acc_t)

    def make(run):
        pairs = [[], []]
        for j in range(size.parts):
            weight = row(weights, j, run, SUB)
            bit = jnp.right_shift(row(keys, j, run, SUB), sub) & 1
            signed = (2 * bit - 1).astype(F32) * jnp.sqrt(weight)
            last = jnp.where(sub == size.rows, weight, 0.0)
            pairs[0].append(halves_of(jnp.where(is_sign, signed, last)))
            pairs[1].append(halves_of(jnp.where(is_sign, -signed, last)))
        return [jnp.concatenate(pair, axis=1) for pair in pairs]

    sweep(size, bounds, (heads, tails), make, lambda run, every: (make(run), None), (acc_h, acc_t), (buf_a, buf_b))
    collect(size, acc_h, acc_t, out_l, out_r)
    for g in range(size.group):
        for r in range(size.ground_rows):
            at = size.reach + g * size.verts + r * LANES
            out, at = (out_l, at) if at < size.domain else (out_r, at - size.domain)
            line = 5 * size.section + r
            value = jnp.broadcast_to(pay[g, line : line + 1, :], (SUB, LANES))
            out[:, at : at + LANES] += jnp.where(sub == size.rows, value, 0.0)


def operator_core(size, bounds, heads, tails, weights, table, out_l, out_r, bufs):
    acc_h, acc_t, buf_a, buf_b, tables = bufs
    clear(acc_h, acc_t)
    for a in range(size.extent // LANES):
        tables[a] = table[:, a * LANES : (a + 1) * LANES]
    ends = (heads, tails)

    def take(which, low, high, a, out):
        shift = size.reach // LANES if which == 0 else 0
        got = jnp.take_along_axis(tables[shift + a], low, axis=1, mode="promise_in_bounds")
        return jnp.where(high == a, got, out)

    nothing = jnp.zeros((SUB, LANES), F32)

    def gathered(run, blocks):
        pairs = [[], []]
        for j in range(size.parts):
            weight = row(weights, j, run, SUB)
            for which in range(2):
                index = row(ends[which], j, run, SUB)
                first, (begin, end) = first_block(bounds, which, run), blocks[which]
                low, high = index % LANES, index // LANES
                if end is None:
                    out = lax.fori_loop(
                        first + begin, last_block(bounds, which, run) + 1,
                        lambda a, out: take(which, low, high, a, out), nothing,
                    )
                else:
                    out = nothing
                    for a in range(begin, end):
                        out = take(which, low, high, first + a, out)
                pairs[1 - which].append(halves_of(out * weight))
        return [jnp.concatenate(pair, axis=1) for pair in pairs]

    def make(run):
        return gathered(run, [(0, size.blocks[which]) for which in range(2)])

    def make_far(run, every):
        ends_at = [None, None] if every else size.most
        return (
            gathered(run, [(0, ends_at[which]) for which in range(2)]),
            gathered(run, [(size.blocks[which], ends_at[which]) for which in range(2)]),
        )

    sweep(size, bounds, ends, make, make_far, (acc_h, acc_t), (buf_a, buf_b))
    collect(size, acc_h, acc_t, out_l, out_r)


def halves(size, own_l, own_r, got_l, got_r):
    return ((0, own_l, got_l), (size.domain, own_r, got_r))


def first_kernel(size, bounds, heads, tails, weights, own_l, own_r, got_l, got_r, out_l, out_r, v, diag, *bufs):
    sub = lax.broadcasted_iota(jnp.int32, (SUB, size.domain), 0)
    for at, own, got in halves(size, own_l, own_r, got_l, got_r):
        total = own[...] + got[...]
        spread = jnp.broadcast_to(total[size.rows : size.rows + 1, :], total.shape)
        safe = jnp.where(spread > 0.0, spread, 1.0)
        diag[:, at : at + size.domain] = safe
        v[:, at : at + size.domain] = jnp.where(sub < size.rows, total / safe, 0.0)
    operator_core(size, bounds, heads, tails, weights, v, out_l, out_r, bufs)


def next_v(size, own_l, own_r, got_l, got_r, diag, v):
    for at, own, got in halves(size, own_l, own_r, got_l, got_r):
        v[:, at : at + size.domain] = (own[...] + got[...]) / diag[:, at : at + size.domain]


def second_kernel(size, bounds, heads, tails, weights, own_l, own_r, got_l, got_r, diag, out_l, out_r, v, *bufs):
    next_v(size, own_l, own_r, got_l, got_r, diag, v)
    operator_core(size, bounds, heads, tails, weights, v, out_l, out_r, bufs)


def third_kernel(size, bounds, heads, tails, weights, own_l, own_r, got_l, got_r, diag, v0, v1, out_l, out_r, v2, moments, *bufs):
    next_v(size, own_l, own_r, got_l, got_r, diag, v2)
    operator_core(size, bounds, heads, tails, weights, v2, out_l, out_r, bufs)
    lane = lax.broadcasted_iota(jnp.int32, (SUB, LANES), 1)
    middle = slice(size.reach, size.reach + size.domain)
    weighted = diag[:, middle] * v0[:, middle]
    other = diag[:, middle] * v1[:, middle]
    sums = [
        weighted * v0[:, middle],
        weighted * v1[:, middle],
        other * v1[:, middle],
        other * v2[:, middle],
        diag[:, middle] * v2[:, middle] * v2[:, middle],
        v2[:, : size.domain] * out_l[...] + v2[:, size.domain :] * out_r[...],
    ]
    out = jnp.zeros((SUB, LANES), F32)
    for k, value in enumerate(sums):
        out = jnp.where(lane == k, jnp.sum(value, axis=1, keepdims=True), out)
    moments[...] = out


def coefficients(mu):
    zero = jnp.zeros_like(mu[0])

    def inner(a, b):
        total = None
        for i, x in enumerate(a):
            for j, y in enumerate(b):
                term = mu[i + j] if x is None and y is None else mu[i + j] * (y if x is None else x if y is None else x * y)
                total = term if total is None else total + term
        return total

    def image(a):
        a = [jnp.ones_like(zero) if x is None else x for x in a] + [zero]
        return [a[0]] + [a[i] - a[i - 1] for i in range(1, len(a))]

    def ratio(top, bottom):
        return jnp.where(bottom > 0.0, top / jnp.where(bottom > 0.0, bottom, 1.0), 0.0)

    rho, pi, x = [jnp.ones_like(zero)], [jnp.ones_like(zero)], []
    gamma = inner(rho, rho)
    for step in range(3):
        moved = image(pi)
        alpha = ratio(gamma, inner(pi, moved))
        x = [(x[i] if i < len(x) else zero) + alpha * pi[i] for i in range(len(pi))]
        rho = [(rho[i] if i < len(rho) else zero) - alpha * moved[i] for i in range(len(moved))]
        if step < 2:
            following = inner(rho, rho)
            beta = ratio(following, gamma)
            pi = [rho[i] + (beta * pi[i] if i < len(pi) else zero) for i in range(len(rho))]
            gamma = following
    return x, rho


def last_kernel(size, moments, own_l, own_r, got_l, got_r, diag, v0, v1, v2, out):
    total = moments[0]
    for d in range(1, moments.shape[0]):
        total = total + moments[d]
    mu = [jnp.broadcast_to(total[:, k : k + 1], (SUB, LANES)) for k in range(6)]
    x, rho = coefficients(mu)
    x = [value[:, :1] for value in x]
    rho = [value[:, :1] for value in rho]
    for g in range(size.group):
        at = size.reach + g * size.verts
        here = slice(at, at + size.verts)
        if at < size.domain:
            sums = own_l[:, here] + got_l[:, g * size.verts : (g + 1) * size.verts]
        else:
            back = at - size.domain
            inside = slice(back, back + size.verts)
            sums = own_r[:, inside] + got_r[:, inside]
        a, b, c, scale = v0[:, here], v1[:, here], v2[:, here], diag[:, here]
        out[g, 0] = x[0] * a + x[1] * b + x[2] * c
        out[g, 1] = scale * (rho[0] * a + rho[1] * b + rho[2] * c) + rho[3] * sums


def order_kernel(size, parts, x, r):
    for g in range(size.group):
        here = slice(g * size.rows, (g + 1) * size.rows)
        x[here, :] = parts[g, 0, : size.rows]
        r[here, :] = parts[g, 1, : size.rows]


def on_device(heads, tails, signs, edge_weights, ground):
    group = lax.axis_size("grp")
    count = lax.axis_size("dom")
    size = Sizes(heads.shape[0], ground.shape[0], group)
    vmem = pl.BlockSpec(memory_space=pltpu.VMEM)
    smem = pl.BlockSpec(memory_space=pltpu.SMEM)
    params = pltpu.CompilerParams(vmem_limit_bytes=48 * 1024 * 1024)

    def flat(value):
        return value.astype(F32).reshape(-1, LANES)

    parts = [flat(heads), flat(tails), flat(signs[0]), flat(signs[1]), flat(edge_weights), flat(ground)]
    used = sum(part.shape[0] for part in parts)
    parts.append(jnp.zeros((size.payload - used, LANES), F32))
    pay = lax.all_gather(jnp.concatenate(parts, axis=0), "grp")

    half = jax.ShapeDtypeStruct((SUB, size.domain), F32)
    full = jax.ShapeDtypeStruct((SUB, size.extent), F32)

    def exchange(left, right):
        up = [(i, i + 1) for i in range(count - 1)]
        down = [(i + 1, i) for i in range(count - 1)]
        return lax.ppermute(right, "dom", up), lax.ppermute(left, "dom", down)

    me = lax.axis_index("grp")
    first_row = me * size.rows
    place = jnp.stack([first_row // HALF, first_row % HALF]).astype(jnp.int32)
    spread = (size.parts, LANES, LANES)
    keys, heads, tails, weights, bounds = pl.pallas_call(
        functools.partial(sort_kernel, size),
        out_shape=(
            jax.ShapeDtypeStruct(spread, jnp.int32),
            jax.ShapeDtypeStruct(spread, jnp.int32),
            jax.ShapeDtypeStruct(spread, jnp.int32),
            jax.ShapeDtypeStruct(spread, F32),
            jax.ShapeDtypeStruct((SUB, LANES), jnp.int32),
        ),
        in_specs=[smem, vmem],
        out_specs=(vmem,) * 5,
        scratch_shapes=[
            pltpu.VMEM((size.regs, SUB, LANES), jnp.int32),
            pltpu.VMEM((size.regs, SUB, LANES), F32),
        ],
        compiler_params=params,
        name="sort_edges",
    )(place, pay)
    edges = (bounds, heads, tails, weights)
    edge_specs = [smem, vmem, vmem, vmem]
    scratch = [
        pltpu.VMEM((size.padded(0), 16, LANES), F32),
        pltpu.VMEM((size.extent + size.window + size.further, LANES), F32),
        pltpu.VMEM((2, SUB, 16, size.parts * LANES), BF),
        pltpu.VMEM((2, SUB, 16, size.parts * LANES), BF),
        pltpu.VMEM((size.padded(1) + size.most[0], SUB, LANES), F32),
    ]
    acc = pl.pallas_call(
        functools.partial(sketch_kernel, size),
        out_shape=(half, half),
        in_specs=edge_specs + [vmem] * 2,
        out_specs=(vmem, vmem),
        scratch_shapes=scratch,
        compiler_params=params,
        name="sketch",
    )(bounds, keys, heads, tails, weights, pay)
    got = exchange(*acc)
    *acc, v0, diag = pl.pallas_call(
        functools.partial(first_kernel, size),
        out_shape=(half, half, full, full),
        in_specs=edge_specs + [vmem] * 4,
        out_specs=(vmem,) * 4,
        scratch_shapes=scratch,
        compiler_params=params,
        name="operator_first",
    )(*edges, *acc, *got)
    got = exchange(*acc)
    *acc, v1 = pl.pallas_call(
        functools.partial(second_kernel, size),
        out_shape=(half, half, full),
        in_specs=edge_specs + [vmem] * 5,
        out_specs=(vmem,) * 3,
        scratch_shapes=scratch,
        compiler_params=params,
        name="operator_second",
    )(*edges, *acc, *got, diag)
    got = exchange(*acc)
    *acc, v2, moments = pl.pallas_call(
        functools.partial(third_kernel, size),
        out_shape=(half, half, full, jax.ShapeDtypeStruct((SUB, LANES), F32)),
        in_specs=edge_specs + [vmem] * 7,
        out_specs=(vmem,) * 4,
        scratch_shapes=scratch,
        compiler_params=params,
        name="operator_third",
    )(*edges, *acc, *got, diag, v0, v1)
    up = [(i, i + 1) for i in range(count - 1)]
    down = [(i + 1, i) for i in range(count - 1)]
    got_l = lax.ppermute(acc[1][:, size.reach :], "dom", up)
    got_r = lax.ppermute(acc[0][:, : size.reach], "dom", down)
    shared = lax.all_to_all(jnp.broadcast_to(moments, (count, SUB, LANES)), "dom", 0, 0)
    out = pl.pallas_call(
        functools.partial(last_kernel, size),
        out_shape=jax.ShapeDtypeStruct((group, 2, SUB, size.verts), F32),
        in_specs=[vmem] * 9,
        out_specs=vmem,
        compiler_params=params,
        name="combine",
    )(shared, *acc, got_l, got_r, diag, v0, v1, v2)
    out = lax.all_to_all(out, "grp", 0, 0)
    result = jax.ShapeDtypeStruct((K, size.verts), F32)
    return pl.pallas_call(
        functools.partial(order_kernel, size),
        out_shape=(result, result),
        in_specs=[vmem],
        out_specs=(vmem, vmem),
        compiler_params=params,
        name="order",
    )(out)


def solution(mesh):
    in_specs = (
        P(("dom", "grp")),
        P(("dom", "grp")),
        P(None, ("dom", "grp")),
        P(("dom", "grp")),
        P(("dom", "grp")),
    )
    out_specs = (P(None, ("dom", "grp")), P(None, ("dom", "grp")))
    return jax.shard_map(
        on_device, mesh=mesh, in_specs=in_specs, out_specs=out_specs, check_vma=False
    )
```

```python
import functools

import jax
import jax.numpy as jnp
from jax import lax
from jax.experimental import pallas as pl
from jax.experimental.pallas import tpu as pltpu
from jax.sharding import PartitionSpec as P

K = 24
HALF = 12
LANES = 128
SUB = 8
BF = jnp.bfloat16
F32 = jnp.float32


def row_of(block, r, count):
    return jnp.broadcast_to(block[r : r + 1, :], (count, LANES))


def bits_of(n):
    return (n - 1).bit_length()


class Sizes:
    def __init__(self, edev, verts, group):
        self.edev, self.verts, self.group = edev, verts, group
        self.domain = verts * group
        self.reach = self.domain // 2
        self.extent = self.domain + 2 * self.reach
        self.rows = K // group
        self.section = edev // LANES
        self.ground_rows = verts // LANES
        self.payload = -(-(5 * self.section + self.ground_rows) // SUB) * SUB
        self.regs = edev * group // (SUB * LANES)
        self.parts = self.regs * SUB // LANES
        self.strip = self.domain // 8
        self.blocks = (self.strip // LANES, self.extent // 16 // LANES + 2)
        self.most = (2 * self.blocks[0], self.blocks[1])
        self.window = self.extent // 16 + 64
        self.further = self.extent // 64
        self.batch = 16

    def padded(self, which):
        return (self.domain, self.extent)[which] // LANES + self.most[which]

    def pack(self, heads, tails, signs):
        strip = heads // self.strip
        turned = jnp.where(strip % 2 == 1, self.extent - 1 - tails, tails)
        key = strip * self.extent + turned
        key = key * self.strip + heads % self.strip
        return (key << self.rows) | signs

    def unpack(self, key):
        key = jnp.right_shift(key, self.rows)
        low, key = key & (self.strip - 1), jnp.right_shift(key, bits_of(self.strip))
        turned, strip = key & (self.extent - 1), jnp.right_shift(key, bits_of(self.extent))
        tails = jnp.where(strip & 1 == 1, self.extent - 1 - turned, turned)
        return strip * self.strip + low, tails


def flip_mask(size, level):
    low = bits_of(size.regs)
    if level >= low + 10:
        return None
    if level < low + 3:
        place = lax.broadcasted_iota(jnp.int32, (SUB, LANES), 0)
        bit = level - low
    else:
        place = lax.broadcasted_iota(jnp.int32, (SUB, LANES), 1)
        bit = level - low - 3
    return -(jnp.right_shift(place, bit) & 1)


def partner(size, j):
    low = bits_of(size.regs)
    axis, bit = (0, j - low) if j < low + 3 else (1, j - low - 3)
    place = lax.broadcasted_iota(jnp.int32, (SUB, LANES), axis)
    lower = (jnp.right_shift(place, bit) & 1) == 0
    index = jnp.bitwise_xor(place, 1 << bit)
    return axis, index, lower


def sort_edges(size, keys, weights):
    low = bits_of(size.regs)
    levels = low + 10

    def between(group, stages):
        key = {v: keys[v] for v in group}
        weight = {v: weights[v] for v in group}
        for level, j in stages:
            for v in group:
                if v >> j & 1:
                    continue
                a, b = v, v | 1 << j
                if level < low and v >> level & 1:
                    a, b = b, a
                swap = key[a] > key[b]
                key[a], key[b] = jnp.where(swap, key[b], key[a]), jnp.where(swap, key[a], key[b])
                weight[a], weight[b] = (
                    jnp.where(swap, weight[b], weight[a]),
                    jnp.where(swap, weight[a], weight[b]),
                )
        for v in group:
            keys[v] = key[v]
            weights[v] = weight[v]

    def registers(level):
        top = min(level, low)
        if top > 3:
            for v in range(8):
                between(list(range(v, size.regs, 8)), [(level, j) for j in range(top - 1, 2, -1)])
        for v in range(0, size.regs, 8):
            between(list(range(v, v + 8)), [(level, j) for j in range(min(top, 3) - 1, -1, -1)])

    for v in range(0, size.regs, 8):
        between(list(range(v, v + 8)), [(level, j) for level in (1, 2, 3) for j in range(level - 1, -1, -1)])
    for level in range(4, low):
        registers(level)

    for level in range(low, levels + 1):
        before = flip_mask(size, level - 1) if level > low else None
        now = flip_mask(size, level)
        flip = now if before is None else before if now is None else jnp.bitwise_xor(before, now)
        stages = [partner(size, j) for j in range(level - 1, low - 1, -1)]

        wide = min(32, size.regs)

        def across(i, carry, flip=flip, stages=stages):
            group = [i * wide + u for u in range(wide)]
            key = [jnp.bitwise_xor(keys[v], flip) for v in group]
            weight = [weights[v] for v in group]
            for axis, index, lower in stages:
                for u in range(wide):
                    k, w = key[u], weight[u]
                    other = jnp.take_along_axis(k, index, axis=axis, mode="promise_in_bounds")
                    other_w = jnp.take_along_axis(w, index, axis=axis, mode="promise_in_bounds")
                    best = jnp.where(lower, jnp.minimum(k, other), jnp.maximum(k, other))
                    weight[u] = jnp.where(best == k, w, other_w)
                    key[u] = best
            for u, v in enumerate(group):
                keys[v] = key[u]
                weights[v] = weight[u]
            return carry

        lax.fori_loop(0, size.regs // wide, across, 0)
        registers(level)


def sort_kernel(size, place, pay, key_out, heads_out, tails_out, weight_out, bounds, keys, weights):
    word, shift = place[0], place[1]
    per = size.section // SUB
    mask = (1 << size.rows) - 1

    def section(which, g, c):
        return pay[g, which * size.section + c * SUB : which * size.section + (c + 1) * SUB, :]

    for g in range(size.group):
        for c in range(per):
            heads = section(0, g, c).astype(jnp.int32)
            tails = section(1, g, c).astype(jnp.int32)
            signs = jnp.where(word == 0, section(2, g, c), section(3, g, c)).astype(jnp.int32)
            v = g * per + c
            keys[v] = size.pack(heads, tails, jnp.right_shift(signs, shift) & mask)
            weights[v] = section(4, g, c)
    sort_edges(size, keys, weights)
    ends = [size.unpack(keys[v]) for v in range(size.regs)]
    lane = lax.broadcasted_iota(jnp.int32, (1, LANES), 1)
    far = rare = lane < 0
    for which in range(2):
        least = functools.reduce(jnp.minimum, [end[which] for end in ends])
        most = functools.reduce(jnp.maximum, [end[which] for end in ends])
        least = jnp.min(least, axis=0, keepdims=True)
        most = jnp.max(most, axis=0, keepdims=True)
        bounds[2 * which : 2 * which + 1, :] = least
        bounds[2 * which + 1 : 2 * which + 2, :] = most
        if which == 1:
            far = far | (most - (least & -8) >= size.window)
            rare = rare | (most - (least & -8) >= size.window + size.further)
        least, most = least // LANES, most // LANES
        far = far | (most - least >= size.blocks[which])
        rare = rare | (most - least >= size.most[which])
    runs = jnp.where(far, lane, LANES)
    count = jnp.sum(far.astype(F32), axis=1, keepdims=True)
    rare = jnp.max(jnp.where(rare, 1.0, 0.0), axis=1, keepdims=True)
    rare, count = rare.astype(jnp.int32), count.astype(jnp.int32)
    for step in (1, 2, 4, 8, 16, 32, 64):
        after = jnp.where(lane + step < LANES, jnp.roll(runs, -step, axis=1), LANES)
        runs = jnp.minimum(runs, after)
    bounds[4:5, :] = runs
    bounds[5:6, :] = jnp.broadcast_to(rare, (1, LANES))
    bounds[6:7, :] = jnp.broadcast_to(count, (1, LANES))
    for j in range(size.parts):
        here = range(j * 16, (j + 1) * 16)
        key = jnp.concatenate([keys[v] for v in here], axis=0).T
        key_out[j] = key
        heads_out[j], tails_out[j] = size.unpack(key)
        weight_out[j] = jnp.concatenate([weights[v] for v in here], axis=0).T


def halves_of(value):
    high = value.astype(BF).astype(F32)
    return jnp.concatenate([high, value - high], axis=0).astype(BF)


def row(ref, j, run, count):
    return jnp.broadcast_to(ref[j, pl.ds(run, 1), :], (count, LANES))


def next_far(bounds, run):
    following = bounds[4, jnp.minimum(run + 1, LANES - 1)]
    return jnp.where(run + 1 < LANES, following, LANES)


def one_hot(size, index, run, start, window):
    iota = lax.broadcasted_iota(jnp.int32, (16, LANES), 0)
    rows = [(iota + 16 * m).astype(F32).astype(BF) for m in range(16)]
    zero, one = jnp.zeros((16, LANES), BF), jnp.ones((16, LANES), BF)
    hot = []
    for j in range(size.parts):
        column = []
        for at in range(0, window, 256):
            local = (row(index, j, run, 16) - (start + at)).astype(F32).astype(BF)
            count = min(256, window - at) // 16
            column += [jnp.where(local == rows[m], one, zero) for m in range(count)]
        hot.append(jnp.concatenate(column, axis=0))
    return jnp.concatenate(hot, axis=1)


def times(left, right):
    return lax.dot_general(left, right, (((1,), (1,)), ((), ())), preferred_element_type=F32)


def add_blocks(size, heads, run, first, begin, end, pair, acc, valid=True):
    start = (first + begin) * LANES
    if valid is not True:
        start = jnp.where(valid, start, -(1 << 20))
    got = times(pair, one_hot(size, heads, run, start, (end - begin) * LANES))
    for b in range(end - begin):
        acc[first + begin + b] += got[:, b * LANES : (b + 1) * LANES]


def add_rows(size, tails, run, start, window, pair, acc, valid=True):
    start = pl.multiple_of(start, SUB)
    from_ = start if valid is True else jnp.where(valid, start, -(1 << 20))
    acc[pl.ds(start, window), 0:16] += times(one_hot(size, tails, run, from_, window), pair)


def first_block(bounds, which, run):
    return bounds[2 * which, run] // LANES


def last_block(bounds, which, run):
    return bounds[2 * which + 1, run] // LANES


def first_row(bounds, run):
    return bounds[2, run] & -8


def sweep(size, bounds, ends, make, make_far, accs, bufs):
    def fill(buf, base):
        for q in range(size.batch):
            for which, pair in enumerate(make(base + q)):
                buf[which, q] = pair

    heads, tails = ends
    acc_h, acc_t = accs

    def use(buf, base):
        for q in range(size.batch):
            run = base + q
            add_blocks(size, heads, run, first_block(bounds, 0, run), 0, size.blocks[0], buf[0, q], acc_h)
            add_rows(size, tails, run, first_row(bounds, run), size.window, buf[1, q], acc_t)

    fill(bufs[0], 0)

    def step(i, carry):
        base = i * 2 * size.batch
        use(bufs[0], base)
        fill(bufs[1], base + size.batch)
        use(bufs[1], base + size.batch)
        fill(bufs[0], (base + 2 * size.batch) % LANES)
        return carry

    lax.fori_loop(0, LANES // (2 * size.batch), step, 0)

    @pl.when(bounds[5, 0] == 0)
    def _():
        def four(i, run):
            for _ in range(4):
                valid, here = run < LANES, jnp.minimum(run, LANES - 1)
                full, beyond = make_far(here, False)
                first = first_block(bounds, 0, here)
                add_blocks(size, heads, here, first, size.blocks[0], size.most[0], full[0], acc_h, valid)
                start = first_row(bounds, here)
                add_rows(size, tails, here, start + size.window, size.further, full[1], acc_t, valid)
                if beyond is not None:
                    add_rows(size, tails, here, start, size.window, beyond[1], acc_t, valid)
                run = jnp.where(valid, next_far(bounds, here), LANES)
            return run

        lax.fori_loop(0, (bounds[6, 0] + 3) // 4, four, bounds[4, 0])

    @pl.when(bounds[5, 0] != 0)
    def _():
        def more(run):
            full, beyond = make_far(run, True)
            first, start = first_block(bounds, 0, run), first_row(bounds, run)

            def block(a, carry):
                add_blocks(size, heads, run, a, 0, 1, full[0], acc_h)
                return carry

            def window(m, carry):
                add_rows(size, tails, run, start + m * size.window, size.window, full[1], acc_t)
                return carry

            lax.fori_loop(first + size.blocks[0], last_block(bounds, 0, run) + 1, block, 0)
            lax.fori_loop(1, (bounds[3, run] - start) // size.window + 1, window, 0)
            if beyond is not None:
                add_blocks(size, heads, run, first, 0, size.blocks[0], beyond[0], acc_h)
                add_rows(size, tails, run, start, size.window, beyond[1], acc_t)
            return next_far(bounds, run)

        lax.while_loop(lambda run: run < LANES, more, bounds[4, 0])


def collect(size, acc_h, acc_t, out_l, out_r):
    shift = size.reach // LANES
    half = size.domain // LANES
    for a in range(size.extent // LANES):
        value = acc_t[a * LANES : (a + 1) * LANES, :].T
        value = value[0:8, :] + value[8:16, :]
        h = a - shift
        if 0 <= h < half:
            value += acc_h[h, 0:8] + acc_h[h, 8:16]
        out, at = (out_l, a) if a < half else (out_r, a - half)
        out[:, at * LANES : (at + 1) * LANES] = value


def clear(acc_h, acc_t):
    acc_h[...] = jnp.zeros_like(acc_h)
    acc_t[...] = jnp.zeros_like(acc_t)


def sketch_kernel(size, bounds, keys, heads, tails, weights, pay, out_l, out_r, acc_h, acc_t, buf_a, buf_b, tables):
    sub = lax.broadcasted_iota(jnp.int32, (SUB, LANES), 0)
    is_sign = sub < size.rows
    clear(acc_h, acc_t)

    def make(run):
        pairs = [[], []]
        for j in range(size.parts):
            weight = row(weights, j, run, SUB)
            bit = jnp.right_shift(row(keys, j, run, SUB), sub) & 1
            signed = (2 * bit - 1).astype(F32) * jnp.sqrt(weight)
            last = jnp.where(sub == size.rows, weight, 0.0)
            pairs[0].append(halves_of(jnp.where(is_sign, signed, last)))
            pairs[1].append(halves_of(jnp.where(is_sign, -signed, last)))
        return [jnp.concatenate(pair, axis=1) for pair in pairs]

    sweep(size, bounds, (heads, tails), make, lambda run, every: (make(run), None), (acc_h, acc_t), (buf_a, buf_b))
    collect(size, acc_h, acc_t, out_l, out_r)
    for g in range(size.group):
        for r in range(size.ground_rows):
            at = size.reach + g * size.verts + r * LANES
            out, at = (out_l, at) if at < size.domain else (out_r, at - size.domain)
            line = 5 * size.section + r
            value = jnp.broadcast_to(pay[g, line : line + 1, :], (SUB, LANES))
            out[:, at : at + LANES] += jnp.where(sub == size.rows, value, 0.0)


def operator_core(size, bounds, heads, tails, weights, table, out_l, out_r, bufs):
    acc_h, acc_t, buf_a, buf_b, tables = bufs
    clear(acc_h, acc_t)
    for a in range(size.extent // LANES):
        tables[a] = table[:, a * LANES : (a + 1) * LANES]
    ends = (heads, tails)

    def take(which, low, high, a, out):
        shift = size.reach // LANES if which == 0 else 0
        got = jnp.take_along_axis(tables[shift + a], low, axis=1, mode="promise_in_bounds")
        return jnp.where(high == a, got, out)

    nothing = jnp.zeros((SUB, LANES), F32)

    def gathered(run, blocks):
        pairs = [[], []]
        for j in range(size.parts):
            weight = row(weights, j, run, SUB)
            for which in range(2):
                index = row(ends[which], j, run, SUB)
                first, (begin, end) = first_block(bounds, which, run), blocks[which]
                low, high = index % LANES, index // LANES
                if end is None:
                    out = lax.fori_loop(
                        first + begin, last_block(bounds, which, run) + 1,
                        lambda a, out: take(which, low, high, a, out), nothing,
                    )
                else:
                    out = nothing
                    for a in range(begin, end):
                        out = take(which, low, high, first + a, out)
                pairs[1 - which].append(halves_of(out * weight))
        return [jnp.concatenate(pair, axis=1) for pair in pairs]

    def make(run):
        return gathered(run, [(0, size.blocks[which]) for which in range(2)])

    def make_far(run, every):
        ends_at = [None, None] if every else size.most
        return (
            gathered(run, [(0, ends_at[which]) for which in range(2)]),
            gathered(run, [(size.blocks[which], ends_at[which]) for which in range(2)]),
        )

    sweep(size, bounds, ends, make, make_far, (acc_h, acc_t), (buf_a, buf_b))
    collect(size, acc_h, acc_t, out_l, out_r)


def halves(size, own_l, own_r, got_l, got_r):
    return ((0, own_l, got_l), (size.domain, own_r, got_r))


def first_kernel(size, bounds, heads, tails, weights, own_l, own_r, got_l, got_r, out_l, out_r, v, diag, *bufs):
    sub = lax.broadcasted_iota(jnp.int32, (SUB, size.domain), 0)
    for at, own, got in halves(size, own_l, own_r, got_l, got_r):
        total = own[...] + got[...]
        spread = jnp.broadcast_to(total[size.rows : size.rows + 1, :], total.shape)
        safe = jnp.where(spread > 0.0, spread, 1.0)
        diag[:, at : at + size.domain] = safe
        v[:, at : at + size.domain] = jnp.where(sub < size.rows, total / safe, 0.0)
    operator_core(size, bounds, heads, tails, weights, v, out_l, out_r, bufs)


def next_v(size, own_l, own_r, got_l, got_r, diag, v):
    for at, own, got in halves(size, own_l, own_r, got_l, got_r):
        v[:, at : at + size.domain] = (own[...] + got[...]) / diag[:, at : at + size.domain]


def second_kernel(size, bounds, heads, tails, weights, own_l, own_r, got_l, got_r, diag, out_l, out_r, v, *bufs):
    next_v(size, own_l, own_r, got_l, got_r, diag, v)
    operator_core(size, bounds, heads, tails, weights, v, out_l, out_r, bufs)


def third_kernel(size, bounds, heads, tails, weights, own_l, own_r, got_l, got_r, diag, v0, v1, out_l, out_r, v2, moments, *bufs):
    next_v(size, own_l, own_r, got_l, got_r, diag, v2)
    operator_core(size, bounds, heads, tails, weights, v2, out_l, out_r, bufs)
    lane = lax.broadcasted_iota(jnp.int32, (SUB, LANES), 1)
    middle = slice(size.reach, size.reach + size.domain)
    weighted = diag[:, middle] * v0[:, middle]
    other = diag[:, middle] * v1[:, middle]
    sums = [
        weighted * v0[:, middle],
        weighted * v1[:, middle],
        other * v1[:, middle],
        other * v2[:, middle],
        diag[:, middle] * v2[:, middle] * v2[:, middle],
        v2[:, : size.domain] * out_l[...] + v2[:, size.domain :] * out_r[...],
    ]
    out = jnp.zeros((SUB, LANES), F32)
    for k, value in enumerate(sums):
        out = jnp.where(lane == k, jnp.sum(value, axis=1, keepdims=True), out)
    for d in range(moments.shape[0]):
        moments[d] = out


def coefficients(mu):
    zero = jnp.zeros_like(mu[0])

    def inner(a, b):
        total = None
        for i, x in enumerate(a):
            for j, y in enumerate(b):
                term = mu[i + j] if x is None and y is None else mu[i + j] * (y if x is None else x if y is None else x * y)
                total = term if total is None else total + term
        return total

    def image(a):
        a = [jnp.ones_like(zero) if x is None else x for x in a] + [zero]
        return [a[0]] + [a[i] - a[i - 1] for i in range(1, len(a))]

    def ratio(top, bottom):
        return jnp.where(bottom > 0.0, top / jnp.where(bottom > 0.0, bottom, 1.0), 0.0)

    rho, pi, x = [jnp.ones_like(zero)], [jnp.ones_like(zero)], []
    gamma = inner(rho, rho)
    for step in range(3):
        moved = image(pi)
        alpha = ratio(gamma, inner(pi, moved))
        x = [(x[i] if i < len(x) else zero) + alpha * pi[i] for i in range(len(pi))]
        rho = [(rho[i] if i < len(rho) else zero) - alpha * moved[i] for i in range(len(moved))]
        if step < 2:
            following = inner(rho, rho)
            beta = ratio(following, gamma)
            pi = [rho[i] + (beta * pi[i] if i < len(pi) else zero) for i in range(len(rho))]
            gamma = following
    return x, rho


def last_kernel(size, moments, own_l, own_r, got_l, got_r, diag, v0, v1, v2, out):
    total = moments[0]
    for d in range(1, moments.shape[0]):
        total = total + moments[d]
    mu = [jnp.broadcast_to(total[:, k : k + 1], (SUB, LANES)) for k in range(6)]
    x, rho = coefficients(mu)
    x = [value[:, :1] for value in x]
    rho = [value[:, :1] for value in rho]
    for g in range(size.group):
        at = size.reach + g * size.verts
        here = slice(at, at + size.verts)
        if at < size.domain:
            sums = own_l[:, here] + got_l[:, g * size.verts : (g + 1) * size.verts]
        else:
            back = at - size.domain
            inside = slice(back, back + size.verts)
            sums = own_r[:, inside] + got_r[:, inside]
        a, b, c, scale = v0[:, here], v1[:, here], v2[:, here], diag[:, here]
        out[g, 0] = x[0] * a + x[1] * b + x[2] * c
        out[g, 1] = scale * (rho[0] * a + rho[1] * b + rho[2] * c) + rho[3] * sums


def order_kernel(size, parts, x, r):
    for g in range(size.group):
        here = slice(g * size.rows, (g + 1) * size.rows)
        x[here, :] = parts[g, 0, : size.rows]
        r[here, :] = parts[g, 1, : size.rows]


def on_device(heads, tails, signs, edge_weights, ground):
    group = lax.axis_size("grp")
    count = lax.axis_size("dom")
    size = Sizes(heads.shape[0], ground.shape[0], group)
    vmem = pl.BlockSpec(memory_space=pltpu.VMEM)
    smem = pl.BlockSpec(memory_space=pltpu.SMEM)
    params = pltpu.CompilerParams(vmem_limit_bytes=48 * 1024 * 1024)

    def flat(value):
        return value.astype(F32).reshape(-1, LANES)

    parts = [flat(heads), flat(tails), flat(signs[0]), flat(signs[1]), flat(edge_weights), flat(ground)]
    used = sum(part.shape[0] for part in parts)
    parts.append(jnp.zeros((size.payload - used, LANES), F32))
    pay = lax.all_gather(jnp.concatenate(parts, axis=0), "grp")

    half = jax.ShapeDtypeStruct((SUB, size.domain), F32)
    full = jax.ShapeDtypeStruct((SUB, size.extent), F32)

    def exchange(left, right):
        up = [(i, i + 1) for i in range(count - 1)]
        down = [(i + 1, i) for i in range(count - 1)]
        return lax.ppermute(right, "dom", up), lax.ppermute(left, "dom", down)

    me = lax.axis_index("grp")
    first_row = me * size.rows
    place = jnp.stack([first_row // HALF, first_row % HALF]).astype(jnp.int32)
    spread = (size.parts, LANES, LANES)
    keys, heads, tails, weights, bounds = pl.pallas_call(
        functools.partial(sort_kernel, size),
        out_shape=(
            jax.ShapeDtypeStruct(spread, jnp.int32),
            jax.ShapeDtypeStruct(spread, jnp.int32),
            jax.ShapeDtypeStruct(spread, jnp.int32),
            jax.ShapeDtypeStruct(spread, F32),
            jax.ShapeDtypeStruct((SUB, LANES), jnp.int32),
        ),
        in_specs=[smem, vmem],
        out_specs=(vmem,) * 5,
        scratch_shapes=[
            pltpu.VMEM((size.regs, SUB, LANES), jnp.int32),
            pltpu.VMEM((size.regs, SUB, LANES), F32),
        ],
        compiler_params=params,
        name="sort_edges",
    )(place, pay)
    edges = (bounds, heads, tails, weights)
    edge_specs = [smem, vmem, vmem, vmem]
    scratch = [
        pltpu.VMEM((size.padded(0), 16, LANES), F32),
        pltpu.VMEM((size.extent + size.window + size.further, LANES), F32),
        pltpu.VMEM((2, size.batch, 16, size.parts * LANES), BF),
        pltpu.VMEM((2, size.batch, 16, size.parts * LANES), BF),
        pltpu.VMEM((size.padded(1) + size.most[0], SUB, LANES), F32),
    ]
    acc = pl.pallas_call(
        functools.partial(sketch_kernel, size),
        out_shape=(half, half),
        in_specs=edge_specs + [vmem] * 2,
        out_specs=(vmem, vmem),
        scratch_shapes=scratch,
        compiler_params=params,
        name="sketch",
    )(bounds, keys, heads, tails, weights, pay)
    got = exchange(*acc)
    *acc, v0, diag = pl.pallas_call(
        functools.partial(first_kernel, size),
        out_shape=(half, half, full, full),
        in_specs=edge_specs + [vmem] * 4,
        out_specs=(vmem,) * 4,
        scratch_shapes=scratch,
        compiler_params=params,
        name="operator_first",
    )(*edges, *acc, *got)
    got = exchange(*acc)
    *acc, v1 = pl.pallas_call(
        functools.partial(second_kernel, size),
        out_shape=(half, half, full),
        in_specs=edge_specs + [vmem] * 5,
        out_specs=(vmem,) * 3,
        scratch_shapes=scratch,
        compiler_params=params,
        name="operator_second",
    )(*edges, *acc, *got, diag)
    got = exchange(*acc)
    *acc, v2, moments = pl.pallas_call(
        functools.partial(third_kernel, size),
        out_shape=(half, half, full, jax.ShapeDtypeStruct((count, SUB, LANES), F32)),
        in_specs=edge_specs + [vmem] * 7,
        out_specs=(vmem,) * 4,
        scratch_shapes=scratch,
        compiler_params=params,
        name="operator_third",
    )(*edges, *acc, *got, diag, v0, v1)
    up = [(i, i + 1) for i in range(count - 1)]
    down = [(i + 1, i) for i in range(count - 1)]
    got_l = lax.ppermute(acc[1][:, size.reach :], "dom", up)
    got_r = lax.ppermute(acc[0][:, : size.reach], "dom", down)
    shared = lax.all_to_all(moments, "dom", 0, 0)
    out = pl.pallas_call(
        functools.partial(last_kernel, size),
        out_shape=jax.ShapeDtypeStruct((group, 2, SUB, size.verts), F32),
        in_specs=[vmem] * 9,
        out_specs=vmem,
        compiler_params=params,
        name="combine",
    )(shared, *acc, got_l, got_r, diag, v0, v1, v2)
    out = lax.all_to_all(out, "grp", 0, 0)
    result = jax.ShapeDtypeStruct((K, size.verts), F32)
    return pl.pallas_call(
        functools.partial(order_kernel, size),
        out_shape=(result, result),
        in_specs=[vmem],
        out_specs=(vmem, vmem),
        compiler_params=params,
        name="order",
    )(out)


def solution(mesh):
    in_specs = (
        P(("dom", "grp")),
        P(("dom", "grp")),
        P(None, ("dom", "grp")),
        P(("dom", "grp")),
        P(("dom", "grp")),
    )
    out_specs = (P(None, ("dom", "grp")), P(None, ("dom", "grp")))
    return jax.shard_map(
        on_device, mesh=mesh, in_specs=in_specs, out_specs=out_specs, check_vma=False
    )
```

```python
import functools

import jax
import jax.numpy as jnp
from jax import lax
from jax.experimental import pallas as pl
from jax.experimental.pallas import tpu as pltpu
from jax.sharding import PartitionSpec as P

K = 24
HALF = 12
LANES = 128
SUB = 8
BF = jnp.bfloat16
F32 = jnp.float32


def row_of(block, r, count):
    return jnp.broadcast_to(block[r : r + 1, :], (count, LANES))


def bits_of(n):
    return (n - 1).bit_length()


class Sizes:
    def __init__(self, edev, verts, group):
        self.edev, self.verts, self.group = edev, verts, group
        self.domain = verts * group
        self.reach = self.domain // 2
        self.extent = self.domain + 2 * self.reach
        self.rows = K // group
        self.section = edev // LANES
        self.ground_rows = verts // LANES
        self.payload = -(-(5 * self.section + self.ground_rows) // SUB) * SUB
        self.regs = edev * group // (SUB * LANES)
        self.parts = self.regs * SUB // LANES
        self.strip = self.domain // 8
        self.blocks = (self.strip // LANES, self.extent // 16 // LANES + 2)
        self.most = (2 * self.blocks[0], self.blocks[1])
        self.window = self.extent // 16 + 64
        self.further = self.extent // 64
        self.batch = 16

    def padded(self, which):
        return (self.domain, self.extent)[which] // LANES + self.most[which]

    def pack(self, heads, tails, signs):
        strip = heads // self.strip
        turned = jnp.where(strip % 2 == 1, self.extent - 1 - tails, tails)
        key = strip * self.extent + turned
        key = key * self.strip + heads % self.strip
        return (key << self.rows) | signs

    def unpack(self, key):
        key = jnp.right_shift(key, self.rows)
        low, key = key & (self.strip - 1), jnp.right_shift(key, bits_of(self.strip))
        turned, strip = key & (self.extent - 1), jnp.right_shift(key, bits_of(self.extent))
        tails = jnp.where(strip & 1 == 1, self.extent - 1 - turned, turned)
        return strip * self.strip + low, tails


def flip_mask(size, level):
    low = bits_of(size.regs)
    if level >= low + 10:
        return None
    if level < low + 3:
        place = lax.broadcasted_iota(jnp.int32, (SUB, LANES), 0)
        bit = level - low
    else:
        place = lax.broadcasted_iota(jnp.int32, (SUB, LANES), 1)
        bit = level - low - 3
    return -(jnp.right_shift(place, bit) & 1)


def partner(size, j):
    low = bits_of(size.regs)
    axis, bit = (0, j - low) if j < low + 3 else (1, j - low - 3)
    place = lax.broadcasted_iota(jnp.int32, (SUB, LANES), axis)
    lower = (jnp.right_shift(place, bit) & 1) == 0
    index = jnp.bitwise_xor(place, 1 << bit)
    return axis, index, lower


def sort_edges(size, keys, weights):
    low = bits_of(size.regs)
    levels = low + 10

    def between(group, stages):
        key = {v: keys[v] for v in group}
        weight = {v: weights[v] for v in group}
        for level, j in stages:
            for v in group:
                if v >> j & 1:
                    continue
                a, b = v, v | 1 << j
                if level < low and v >> level & 1:
                    a, b = b, a
                swap = key[a] > key[b]
                key[a], key[b] = jnp.where(swap, key[b], key[a]), jnp.where(swap, key[a], key[b])
                weight[a], weight[b] = (
                    jnp.where(swap, weight[b], weight[a]),
                    jnp.where(swap, weight[a], weight[b]),
                )
        for v in group:
            keys[v] = key[v]
            weights[v] = weight[v]

    def registers(level):
        top = min(level, low)
        if top > 3:
            for v in range(8):
                between(list(range(v, size.regs, 8)), [(level, j) for j in range(top - 1, 2, -1)])
        for v in range(0, size.regs, 8):
            between(list(range(v, v + 8)), [(level, j) for j in range(min(top, 3) - 1, -1, -1)])

    for v in range(0, size.regs, 8):
        between(list(range(v, v + 8)), [(level, j) for level in (1, 2, 3) for j in range(level - 1, -1, -1)])
    for level in range(4, low):
        registers(level)

    for level in range(low, levels + 1):
        before = flip_mask(size, level - 1) if level > low else None
        now = flip_mask(size, level)
        flip = now if before is None else before if now is None else jnp.bitwise_xor(before, now)
        stages = [partner(size, j) for j in range(level - 1, low - 1, -1)]

        wide = min(32, size.regs)

        def across(i, carry, flip=flip, stages=stages):
            group = [i * wide + u for u in range(wide)]
            key = [jnp.bitwise_xor(keys[v], flip) for v in group]
            weight = [weights[v] for v in group]
            for axis, index, lower in stages:
                for u in range(wide):
                    k, w = key[u], weight[u]
                    other = jnp.take_along_axis(k, index, axis=axis, mode="promise_in_bounds")
                    other_w = jnp.take_along_axis(w, index, axis=axis, mode="promise_in_bounds")
                    best = jnp.where(lower, jnp.minimum(k, other), jnp.maximum(k, other))
                    weight[u] = jnp.where(best == k, w, other_w)
                    key[u] = best
            for u, v in enumerate(group):
                keys[v] = key[u]
                weights[v] = weight[u]
            return carry

        lax.fori_loop(0, size.regs // wide, across, 0)
        registers(level)


def sort_kernel(size, place, pay, key_out, heads_out, tails_out, weight_out, bounds, keys, weights):
    word, shift = place[0], place[1]
    per = size.section // SUB
    mask = (1 << size.rows) - 1

    def section(which, g, c):
        return pay[g, which * size.section + c * SUB : which * size.section + (c + 1) * SUB, :]

    for g in range(size.group):
        for c in range(per):
            heads = section(0, g, c).astype(jnp.int32)
            tails = section(1, g, c).astype(jnp.int32)
            signs = jnp.where(word == 0, section(2, g, c), section(3, g, c)).astype(jnp.int32)
            v = g * per + c
            keys[v] = size.pack(heads, tails, jnp.right_shift(signs, shift) & mask)
            weights[v] = section(4, g, c)
    sort_edges(size, keys, weights)
    ends = [size.unpack(keys[v]) for v in range(size.regs)]
    lane = lax.broadcasted_iota(jnp.int32, (1, LANES), 1)
    far = rare = lane < 0
    for which in range(2):
        least = functools.reduce(jnp.minimum, [end[which] for end in ends])
        most = functools.reduce(jnp.maximum, [end[which] for end in ends])
        least = jnp.min(least, axis=0, keepdims=True)
        most = jnp.max(most, axis=0, keepdims=True)
        bounds[2 * which : 2 * which + 1, :] = least
        bounds[2 * which + 1 : 2 * which + 2, :] = most
        if which == 1:
            far = far | (most - (least & -8) >= size.window)
            rare = rare | (most - (least & -8) >= size.window + size.further)
        least, most = least // LANES, most // LANES
        far = far | (most - least >= size.blocks[which])
        rare = rare | (most - least >= size.most[which])
    runs = jnp.where(far, lane, LANES)
    count = jnp.sum(far.astype(F32), axis=1, keepdims=True)
    rare = jnp.max(jnp.where(rare, 1.0, 0.0), axis=1, keepdims=True)
    rare, count = rare.astype(jnp.int32), count.astype(jnp.int32)
    for step in (1, 2, 4, 8, 16, 32, 64):
        after = jnp.where(lane + step < LANES, jnp.roll(runs, -step, axis=1), LANES)
        runs = jnp.minimum(runs, after)
    bounds[4:5, :] = runs
    bounds[5:6, :] = jnp.broadcast_to(rare, (1, LANES))
    bounds[6:7, :] = jnp.broadcast_to(count, (1, LANES))
    for j in range(size.parts):
        here = range(j * 16, (j + 1) * 16)
        key = jnp.concatenate([keys[v] for v in here], axis=0).T
        key_out[j] = key
        heads_out[j], tails_out[j] = size.unpack(key)
        weight_out[j] = jnp.concatenate([weights[v] for v in here], axis=0).T


def halves_of(value):
    high = value.astype(BF).astype(F32)
    return jnp.concatenate([high, value - high], axis=0).astype(BF)


def row(ref, j, run, count):
    return jnp.broadcast_to(ref[j, pl.ds(run, 1), :], (count, LANES))


def next_far(bounds, run):
    following = bounds[4, jnp.minimum(run + 1, LANES - 1)]
    return jnp.where(run + 1 < LANES, following, LANES)


def one_hot(size, index, run, start, window):
    iota = lax.broadcasted_iota(jnp.int32, (16, LANES), 0)
    rows = [(iota + 16 * m).astype(F32).astype(BF) for m in range(16)]
    zero, one = jnp.zeros((16, LANES), BF), jnp.ones((16, LANES), BF)
    hot = []
    for j in range(size.parts):
        column = []
        for at in range(0, window, 256):
            local = (row(index, j, run, 16) - (start + at)).astype(F32).astype(BF)
            count = min(256, window - at) // 16
            column += [jnp.where(local == rows[m], one, zero) for m in range(count)]
        hot.append(jnp.concatenate(column, axis=0))
    return jnp.concatenate(hot, axis=1)


def times(left, right):
    return lax.dot_general(left, right, (((1,), (1,)), ((), ())), preferred_element_type=F32)


def add_blocks(size, heads, run, first, begin, end, pair, acc, valid=True):
    start = (first + begin) * LANES
    if valid is not True:
        start = jnp.where(valid, start, -(1 << 20))
    got = times(pair, one_hot(size, heads, run, start, (end - begin) * LANES))
    for b in range(end - begin):
        acc[first + begin + b] += got[:, b * LANES : (b + 1) * LANES]


def add_rows(size, tails, run, start, window, pair, acc, valid=True):
    start = pl.multiple_of(start, SUB)
    from_ = start if valid is True else jnp.where(valid, start, -(1 << 20))
    acc[pl.ds(start, window), 0:16] += times(one_hot(size, tails, run, from_, window), pair)


def first_block(bounds, which, run):
    return bounds[2 * which, run] // LANES


def last_block(bounds, which, run):
    return bounds[2 * which + 1, run] // LANES


def first_row(bounds, run):
    return bounds[2, run] & -8


def sweep(size, bounds, ends, make, make_far, accs, bufs):
    def fill(buf, base):
        for q in range(size.batch):
            for which, pair in enumerate(make(base + q)):
                buf[which, q] = pair

    heads, tails = ends
    acc_h, acc_t = accs

    def use(buf, base):
        for q in range(size.batch):
            run = base + q
            add_blocks(size, heads, run, first_block(bounds, 0, run), 0, size.blocks[0], buf[0, q], acc_h)
            add_rows(size, tails, run, first_row(bounds, run), size.window, buf[1, q], acc_t)

    fill(bufs[0], 0)

    def step(i, carry):
        base = i * 2 * size.batch
        use(bufs[0], base)
        fill(bufs[1], base + size.batch)
        use(bufs[1], base + size.batch)
        fill(bufs[0], (base + 2 * size.batch) % LANES)
        return carry

    lax.fori_loop(0, LANES // (2 * size.batch), step, 0)

    @pl.when(bounds[5, 0] == 0)
    def _():
        def four(i, run):
            for _ in range(4):
                valid, here = run < LANES, jnp.minimum(run, LANES - 1)
                full, beyond = make_far(here, False)
                first = first_block(bounds, 0, here)
                add_blocks(size, heads, here, first, size.blocks[0], size.most[0], full[0], acc_h, valid)
                start = first_row(bounds, here)
                add_rows(size, tails, here, start + size.window, size.further, full[1], acc_t, valid)
                if beyond is not None:
                    add_rows(size, tails, here, start, size.window, beyond[1], acc_t, valid)
                run = jnp.where(valid, next_far(bounds, here), LANES)
            return run

        lax.fori_loop(0, (bounds[6, 0] + 3) // 4, four, bounds[4, 0])

    @pl.when(bounds[5, 0] != 0)
    def _():
        def more(run):
            full, beyond = make_far(run, True)
            first, start = first_block(bounds, 0, run), first_row(bounds, run)

            def block(a, carry):
                add_blocks(size, heads, run, a, 0, 1, full[0], acc_h)
                return carry

            def window(m, carry):
                add_rows(size, tails, run, start + m * size.window, size.window, full[1], acc_t)
                return carry

            lax.fori_loop(first + size.blocks[0], last_block(bounds, 0, run) + 1, block, 0)
            lax.fori_loop(1, (bounds[3, run] - start) // size.window + 1, window, 0)
            if beyond is not None:
                add_blocks(size, heads, run, first, 0, size.blocks[0], beyond[0], acc_h)
                add_rows(size, tails, run, start, size.window, beyond[1], acc_t)
            return next_far(bounds, run)

        lax.while_loop(lambda run: run < LANES, more, bounds[4, 0])


def collect(size, acc_h, acc_t, out_l, out_r):
    shift = size.reach // LANES
    half = size.domain // LANES
    for a in range(size.extent // LANES):
        value = acc_t[a * LANES : (a + 1) * LANES, :].T
        value = value[0:8, :] + value[8:16, :]
        h = a - shift
        if 0 <= h < half:
            value += acc_h[h, 0:8] + acc_h[h, 8:16]
        out, at = (out_l, a) if a < half else (out_r, a - half)
        out[:, at * LANES : (at + 1) * LANES] = value


def clear(acc_h, acc_t):
    acc_h[...] = jnp.zeros_like(acc_h)
    acc_t[...] = jnp.zeros_like(acc_t)


def sketch_kernel(size, bounds, keys, heads, tails, weights, pay, out_l, out_r, acc_h, acc_t, buf_a, buf_b, tables):
    sub = lax.broadcasted_iota(jnp.int32, (SUB, LANES), 0)
    is_sign = sub < size.rows
    clear(acc_h, acc_t)

    def make(run):
        pairs = [[], []]
        for j in range(size.parts):
            weight = row(weights, j, run, SUB)
            bit = jnp.right_shift(row(keys, j, run, SUB), sub) & 1
            signed = (2 * bit - 1).astype(F32) * jnp.sqrt(weight)
            last = jnp.where(sub == size.rows, weight, 0.0)
            pairs[0].append(halves_of(jnp.where(is_sign, signed, last)))
            pairs[1].append(halves_of(jnp.where(is_sign, -signed, last)))
        return [jnp.concatenate(pair, axis=1) for pair in pairs]

    sweep(size, bounds, (heads, tails), make, lambda run, every: (make(run), None), (acc_h, acc_t), (buf_a, buf_b))
    collect(size, acc_h, acc_t, out_l, out_r)
    for g in range(size.group):
        for r in range(size.ground_rows):
            at = size.reach + g * size.verts + r * LANES
            out, at = (out_l, at) if at < size.domain else (out_r, at - size.domain)
            line = 5 * size.section + r
            value = jnp.broadcast_to(pay[g, line : line + 1, :], (SUB, LANES))
            out[:, at : at + LANES] += jnp.where(sub == size.rows, value, 0.0)


def operator_core(size, bounds, heads, tails, weights, table, out_l, out_r, bufs):
    acc_h, acc_t, buf_a, buf_b, tables = bufs
    clear(acc_h, acc_t)
    for a in range(size.extent // LANES):
        tables[a] = table[:, a * LANES : (a + 1) * LANES]
    ends = (heads, tails)

    def take(which, low, high, a, out):
        shift = size.reach // LANES if which == 0 else 0
        got = jnp.take_along_axis(tables[shift + a], low, axis=1, mode="promise_in_bounds")
        return jnp.where(high == a, got, out)

    nothing = jnp.zeros((SUB, LANES), F32)

    def gathered(run, blocks):
        pairs = [[], []]
        for j in range(size.parts):
            weight = row(weights, j, run, SUB)
            for which in range(2):
                index = row(ends[which], j, run, SUB)
                first, (begin, end) = first_block(bounds, which, run), blocks[which]
                low, high = index % LANES, index // LANES
                if end is None:
                    out = lax.fori_loop(
                        first + begin, last_block(bounds, which, run) + 1,
                        lambda a, out: take(which, low, high, a, out), nothing,
                    )
                else:
                    out = nothing
                    for a in range(begin, end):
                        out = take(which, low, high, first + a, out)
                pairs[1 - which].append(halves_of(out * weight))
        return [jnp.concatenate(pair, axis=1) for pair in pairs]

    def make(run):
        return gathered(run, [(0, size.blocks[which]) for which in range(2)])

    def make_far(run, every):
        ends_at = [None, None] if every else size.most
        return (
            gathered(run, [(0, ends_at[which]) for which in range(2)]),
            gathered(run, [(size.blocks[which], ends_at[which]) for which in range(2)]),
        )

    sweep(size, bounds, ends, make, make_far, (acc_h, acc_t), (buf_a, buf_b))
    collect(size, acc_h, acc_t, out_l, out_r)


def halves(size, own_l, own_r, got_l, got_r):
    return ((0, own_l, got_l), (size.domain, own_r, got_r))


def first_kernel(size, bounds, heads, tails, weights, own_l, own_r, got_l, got_r, out_l, out_r, v, diag, *bufs):
    sub = lax.broadcasted_iota(jnp.int32, (SUB, size.domain), 0)
    for at, own, got in halves(size, own_l, own_r, got_l, got_r):
        total = own[...] + got[...]
        spread = jnp.broadcast_to(total[size.rows : size.rows + 1, :], total.shape)
        safe = jnp.where(spread > 0.0, spread, 1.0)
        diag[:, at : at + size.domain] = safe
        v[:, at : at + size.domain] = jnp.where(sub < size.rows, total / safe, 0.0)
    operator_core(size, bounds, heads, tails, weights, v, out_l, out_r, bufs)


def next_v(size, own_l, own_r, got_l, got_r, diag, v):
    for at, own, got in halves(size, own_l, own_r, got_l, got_r):
        v[:, at : at + size.domain] = (own[...] + got[...]) / diag[:, at : at + size.domain]


def second_kernel(size, bounds, heads, tails, weights, own_l, own_r, got_l, got_r, diag, out_l, out_r, v, *bufs):
    next_v(size, own_l, own_r, got_l, got_r, diag, v)
    operator_core(size, bounds, heads, tails, weights, v, out_l, out_r, bufs)


def third_kernel(size, bounds, heads, tails, weights, own_l, own_r, got_l, got_r, diag, v0, v1, out_l, out_r, v2, moments, *bufs):
    next_v(size, own_l, own_r, got_l, got_r, diag, v2)
    operator_core(size, bounds, heads, tails, weights, v2, out_l, out_r, bufs)
    lane = lax.broadcasted_iota(jnp.int32, (SUB, LANES), 1)
    middle = slice(size.reach, size.reach + size.domain)
    weighted = diag[:, middle] * v0[:, middle]
    other = diag[:, middle] * v1[:, middle]
    sums = [
        weighted * v0[:, middle],
        weighted * v1[:, middle],
        other * v1[:, middle],
        other * v2[:, middle],
        diag[:, middle] * v2[:, middle] * v2[:, middle],
        v2[:, : size.domain] * out_l[...] + v2[:, size.domain :] * out_r[...],
    ]
    out = jnp.zeros((SUB, LANES), F32)
    for k, value in enumerate(sums):
        out = jnp.where(lane == k, jnp.sum(value, axis=1, keepdims=True), out)
    for d in range(moments.shape[0]):
        moments[d] = out


def coefficients(mu):
    zero = jnp.zeros_like(mu[0])

    def inner(a, b):
        total = None
        for i, x in enumerate(a):
            for j, y in enumerate(b):
                term = mu[i + j] if x is None and y is None else mu[i + j] * (y if x is None else x if y is None else x * y)
                total = term if total is None else total + term
        return total

    def image(a):
        a = [jnp.ones_like(zero) if x is None else x for x in a] + [zero]
        return [a[0]] + [a[i] - a[i - 1] for i in range(1, len(a))]

    def ratio(top, bottom):
        return jnp.where(bottom > 0.0, top / jnp.where(bottom > 0.0, bottom, 1.0), 0.0)

    rho, pi, x = [jnp.ones_like(zero)], [jnp.ones_like(zero)], []
    gamma = inner(rho, rho)
    for step in range(3):
        moved = image(pi)
        alpha = ratio(gamma, inner(pi, moved))
        x = [(x[i] if i < len(x) else zero) + alpha * pi[i] for i in range(len(pi))]
        rho = [(rho[i] if i < len(rho) else zero) - alpha * moved[i] for i in range(len(moved))]
        if step < 2:
            following = inner(rho, rho)
            beta = ratio(following, gamma)
            pi = [rho[i] + (beta * pi[i] if i < len(pi) else zero) for i in range(len(rho))]
            gamma = following
    return x, rho


def last_kernel(size, moments, own_l, own_r, got_l, got_r, diag, v0, v1, v2, out):
    total = moments[0]
    for d in range(1, moments.shape[0]):
        total = total + moments[d]
    mu = [jnp.broadcast_to(total[:, k : k + 1], (SUB, LANES)) for k in range(6)]
    x, rho = coefficients(mu)
    x = [value[:, :1] for value in x]
    rho = [value[:, :1] for value in rho]
    for g in range(size.group):
        at = size.reach + g * size.verts
        here = slice(at, at + size.verts)
        if at < size.domain:
            sums = own_l[:, here] + got_l[:, g * size.verts : (g + 1) * size.verts]
        else:
            back = at - size.domain
            inside = slice(back, back + size.verts)
            sums = own_r[:, inside] + got_r[:, inside]
        a, b, c, scale = v0[:, here], v1[:, here], v2[:, here], diag[:, here]
        out[g, 0] = x[0] * a + x[1] * b + x[2] * c
        out[g, 1] = scale * (rho[0] * a + rho[1] * b + rho[2] * c) + rho[3] * sums


def order_kernel(size, parts, x, r):
    for g in range(size.group):
        here = slice(g * size.rows, (g + 1) * size.rows)
        x[here, :] = parts[g, 0, : size.rows]
        r[here, :] = parts[g, 1, : size.rows]


def on_device(heads, tails, signs, edge_weights, ground):
    group = lax.axis_size("grp")
    count = lax.axis_size("dom")
    size = Sizes(heads.shape[0], ground.shape[0], group)
    vmem = pl.BlockSpec(memory_space=pltpu.VMEM)
    smem = pl.BlockSpec(memory_space=pltpu.SMEM)
    params = pltpu.CompilerParams(vmem_limit_bytes=48 * 1024 * 1024)

    def flat(value):
        return value.astype(F32).reshape(-1, LANES)

    parts = [flat(heads), flat(tails), flat(signs[0]), flat(signs[1]), flat(edge_weights), flat(ground)]
    used = sum(part.shape[0] for part in parts)
    parts.append(jnp.zeros((size.payload - used, LANES), F32))
    pay = lax.all_gather(jnp.concatenate(parts, axis=0), "grp")

    half = jax.ShapeDtypeStruct((SUB, size.domain), F32)
    full = jax.ShapeDtypeStruct((SUB, size.extent), F32)

    odd = lax.axis_index("dom") % 2 == 1

    def exchange(left, right):
        got = []
        for base in range(2):
            lower = [i for i in range(base, count - 1, 2)]
            pairs = [(i, i + 1) for i in lower] + [(i + 1, i) for i in lower]
            sent = jnp.where(odd, left, right) if base == 0 else jnp.where(odd, right, left)
            got.append(lax.ppermute(sent, "dom", pairs))
        return jnp.where(odd, got[0], got[1]), jnp.where(odd, got[1], got[0])

    me = lax.axis_index("grp")
    first_row = me * size.rows
    place = jnp.stack([first_row // HALF, first_row % HALF]).astype(jnp.int32)
    spread = (size.parts, LANES, LANES)
    keys, heads, tails, weights, bounds = pl.pallas_call(
        functools.partial(sort_kernel, size),
        out_shape=(
            jax.ShapeDtypeStruct(spread, jnp.int32),
            jax.ShapeDtypeStruct(spread, jnp.int32),
            jax.ShapeDtypeStruct(spread, jnp.int32),
            jax.ShapeDtypeStruct(spread, F32),
            jax.ShapeDtypeStruct((SUB, LANES), jnp.int32),
        ),
        in_specs=[smem, vmem],
        out_specs=(vmem,) * 5,
        scratch_shapes=[
            pltpu.VMEM((size.regs, SUB, LANES), jnp.int32),
            pltpu.VMEM((size.regs, SUB, LANES), F32),
        ],
        compiler_params=params,
        name="sort_edges",
    )(place, pay)
    edges = (bounds, heads, tails, weights)
    edge_specs = [smem, vmem, vmem, vmem]
    scratch = [
        pltpu.VMEM((size.padded(0), 16, LANES), F32),
        pltpu.VMEM((size.extent + size.window + size.further, LANES), F32),
        pltpu.VMEM((2, size.batch, 16, size.parts * LANES), BF),
        pltpu.VMEM((2, size.batch, 16, size.parts * LANES), BF),
        pltpu.VMEM((size.padded(1) + size.most[0], SUB, LANES), F32),
    ]
    acc = pl.pallas_call(
        functools.partial(sketch_kernel, size),
        out_shape=(half, half),
        in_specs=edge_specs + [vmem] * 2,
        out_specs=(vmem, vmem),
        scratch_shapes=scratch,
        compiler_params=params,
        name="sketch",
    )(bounds, keys, heads, tails, weights, pay)
    got = exchange(*acc)
    *acc, v0, diag = pl.pallas_call(
        functools.partial(first_kernel, size),
        out_shape=(half, half, full, full),
        in_specs=edge_specs + [vmem] * 4,
        out_specs=(vmem,) * 4,
        scratch_shapes=scratch,
        compiler_params=params,
        name="operator_first",
    )(*edges, *acc, *got)
    got = exchange(*acc)
    *acc, v1 = pl.pallas_call(
        functools.partial(second_kernel, size),
        out_shape=(half, half, full),
        in_specs=edge_specs + [vmem] * 5,
        out_specs=(vmem,) * 3,
        scratch_shapes=scratch,
        compiler_params=params,
        name="operator_second",
    )(*edges, *acc, *got, diag)
    got = exchange(*acc)
    *acc, v2, moments = pl.pallas_call(
        functools.partial(third_kernel, size),
        out_shape=(half, half, full, jax.ShapeDtypeStruct((count, SUB, LANES), F32)),
        in_specs=edge_specs + [vmem] * 7,
        out_specs=(vmem,) * 4,
        scratch_shapes=scratch,
        compiler_params=params,
        name="operator_third",
    )(*edges, *acc, *got, diag, v0, v1)
    got_l, got_r = exchange(acc[0][:, : size.reach], acc[1][:, size.reach :])
    shared = lax.all_to_all(moments, "dom", 0, 0)
    out = pl.pallas_call(
        functools.partial(last_kernel, size),
        out_shape=jax.ShapeDtypeStruct((group, 2, SUB, size.verts), F32),
        in_specs=[vmem] * 9,
        out_specs=vmem,
        compiler_params=params,
        name="combine",
    )(shared, *acc, got_l, got_r, diag, v0, v1, v2)
    out = lax.all_to_all(out, "grp", 0, 0)
    result = jax.ShapeDtypeStruct((K, size.verts), F32)
    return pl.pallas_call(
        functools.partial(order_kernel, size),
        out_shape=(result, result),
        in_specs=[vmem],
        out_specs=(vmem, vmem),
        compiler_params=params,
        name="order",
    )(out)


def solution(mesh):
    in_specs = (
        P(("dom", "grp")),
        P(("dom", "grp")),
        P(None, ("dom", "grp")),
        P(("dom", "grp")),
        P(("dom", "grp")),
    )
    out_specs = (P(None, ("dom", "grp")), P(None, ("dom", "grp")))
    return jax.shard_map(
        on_device, mesh=mesh, in_specs=in_specs, out_specs=out_specs, check_vma=False
    )
```

```python
import functools

import jax
import jax.numpy as jnp
from jax import lax
from jax.experimental import pallas as pl
from jax.experimental.pallas import tpu as pltpu
from jax.sharding import PartitionSpec as P

K = 24
HALF = 12
LANES = 128
SUB = 8
BF = jnp.bfloat16
F32 = jnp.float32


def row_of(block, r, count):
    return jnp.broadcast_to(block[r : r + 1, :], (count, LANES))


def bits_of(n):
    return (n - 1).bit_length()


class Sizes:
    def __init__(self, edev, verts, group):
        self.edev, self.verts, self.group = edev, verts, group
        self.domain = verts * group
        self.reach = self.domain // 2
        self.extent = self.domain + 2 * self.reach
        self.rows = K // group
        self.section = edev // LANES
        self.ground_rows = verts // LANES
        self.payload = -(-(5 * self.section + self.ground_rows) // SUB) * SUB
        self.regs = edev * group // (SUB * LANES)
        self.parts = self.regs * SUB // LANES
        self.strip = self.domain // 8
        self.blocks = (self.strip // LANES, self.extent // 16 // LANES + 2)
        self.most = (2 * self.blocks[0], self.blocks[1])
        self.window = self.extent // 16 + 32
        self.further = self.extent // 64 + 32
        self.batch = 16

    def padded(self, which):
        return (self.domain, self.extent)[which] // LANES + self.most[which]

    def pack(self, heads, tails, signs):
        strip = heads // self.strip
        turned = jnp.where(strip % 2 == 1, self.extent - 1 - tails, tails)
        key = strip * self.extent + turned
        key = key * self.strip + heads % self.strip
        return (key << self.rows) | signs

    def unpack(self, key):
        key = jnp.right_shift(key, self.rows)
        low, key = key & (self.strip - 1), jnp.right_shift(key, bits_of(self.strip))
        turned, strip = key & (self.extent - 1), jnp.right_shift(key, bits_of(self.extent))
        tails = jnp.where(strip & 1 == 1, self.extent - 1 - turned, turned)
        return strip * self.strip + low, tails


def flip_mask(size, level):
    low = bits_of(size.regs)
    if level >= low + 10:
        return None
    if level < low + 3:
        place = lax.broadcasted_iota(jnp.int32, (SUB, LANES), 0)
        bit = level - low
    else:
        place = lax.broadcasted_iota(jnp.int32, (SUB, LANES), 1)
        bit = level - low - 3
    return -(jnp.right_shift(place, bit) & 1)


def partner(size, j):
    low = bits_of(size.regs)
    axis, bit = (0, j - low) if j < low + 3 else (1, j - low - 3)
    place = lax.broadcasted_iota(jnp.int32, (SUB, LANES), axis)
    lower = (jnp.right_shift(place, bit) & 1) == 0
    index = jnp.bitwise_xor(place, 1 << bit)
    return axis, index, lower


def sort_edges(size, keys, weights):
    low = bits_of(size.regs)
    levels = low + 10

    def between(group, stages):
        key = {v: keys[v] for v in group}
        weight = {v: weights[v] for v in group}
        for level, j in stages:
            for v in group:
                if v >> j & 1:
                    continue
                a, b = v, v | 1 << j
                if level < low and v >> level & 1:
                    a, b = b, a
                swap = key[a] > key[b]
                key[a], key[b] = jnp.where(swap, key[b], key[a]), jnp.where(swap, key[a], key[b])
                weight[a], weight[b] = (
                    jnp.where(swap, weight[b], weight[a]),
                    jnp.where(swap, weight[a], weight[b]),
                )
        for v in group:
            keys[v] = key[v]
            weights[v] = weight[v]

    def registers(level):
        top = min(level, low)
        if top > 3:
            for v in range(8):
                between(list(range(v, size.regs, 8)), [(level, j) for j in range(top - 1, 2, -1)])
        for v in range(0, size.regs, 8):
            between(list(range(v, v + 8)), [(level, j) for j in range(min(top, 3) - 1, -1, -1)])

    for v in range(0, size.regs, 8):
        between(list(range(v, v + 8)), [(level, j) for level in (1, 2, 3) for j in range(level - 1, -1, -1)])
    for level in range(4, low):
        registers(level)

    for level in range(low, levels + 1):
        before = flip_mask(size, level - 1) if level > low else None
        now = flip_mask(size, level)
        flip = now if before is None else before if now is None else jnp.bitwise_xor(before, now)
        stages = [partner(size, j) for j in range(level - 1, low - 1, -1)]

        wide = min(32, size.regs)

        def across(i, carry, flip=flip, stages=stages):
            group = [i * wide + u for u in range(wide)]
            key = [jnp.bitwise_xor(keys[v], flip) for v in group]
            weight = [weights[v] for v in group]
            for axis, index, lower in stages:
                for u in range(wide):
                    k, w = key[u], weight[u]
                    other = jnp.take_along_axis(k, index, axis=axis, mode="promise_in_bounds")
                    other_w = jnp.take_along_axis(w, index, axis=axis, mode="promise_in_bounds")
                    best = jnp.where(lower, jnp.minimum(k, other), jnp.maximum(k, other))
                    weight[u] = jnp.where(best == k, w, other_w)
                    key[u] = best
            for u, v in enumerate(group):
                keys[v] = key[u]
                weights[v] = weight[u]
            return carry

        lax.fori_loop(0, size.regs // wide, across, 0)
        registers(level)


def sort_kernel(size, place, pay, key_out, heads_out, tails_out, weight_out, bounds, keys, weights):
    word, shift = place[0], place[1]
    per = size.section // SUB
    mask = (1 << size.rows) - 1

    def section(which, g, c):
        return pay[g, which * size.section + c * SUB : which * size.section + (c + 1) * SUB, :]

    for g in range(size.group):
        for c in range(per):
            heads = section(0, g, c).astype(jnp.int32)
            tails = section(1, g, c).astype(jnp.int32)
            signs = jnp.where(word == 0, section(2, g, c), section(3, g, c)).astype(jnp.int32)
            v = g * per + c
            keys[v] = size.pack(heads, tails, jnp.right_shift(signs, shift) & mask)
            weights[v] = section(4, g, c)
    sort_edges(size, keys, weights)
    ends = [size.unpack(keys[v]) for v in range(size.regs)]
    lane = lax.broadcasted_iota(jnp.int32, (1, LANES), 1)
    far = rare = lane < 0
    for which in range(2):
        least = functools.reduce(jnp.minimum, [end[which] for end in ends])
        most = functools.reduce(jnp.maximum, [end[which] for end in ends])
        least = jnp.min(least, axis=0, keepdims=True)
        most = jnp.max(most, axis=0, keepdims=True)
        bounds[2 * which : 2 * which + 1, :] = least
        bounds[2 * which + 1 : 2 * which + 2, :] = most
        if which == 1:
            far = far | (most - (least & -8) >= size.window)
            rare = rare | (most - (least & -8) >= size.window + size.further)
        least, most = least // LANES, most // LANES
        far = far | (most - least >= size.blocks[which])
        rare = rare | (most - least >= size.most[which])
    runs = jnp.where(far, lane, LANES)
    count = jnp.sum(far.astype(F32), axis=1, keepdims=True)
    rare = jnp.max(jnp.where(rare, 1.0, 0.0), axis=1, keepdims=True)
    rare, count = rare.astype(jnp.int32), count.astype(jnp.int32)
    for step in (1, 2, 4, 8, 16, 32, 64):
        after = jnp.where(lane + step < LANES, jnp.roll(runs, -step, axis=1), LANES)
        runs = jnp.minimum(runs, after)
    bounds[4:5, :] = runs
    bounds[5:6, :] = jnp.broadcast_to(rare, (1, LANES))
    bounds[6:7, :] = jnp.broadcast_to(count, (1, LANES))
    for j in range(size.parts):
        here = range(j * 16, (j + 1) * 16)
        key = jnp.concatenate([keys[v] for v in here], axis=0).T
        key_out[j] = key
        heads_out[j], tails_out[j] = size.unpack(key)
        weight_out[j] = jnp.concatenate([weights[v] for v in here], axis=0).T


def halves_of(value):
    high = value.astype(BF).astype(F32)
    return jnp.concatenate([high, value - high], axis=0).astype(BF)


def row(ref, j, run, count):
    return jnp.broadcast_to(ref[j, pl.ds(run, 1), :], (count, LANES))


def next_far(bounds, run):
    following = bounds[4, jnp.minimum(run + 1, LANES - 1)]
    return jnp.where(run + 1 < LANES, following, LANES)


def one_hot(size, index, run, start, window):
    iota = lax.broadcasted_iota(jnp.int32, (16, LANES), 0)
    rows = [(iota + 16 * m).astype(F32).astype(BF) for m in range(16)]
    zero, one = jnp.zeros((16, LANES), BF), jnp.ones((16, LANES), BF)
    hot = []
    for j in range(size.parts):
        column = []
        for at in range(0, window, 256):
            local = (row(index, j, run, 16) - (start + at)).astype(F32).astype(BF)
            count = min(256, window - at) // 16
            column += [jnp.where(local == rows[m], one, zero) for m in range(count)]
        hot.append(jnp.concatenate(column, axis=0))
    return jnp.concatenate(hot, axis=1)


def times(left, right):
    return lax.dot_general(left, right, (((1,), (1,)), ((), ())), preferred_element_type=F32)


def add_blocks(size, heads, run, first, begin, end, pair, acc, valid=True):
    start = (first + begin) * LANES
    if valid is not True:
        start = jnp.where(valid, start, -(1 << 20))
    got = times(pair, one_hot(size, heads, run, start, (end - begin) * LANES))
    for b in range(end - begin):
        acc[first + begin + b] += got[:, b * LANES : (b + 1) * LANES]


def add_rows(size, tails, run, start, window, pair, acc, valid=True):
    start = pl.multiple_of(start, SUB)
    from_ = start if valid is True else jnp.where(valid, start, -(1 << 20))
    acc[pl.ds(start, window), 0:16] += times(one_hot(size, tails, run, from_, window), pair)


def first_block(bounds, which, run):
    return bounds[2 * which, run] // LANES


def last_block(bounds, which, run):
    return bounds[2 * which + 1, run] // LANES


def first_row(bounds, run):
    return bounds[2, run] & -8


def sweep(size, bounds, ends, make, make_far, accs, bufs):
    def fill(buf, base):
        for q in range(size.batch):
            for which, pair in enumerate(make(base + q)):
                buf[which, q] = pair

    heads, tails = ends
    acc_h, acc_t = accs

    def use(buf, base):
        for q in range(size.batch):
            run = base + q
            add_blocks(size, heads, run, first_block(bounds, 0, run), 0, size.blocks[0], buf[0, q], acc_h)
            add_rows(size, tails, run, first_row(bounds, run), size.window, buf[1, q], acc_t)

    fill(bufs[0], 0)

    def step(i, carry):
        base = i * 2 * size.batch
        use(bufs[0], base)
        fill(bufs[1], base + size.batch)
        use(bufs[1], base + size.batch)
        fill(bufs[0], (base + 2 * size.batch) % LANES)
        return carry

    lax.fori_loop(0, LANES // (2 * size.batch), step, 0)

    @pl.when(bounds[5, 0] == 0)
    def _():
        def four(i, run):
            for _ in range(4):
                valid, here = run < LANES, jnp.minimum(run, LANES - 1)
                full, beyond = make_far(here, False)
                first = first_block(bounds, 0, here)
                add_blocks(size, heads, here, first, size.blocks[0], size.most[0], full[0], acc_h, valid)
                start = first_row(bounds, here)
                add_rows(size, tails, here, start + size.window, size.further, full[1], acc_t, valid)
                if beyond is not None:
                    add_rows(size, tails, here, start, size.window, beyond[1], acc_t, valid)
                run = jnp.where(valid, next_far(bounds, here), LANES)
            return run

        lax.fori_loop(0, (bounds[6, 0] + 3) // 4, four, bounds[4, 0])

    @pl.when(bounds[5, 0] != 0)
    def _():
        def more(run):
            full, beyond = make_far(run, True)
            first, start = first_block(bounds, 0, run), first_row(bounds, run)

            def block(a, carry):
                add_blocks(size, heads, run, a, 0, 1, full[0], acc_h)
                return carry

            def window(m, carry):
                add_rows(size, tails, run, start + m * size.window, size.window, full[1], acc_t)
                return carry

            lax.fori_loop(first + size.blocks[0], last_block(bounds, 0, run) + 1, block, 0)
            lax.fori_loop(1, (bounds[3, run] - start) // size.window + 1, window, 0)
            if beyond is not None:
                add_blocks(size, heads, run, first, 0, size.blocks[0], beyond[0], acc_h)
                add_rows(size, tails, run, start, size.window, beyond[1], acc_t)
            return next_far(bounds, run)

        lax.while_loop(lambda run: run < LANES, more, bounds[4, 0])


def collect(size, acc_h, acc_t, out_l, out_r):
    shift = size.reach // LANES
    half = size.domain // LANES
    for a in range(size.extent // LANES):
        value = acc_t[a * LANES : (a + 1) * LANES, :].T
        value = value[0:8, :] + value[8:16, :]
        h = a - shift
        if 0 <= h < half:
            value += acc_h[h, 0:8] + acc_h[h, 8:16]
        out, at = (out_l, a) if a < half else (out_r, a - half)
        out[:, at * LANES : (at + 1) * LANES] = value


def clear(acc_h, acc_t):
    acc_h[...] = jnp.zeros_like(acc_h)
    acc_t[...] = jnp.zeros_like(acc_t)


def sketch_kernel(size, bounds, keys, heads, tails, weights, pay, out_l, out_r, acc_h, acc_t, buf_a, buf_b, tables):
    sub = lax.broadcasted_iota(jnp.int32, (SUB, LANES), 0)
    is_sign = sub < size.rows
    clear(acc_h, acc_t)

    def make(run):
        pairs = [[], []]
        for j in range(size.parts):
            weight = row(weights, j, run, SUB)
            bit = jnp.right_shift(row(keys, j, run, SUB), sub) & 1
            signed = (2 * bit - 1).astype(F32) * jnp.sqrt(weight)
            last = jnp.where(sub == size.rows, weight, 0.0)
            pairs[0].append(halves_of(jnp.where(is_sign, signed, last)))
            pairs[1].append(halves_of(jnp.where(is_sign, -signed, last)))
        return [jnp.concatenate(pair, axis=1) for pair in pairs]

    sweep(size, bounds, (heads, tails), make, lambda run, every: (make(run), None), (acc_h, acc_t), (buf_a, buf_b))
    collect(size, acc_h, acc_t, out_l, out_r)
    for g in range(size.group):
        for r in range(size.ground_rows):
            at = size.reach + g * size.verts + r * LANES
            out, at = (out_l, at) if at < size.domain else (out_r, at - size.domain)
            line = 5 * size.section + r
            value = jnp.broadcast_to(pay[g, line : line + 1, :], (SUB, LANES))
            out[:, at : at + LANES] += jnp.where(sub == size.rows, value, 0.0)


def operator_core(size, bounds, heads, tails, weights, table, out_l, out_r, bufs):
    acc_h, acc_t, buf_a, buf_b, tables = bufs
    clear(acc_h, acc_t)
    for a in range(size.extent // LANES):
        tables[a] = table[:, a * LANES : (a + 1) * LANES]
    ends = (heads, tails)

    def take(which, low, high, a, out):
        shift = size.reach // LANES if which == 0 else 0
        got = jnp.take_along_axis(tables[shift + a], low, axis=1, mode="promise_in_bounds")
        return jnp.where(high == a, got, out)

    nothing = jnp.zeros((SUB, LANES), F32)

    def gathered(run, blocks):
        pairs = [[], []]
        for j in range(size.parts):
            weight = row(weights, j, run, SUB)
            for which in range(2):
                index = row(ends[which], j, run, SUB)
                first, (begin, end) = first_block(bounds, which, run), blocks[which]
                low, high = index % LANES, index // LANES
                if end is None:
                    out = lax.fori_loop(
                        first + begin, last_block(bounds, which, run) + 1,
                        lambda a, out: take(which, low, high, a, out), nothing,
                    )
                else:
                    out = nothing
                    for a in range(begin, end):
                        out = take(which, low, high, first + a, out)
                pairs[1 - which].append(halves_of(out * weight))
        return [jnp.concatenate(pair, axis=1) for pair in pairs]

    def make(run):
        return gathered(run, [(0, size.blocks[which]) for which in range(2)])

    def make_far(run, every):
        ends_at = [None, None] if every else size.most
        return (
            gathered(run, [(0, ends_at[which]) for which in range(2)]),
            gathered(run, [(size.blocks[which], ends_at[which]) for which in range(2)]),
        )

    sweep(size, bounds, ends, make, make_far, (acc_h, acc_t), (buf_a, buf_b))
    collect(size, acc_h, acc_t, out_l, out_r)


def halves(size, own_l, own_r, got_l, got_r):
    return ((0, own_l, got_l), (size.domain, own_r, got_r))


def first_kernel(size, bounds, heads, tails, weights, own_l, own_r, got_l, got_r, out_l, out_r, v, diag, *bufs):
    sub = lax.broadcasted_iota(jnp.int32, (SUB, size.domain), 0)
    for at, own, got in halves(size, own_l, own_r, got_l, got_r):
        total = own[...] + got[...]
        spread = jnp.broadcast_to(total[size.rows : size.rows + 1, :], total.shape)
        safe = jnp.where(spread > 0.0, spread, 1.0)
        diag[:, at : at + size.domain] = safe
        v[:, at : at + size.domain] = jnp.where(sub < size.rows, total / safe, 0.0)
    operator_core(size, bounds, heads, tails, weights, v, out_l, out_r, bufs)


def next_v(size, own_l, own_r, got_l, got_r, diag, v):
    for at, own, got in halves(size, own_l, own_r, got_l, got_r):
        v[:, at : at + size.domain] = (own[...] + got[...]) / diag[:, at : at + size.domain]


def second_kernel(size, bounds, heads, tails, weights, own_l, own_r, got_l, got_r, diag, out_l, out_r, v, *bufs):
    next_v(size, own_l, own_r, got_l, got_r, diag, v)
    operator_core(size, bounds, heads, tails, weights, v, out_l, out_r, bufs)


def third_kernel(size, bounds, heads, tails, weights, own_l, own_r, got_l, got_r, diag, v0, v1, out_l, out_r, v2, moments, *bufs):
    next_v(size, own_l, own_r, got_l, got_r, diag, v2)
    operator_core(size, bounds, heads, tails, weights, v2, out_l, out_r, bufs)
    lane = lax.broadcasted_iota(jnp.int32, (SUB, LANES), 1)
    middle = slice(size.reach, size.reach + size.domain)
    weighted = diag[:, middle] * v0[:, middle]
    other = diag[:, middle] * v1[:, middle]
    sums = [
        weighted * v0[:, middle],
        weighted * v1[:, middle],
        other * v1[:, middle],
        other * v2[:, middle],
        diag[:, middle] * v2[:, middle] * v2[:, middle],
        v2[:, : size.domain] * out_l[...] + v2[:, size.domain :] * out_r[...],
    ]
    out = jnp.zeros((SUB, LANES), F32)
    for k, value in enumerate(sums):
        out = jnp.where(lane == k, jnp.sum(value, axis=1, keepdims=True), out)
    for d in range(moments.shape[0]):
        moments[d] = out


def coefficients(mu):
    zero = jnp.zeros_like(mu[0])

    def inner(a, b):
        total = None
        for i, x in enumerate(a):
            for j, y in enumerate(b):
                term = mu[i + j] if x is None and y is None else mu[i + j] * (y if x is None else x if y is None else x * y)
                total = term if total is None else total + term
        return total

    def image(a):
        a = [jnp.ones_like(zero) if x is None else x for x in a] + [zero]
        return [a[0]] + [a[i] - a[i - 1] for i in range(1, len(a))]

    def ratio(top, bottom):
        return jnp.where(bottom > 0.0, top / jnp.where(bottom > 0.0, bottom, 1.0), 0.0)

    rho, pi, x = [jnp.ones_like(zero)], [jnp.ones_like(zero)], []
    gamma = inner(rho, rho)
    for step in range(3):
        moved = image(pi)
        alpha = ratio(gamma, inner(pi, moved))
        x = [(x[i] if i < len(x) else zero) + alpha * pi[i] for i in range(len(pi))]
        rho = [(rho[i] if i < len(rho) else zero) - alpha * moved[i] for i in range(len(moved))]
        if step < 2:
            following = inner(rho, rho)
            beta = ratio(following, gamma)
            pi = [rho[i] + (beta * pi[i] if i < len(pi) else zero) for i in range(len(rho))]
            gamma = following
    return x, rho


def last_kernel(size, moments, own_l, own_r, got_l, got_r, diag, v0, v1, v2, out):
    total = moments[0]
    for d in range(1, moments.shape[0]):
        total = total + moments[d]
    mu = [jnp.broadcast_to(total[:, k : k + 1], (SUB, LANES)) for k in range(6)]
    x, rho = coefficients(mu)
    x = [value[:, :1] for value in x]
    rho = [value[:, :1] for value in rho]
    for g in range(size.group):
        at = size.reach + g * size.verts
        here = slice(at, at + size.verts)
        if at < size.domain:
            sums = own_l[:, here] + got_l[:, g * size.verts : (g + 1) * size.verts]
        else:
            back = at - size.domain
            inside = slice(back, back + size.verts)
            sums = own_r[:, inside] + got_r[:, inside]
        a, b, c, scale = v0[:, here], v1[:, here], v2[:, here], diag[:, here]
        out[g, 0] = x[0] * a + x[1] * b + x[2] * c
        out[g, 1] = scale * (rho[0] * a + rho[1] * b + rho[2] * c) + rho[3] * sums


def order_kernel(size, parts, x, r):
    for g in range(size.group):
        here = slice(g * size.rows, (g + 1) * size.rows)
        x[here, :] = parts[g, 0, : size.rows]
        r[here, :] = parts[g, 1, : size.rows]


def on_device(heads, tails, signs, edge_weights, ground):
    group = lax.axis_size("grp")
    count = lax.axis_size("dom")
    size = Sizes(heads.shape[0], ground.shape[0], group)
    vmem = pl.BlockSpec(memory_space=pltpu.VMEM)
    smem = pl.BlockSpec(memory_space=pltpu.SMEM)
    params = pltpu.CompilerParams(vmem_limit_bytes=48 * 1024 * 1024)

    def flat(value):
        return value.astype(F32).reshape(-1, LANES)

    parts = [flat(heads), flat(tails), flat(signs[0]), flat(signs[1]), flat(edge_weights), flat(ground)]
    used = sum(part.shape[0] for part in parts)
    parts.append(jnp.zeros((size.payload - used, LANES), F32))
    pay = lax.all_gather(jnp.concatenate(parts, axis=0), "grp")

    half = jax.ShapeDtypeStruct((SUB, size.domain), F32)
    full = jax.ShapeDtypeStruct((SUB, size.extent), F32)

    odd = lax.axis_index("dom") % 2 == 1

    def exchange(left, right):
        got = []
        for base in range(2):
            lower = [i for i in range(base, count - 1, 2)]
            pairs = [(i, i + 1) for i in lower] + [(i + 1, i) for i in lower]
            sent = jnp.where(odd, left, right) if base == 0 else jnp.where(odd, right, left)
            got.append(lax.ppermute(sent, "dom", pairs))
        return jnp.where(odd, got[0], got[1]), jnp.where(odd, got[1], got[0])

    me = lax.axis_index("grp")
    first_row = me * size.rows
    place = jnp.stack([first_row // HALF, first_row % HALF]).astype(jnp.int32)
    spread = (size.parts, LANES, LANES)
    keys, heads, tails, weights, bounds = pl.pallas_call(
        functools.partial(sort_kernel, size),
        out_shape=(
            jax.ShapeDtypeStruct(spread, jnp.int32),
            jax.ShapeDtypeStruct(spread, jnp.int32),
            jax.ShapeDtypeStruct(spread, jnp.int32),
            jax.ShapeDtypeStruct(spread, F32),
            jax.ShapeDtypeStruct((SUB, LANES), jnp.int32),
        ),
        in_specs=[smem, vmem],
        out_specs=(vmem,) * 5,
        scratch_shapes=[
            pltpu.VMEM((size.regs, SUB, LANES), jnp.int32),
            pltpu.VMEM((size.regs, SUB, LANES), F32),
        ],
        compiler_params=params,
        name="sort_edges",
    )(place, pay)
    edges = (bounds, heads, tails, weights)
    edge_specs = [smem, vmem, vmem, vmem]
    scratch = [
        pltpu.VMEM((size.padded(0), 16, LANES), F32),
        pltpu.VMEM((size.extent + size.window + size.further, LANES), F32),
        pltpu.VMEM((2, size.batch, 16, size.parts * LANES), BF),
        pltpu.VMEM((2, size.batch, 16, size.parts * LANES), BF),
        pltpu.VMEM((size.padded(1) + size.most[0], SUB, LANES), F32),
    ]
    acc = pl.pallas_call(
        functools.partial(sketch_kernel, size),
        out_shape=(half, half),
        in_specs=edge_specs + [vmem] * 2,
        out_specs=(vmem, vmem),
        scratch_shapes=scratch,
        compiler_params=params,
        name="sketch",
    )(bounds, keys, heads, tails, weights, pay)
    got = exchange(*acc)
    *acc, v0, diag = pl.pallas_call(
        functools.partial(first_kernel, size),
        out_shape=(half, half, full, full),
        in_specs=edge_specs + [vmem] * 4,
        out_specs=(vmem,) * 4,
        scratch_shapes=scratch,
        compiler_params=params,
        name="operator_first",
    )(*edges, *acc, *got)
    got = exchange(*acc)
    *acc, v1 = pl.pallas_call(
        functools.partial(second_kernel, size),
        out_shape=(half, half, full),
        in_specs=edge_specs + [vmem] * 5,
        out_specs=(vmem,) * 3,
        scratch_shapes=scratch,
        compiler_params=params,
        name="operator_second",
    )(*edges, *acc, *got, diag)
    got = exchange(*acc)
    *acc, v2, moments = pl.pallas_call(
        functools.partial(third_kernel, size),
        out_shape=(half, half, full, jax.ShapeDtypeStruct((count, SUB, LANES), F32)),
        in_specs=edge_specs + [vmem] * 7,
        out_specs=(vmem,) * 4,
        scratch_shapes=scratch,
        compiler_params=params,
        name="operator_third",
    )(*edges, *acc, *got, diag, v0, v1)
    got_l, got_r = exchange(acc[0][:, : size.reach], acc[1][:, size.reach :])
    shared = lax.all_to_all(moments, "dom", 0, 0)
    out = pl.pallas_call(
        functools.partial(last_kernel, size),
        out_shape=jax.ShapeDtypeStruct((group, 2, SUB, size.verts), F32),
        in_specs=[vmem] * 9,
        out_specs=vmem,
        compiler_params=params,
        name="combine",
    )(shared, *acc, got_l, got_r, diag, v0, v1, v2)
    out = lax.all_to_all(out, "grp", 0, 0)
    result = jax.ShapeDtypeStruct((K, size.verts), F32)
    return pl.pallas_call(
        functools.partial(order_kernel, size),
        out_shape=(result, result),
        in_specs=[vmem],
        out_specs=(vmem, vmem),
        compiler_params=params,
        name="order",
    )(out)


def solution(mesh):
    in_specs = (
        P(("dom", "grp")),
        P(("dom", "grp")),
        P(None, ("dom", "grp")),
        P(("dom", "grp")),
        P(("dom", "grp")),
    )
    out_specs = (P(None, ("dom", "grp")), P(None, ("dom", "grp")))
    return jax.shard_map(
        on_device, mesh=mesh, in_specs=in_specs, out_specs=out_specs, check_vma=False
    )
```
